32 devices in a mesh: dp: 4 (over z), fsdp: 8 (over y, x, core).
Axes of the slice: x: 2, y: 2, z: 4, core: 2. Of those that a mesh axis runs over, the one named last changes fastest.
Arguments:
- tokens: bfloat16 [138752, 768], P(('dp', 'fsdp')), may hold values from -6 to 6
- keep_slots: int32 [256, 268], P(('dp', 'fsdp')), may hold values from 0 to 541, as said below
- cotangent: bfloat16 [138752, 768], P(('dp', 'fsdp')), may hold values from -6 to 6
- project_in: float32 [768, 2304], P(('dp', 'fsdp')), may hold values from -0.21875 to 0.21875
- project_out: float32 [768, 768], P(('dp', 'fsdp')), may hold values from -0.625 to 0.625
- expand: float32 [768, 3072], P(('dp', 'fsdp')), may hold values from -0.21875 to 0.21875
- contract: float32 [3072, 768], P(('dp', 'fsdp')), may hold values from -0.109375 to 0.109375
- vectors: float32 [13, 768], P(None, ('dp', 'fsdp')), may hold values from -1.5 to 4.5
- first_in: float32 [768, 2304], P(('dp', 'fsdp')), may hold values from -0.3 to 0.3
- first_out: float32 [768, 768], P(('dp', 'fsdp')), may hold values from -0.3 to 0.3
- first_expand: float32 [768, 3072], P(('dp', 'fsdp')), may hold values from -0.3 to 0.3
- first_contract: float32 [3072, 768], P(('dp', 'fsdp')), may hold values from -0.3 to 0.3
- first_vectors: float32 [13, 768], P(None, ('dp', 'fsdp')), may hold values from -0.3 to 0.3
- second_in: float32 [768, 2304], P(('dp', 'fsdp')), may hold values from 0.0025 to 0.01
- second_out: float32 [768, 768], P(('dp', 'fsdp')), may hold values from 0.0025 to 0.01
- second_expand: float32 [768, 3072], P(('dp', 'fsdp')), may hold values from 0.0025 to 0.01
- second_contract: float32 [3072, 768], P(('dp', 'fsdp')), may hold values from 0.0025 to 0.01
- second_vectors: float32 [13, 768], P(None, ('dp', 'fsdp')), may hold values from 0.0025 to 0.01
Outputs:
- activations: bfloat16 [138752, 768], P(('dp', 'fsdp'))
- input_grad: bfloat16 [138752, 768], P(('dp', 'fsdp'))
- grad_norm: float32 [1], replicated
- momentum_in: float32 [768, 2304], P(('dp', 'fsdp'))
- momentum_out: float32 [768, 768], P(('dp', 'fsdp'))
- momentum_expand: float32 [768, 3072], P(('dp', 'fsdp'))
- momentum_contract: float32 [3072, 768], P(('dp', 'fsdp'))
- momentum_vectors: float32 [13, 768], P(None, ('dp', 'fsdp'))
- variance_in: float32 [768, 2304], P(('dp', 'fsdp'))
- variance_out: float32 [768, 768], P(('dp', 'fsdp'))
- variance_expand: float32 [768, 3072], P(('dp', 'fsdp'))
- variance_contract: float32 [3072, 768], P(('dp', 'fsdp'))
- variance_vectors: float32 [13, 768], P(None, ('dp', 'fsdp'))
- updated_in: float32 [768, 2304], P(('dp', 'fsdp'))
- updated_out: float32 [768, 768], P(('dp', 'fsdp'))
- updated_expand: float32 [768, 3072], P(('dp', 'fsdp'))
- updated_contract: float32 [3072, 768], P(('dp', 'fsdp'))
- updated_vectors: float32 [13, 768], P(None, ('dp', 'fsdp'))
- copy_in: bfloat16 [768, 2304], P(('dp', 'fsdp'))
- copy_out: bfloat16 [768, 768], P(('dp', 'fsdp'))
- copy_expand: bfloat16 [768, 3072], P(('dp', 'fsdp'))
- copy_contract: bfloat16 [3072, 768], P(('dp', 'fsdp'))
- copy_vectors: bfloat16 [13, 768], P(None, ('dp', 'fsdp'))
The draws below stay inside these ranges and needn't reach their ends.
Inputs may be any that keep to these rules, and one draw needn't show every extreme that they name: `keep_slots`: row i lists the kept positions of image i: slots 0 to 97 hold distinct positions of its first global crop (positions 0 to 196) in ascending order, the next 98 slots distinct positions of the second global crop (the next 197 positions) in ascending order, then 18 slots for each of the four local crops of 37 positions that follow, likewise.
All inputs are finite; a program needn't handle non-finite values.
Results may differ from the reference program's by a relative error of at most 0.012.
The reference program's roundings to bfloat16 on the way count: a program that leaves them out, or rounds other values in their place, can miss the bound.
Values may be sent and summed in bfloat16 or wider, within the bound.
No kernel may reach another device: no remote copies, remote signals or barrier semaphores. Data moves between devices by JAX's collectives and lax.ppermute only.
A program may use at most 320 MiB of HBM per device.

```python
import math
import jax
import jax.numpy as jnp
from jax import lax

D = 768
HEADS = 12
FF = 3072
HEAD_DIM = 64
GLOBAL_LEN = 197
LOCAL_LEN = 37
KEEP_GLOBAL = 98
KEEP_LOCAL = 18
KEEP = 268
IMG_TOK = 542
IMG_DEV = 8
IMAGES = 256
TOKENS = 138752
NVEC = 13
PARAMS = 7087872
STEP = 5
N_DP = 4
N_FSDP = 8
DEVICES = 32


def rising_gain(key, rise):
    columns = jnp.arange(D, dtype=jnp.int32)
    owner = columns // (D // DEVICES)
    outer_place = (owner // N_FSDP).astype(jnp.float32) / max(N_DP - 1, 1)
    inner_place = (owner % N_FSDP).astype(jnp.float32) / max(N_FSDP - 1, 1)
    rough = jnp.exp(jax.random.uniform(key, (D,), jnp.float32, jnp.log(0.7), jnp.log(1.4)))
    return 0.5 * rise ** (0.5 * (outer_place + inner_place)) * rough


def draw_vectors(key, part):
    key = jax.random.fold_in(key, 11)
    rise = 3.0
    first_key, second_key, bias_key, router_key = jax.random.split(key, 4)
    gain_one = rising_gain(first_key, rise)
    gain_two = rising_gain(second_key, rise)
    biases = 0.3 * jax.random.truncated_normal(bias_key, -4.0, 4.0, (NVEC, D), jnp.float32)
    router = jax.random.truncated_normal(router_key, -4.0, 4.0, (D,), jnp.float32) * D ** (-0.5)
    return biases.at[0].set(gain_one).at[5].set(gain_two).at[8].set(router)


def draw_keep_slots(key, part):
    key = jax.random.fold_in(key, 7)

    def global_crop(image, crop):
        sub = jax.random.fold_in(jax.random.fold_in(key, image), crop)
        chosen = jax.random.permutation(sub, GLOBAL_LEN)[:KEEP_GLOBAL].astype(jnp.int32)
        return jnp.sort(chosen) + crop * GLOBAL_LEN

    def local_crop(image, crop):
        sub = jax.random.fold_in(jax.random.fold_in(key, image), crop + 2)
        chosen = jax.random.permutation(sub, LOCAL_LEN)[:KEEP_LOCAL].astype(jnp.int32)
        return jnp.sort(chosen) + 2 * GLOBAL_LEN + crop * LOCAL_LEN
    images = jnp.arange(IMAGES, dtype=jnp.int32)
    wide = jax.vmap(jax.vmap(global_crop, in_axes=(None, 0)), in_axes=(0, None))(images, jnp.arange(2, dtype=jnp.int32))
    narrow = jax.vmap(jax.vmap(local_crop, in_axes=(None, 0)), in_axes=(0, None))(images, jnp.arange(4, dtype=jnp.int32))
    joined = jnp.concatenate([wide.reshape(IMAGES, 2 * KEEP_GLOBAL), narrow.reshape(IMAGES, 4 * KEEP_LOCAL)], axis=1)
    return joined.astype(jnp.int32)


def raised(entries, key, source, target, blocks, factor):
    def block_of(dim):
        return (jnp.arange(entries.shape[dim]) // (entries.shape[dim] // blocks)).reshape((-1,) + (1,) * (entries.ndim - 1 - dim))

    one_side = jax.random.permutation(key, blocks)[block_of(target)]
    second = (block_of(target) + blocks // 2) % blocks
    return jnp.where((block_of(source) == one_side) | (block_of(source) == second), factor * entries, entries)


def shard_levels(key, shape, pieces, least, largest):
    factor_of = 1.0
    for dim, blocks in pieces:
        steps = jax.random.uniform(jax.random.fold_in(jax.random.fold_in(key, 6), dim), (blocks,), jnp.float32, least / len(pieces), largest / len(pieces))
        factor_of = factor_of * jnp.repeat(jnp.exp(steps), shape[dim] // blocks).reshape((-1,) + (1,) * (len(shape) - 1 - dim))
    return factor_of


def bell_draw(rng, extent, deviation, reach, cuts=(), held_as=jnp.bfloat16):
    level = shard_levels(rng, extent, cuts, -0.22, 0.18) if cuts else 1.0
    drawn = jax.random.normal(rng, extent, jnp.float32) * deviation * level
    return jnp.minimum(jnp.maximum(drawn, -reach), reach).astype(held_as)


def noise_with(key, dims, scale, most, pieces, heavy, kind=jnp.bfloat16):
    drawn = scale * jax.random.normal(key, dims, jnp.float32)
    if pieces:
        drawn = drawn * shard_levels(key, dims, pieces, -0.22, 0.18)
    return jnp.clip(raised(drawn, jax.random.fold_in(key, 3), *heavy), -most, most).astype(kind)


def setup_inputs(seed: int = 0) -> dict:
    streams_of = jax.random.split(jax.random.key(seed), 19)
    tokens = bell_draw(streams_of[0], (TOKENS, D), 1.0, 6.0, ((0, 32),))
    keep_slots = draw_keep_slots(jax.random.fold_in(streams_of[18], 71), 0)
    cotangent = noise_with(streams_of[2], (TOKENS, D), 1.0, 6.0, ((0, 32),), (0, 1, 32, 2.75))
    project_in = bell_draw(streams_of[3], (D, 3 * D), D ** -0.5, 0.21875, ((0, 32),), jnp.float32)
    project_out = bell_draw(streams_of[4], (D, D), (D // 8) ** -0.5, 0.625, ((0, 32),), jnp.float32)
    expand = bell_draw(streams_of[5], (D, FF), D ** -0.5, 0.21875, ((0, 32),), jnp.float32)
    contract = bell_draw(streams_of[6], (FF, D), FF ** -0.5, 0.109375, ((0, 32),), jnp.float32)
    vectors = draw_vectors(jax.random.fold_in(streams_of[18], 71), 0)
    first_in = bell_draw(streams_of[8], (D, 3 * D), 0.05, 0.3, ((0, 32),), jnp.float32)
    first_out = bell_draw(streams_of[9], (D, D), 0.05, 0.3, ((0, 32),), jnp.float32)
    first_expand = bell_draw(streams_of[10], (D, FF), 0.05, 0.3, ((0, 32),), jnp.float32)
    first_contract = bell_draw(streams_of[11], (FF, D), 0.05, 0.3, ((0, 32),), jnp.float32)
    first_vectors = bell_draw(streams_of[12], (NVEC, D), 0.05, 0.3, ((1, 32),), jnp.float32)
    second_in = jnp.clip(jnp.exp(math.log(0.01) - 1.3862944 * jax.random.uniform(streams_of[13], (D, 3 * D), jnp.float32) ** shard_levels(streams_of[13], (D, 3 * D), ((0, 32),), -0.2, 0.2)), 0.0025, 0.01)
    second_out = jnp.clip(jnp.exp(math.log(0.01) - 1.3862944 * jax.random.uniform(streams_of[14], (D, D), jnp.float32) ** shard_levels(streams_of[14], (D, D), ((0, 32),), -0.2, 0.2)), 0.0025, 0.01)
    second_expand = jnp.clip(jnp.exp(math.log(0.01) - 1.3862944 * jax.random.uniform(streams_of[15], (D, FF), jnp.float32) ** shard_levels(streams_of[15], (D, FF), ((0, 32),), -0.2, 0.2)), 0.0025, 0.01)
    second_contract = jnp.clip(jnp.exp(math.log(0.01) - 1.3862944 * jax.random.uniform(streams_of[16], (FF, D), jnp.float32) ** shard_levels(streams_of[16], (FF, D), ((0, 32),), -0.2, 0.2)), 0.0025, 0.01)
    second_vectors = jnp.clip(jnp.exp(math.log(0.01) - 1.3862944 * jax.random.uniform(streams_of[17], (NVEC, D), jnp.float32) ** shard_levels(streams_of[17], (NVEC, D), ((1, 32),), -0.2, 0.2)), 0.0025, 0.01)
    return dict(tokens=tokens, keep_slots=keep_slots, cotangent=cotangent, project_in=project_in, project_out=project_out, expand=expand, contract=contract, vectors=vectors, first_in=first_in, first_out=first_out, first_expand=first_expand, first_contract=first_contract, first_vectors=first_vectors, second_in=second_in, second_out=second_out, second_expand=second_expand, second_contract=second_contract, second_vectors=second_vectors)


@jax.custom_vjp
def low(v):
    return lax.optimization_barrier(v.astype(jnp.bfloat16)).astype(jnp.float32)

@jax.custom_vjp
def low_back(v):
    return v

def low_keep(v):
    return (low(v), None)

def low_pass(kept, grad):
    return (grad,)

def back_keep(v):
    return (v, None)

def back_low(kept, grad):
    return (low(grad),)
low.defvjp(low_keep, low_pass)
low_back.defvjp(back_keep, back_low)
highest = lax.Precision.HIGHEST
norm_eps = 1e-06
clip_share = 0.05
matrix_rate = 0.04
vector_rate = 0.3
matrix_decay = 0.05
first_beta = 0.5
second_beta = 0.5
adam_eps = 1e-08

def layer_norm(values, gain, shift):
    centred = values - lax.optimization_barrier(jnp.mean(values, axis=-1, keepdims=True))
    spread = lax.optimization_barrier(jnp.mean(centred * centred, axis=-1, keepdims=True))
    return centred * lax.rsqrt(spread + norm_eps) * gain + shift

def to_crops(flat, count):
    shaped = flat.reshape(count, KEEP, HEADS, HEAD_DIM)
    wide = shaped[:, :2 * KEEP_GLOBAL].reshape(count * 2, KEEP_GLOBAL, HEADS, HEAD_DIM)
    narrow = shaped[:, 2 * KEEP_GLOBAL:].reshape(count * 4, KEEP_LOCAL, HEADS, HEAD_DIM)
    return (wide, narrow)

def from_crops(wide, narrow, count):
    joined = jnp.concatenate([wide.reshape(count, 2 * KEEP_GLOBAL, D), narrow.reshape(count, 4 * KEEP_LOCAL, D)], axis=1)
    return joined.reshape(count * KEEP, D)

def crop_attention(query, key_rows, value):
    scores = jnp.einsum('cqhe,ckhe->chqk', query, key_rows, precision=highest) * HEAD_DIM ** (-0.5)
    scores = low_back(scores)
    probs = low(jax.nn.softmax(scores, axis=-1))
    return jnp.einsum('chqk,ckhe->cqhe', probs, value, precision=highest)

def group_forward(inputs, slots, in_matrix, out_matrix, up_matrix, down_matrix, row_params):
    count = inputs.shape[0]
    picked = jnp.take_along_axis(inputs, slots[:, :, None], axis=1).reshape(count * KEEP, D)
    routed = jnp.dot(picked, row_params[8], precision=highest)
    normed = low(layer_norm(picked, row_params[0], row_params[1]))
    in_bias = jnp.concatenate([row_params[2], jnp.zeros((D,), jnp.float32), row_params[3]])
    mixed = jnp.dot(normed, in_matrix, precision=highest) + in_bias
    query = low(low_back(mixed[:, :D]))
    key_rows = low(low_back(mixed[:, D:2 * D]))
    value = low(low_back(mixed[:, 2 * D:]))
    wide_q, narrow_q = to_crops(query, count)
    wide_k, narrow_k = to_crops(key_rows, count)
    wide_v, narrow_v = to_crops(value, count)
    heads_out = from_crops(crop_attention(wide_q, wide_k, wide_v), crop_attention(narrow_q, narrow_k, narrow_v), count)
    heads_out = low(low_back(heads_out))
    attended = low_back(jnp.dot(heads_out, out_matrix, precision=highest) + row_params[4])
    residual = picked + attended
    normed_two = low(layer_norm(residual, row_params[5], row_params[6]))
    before = low_back(jnp.dot(normed_two, up_matrix, precision=highest) + row_params[9:].reshape(FF))
    active = low(jax.nn.gelu(before, approximate=False))
    mlp_out = low_back(jnp.dot(active, down_matrix, precision=highest) + row_params[7])
    branch = (attended + mlp_out) * routed[:, None]
    image_rows = jnp.arange(count, dtype=jnp.int32)[:, None]
    return inputs.at[image_rows, slots].add(branch.reshape(count, KEEP, D))

def adam_update(master, grad, first, second, rate, decay):
    first_new = first_beta * first + (1.0 - first_beta) * grad
    second_new = second_beta * second + (1.0 - second_beta) * grad * grad
    first_hat = first_new / (1.0 - first_beta ** STEP)
    second_hat = second_new / (1.0 - second_beta ** STEP)
    updated = master - rate * (first_hat / (jnp.sqrt(second_hat) + adam_eps) + decay * master)
    return (first_new, second_new, updated)

def reference(tokens, keep_slots, cotangent, project_in, project_out, expand, contract, vectors, first_in, first_out, first_expand, first_contract, first_vectors, second_in, second_out, second_expand, second_contract, second_vectors):
    slots = keep_slots.reshape(DEVICES, IMG_DEV, KEEP).astype(jnp.int32)

    def forward(inputs, in_matrix, out_matrix, up_matrix, down_matrix, row_params):
        lowered = (low(in_matrix), low(out_matrix), low(up_matrix), low(down_matrix), low(row_params))

        def one_group(pair):
            return group_forward(pair[0], pair[1], lowered[0], lowered[1], lowered[2], lowered[3], lowered[4])
        return lax.map(jax.checkpoint(one_group), (inputs, slots))
    images = tokens.reshape(DEVICES, IMG_DEV, IMG_TOK, D).astype(jnp.float32)
    outputs, pull = jax.vjp(forward, images, project_in, project_out, expand, contract, vectors)
    grads = pull(cotangent.reshape(DEVICES, IMG_DEV, IMG_TOK, D).astype(jnp.float32))
    activations = outputs.reshape(TOKENS, D).astype(jnp.bfloat16)
    input_grad = grads[0].reshape(TOKENS, D).astype(jnp.bfloat16)
    weight_grads = grads[1:]
    squares = jnp.sum(weight_grads[0] * weight_grads[0])
    for piece in weight_grads[1:]:
        squares = squares + jnp.sum(piece * piece)
    grad_norm = jnp.sqrt(squares)
    factor = jnp.minimum(1.0, clip_share * jnp.sqrt(jnp.float32(PARAMS)) / (grad_norm + 1e-06))
    masters = (project_in, project_out, expand, contract, vectors)
    firsts = (first_in, first_out, first_expand, first_contract, first_vectors)
    seconds = (second_in, second_out, second_expand, second_contract, second_vectors)
    rates = (matrix_rate, matrix_rate, matrix_rate, matrix_rate, vector_rate)
    decays = (matrix_decay, matrix_decay, matrix_decay, matrix_decay, 0.0)
    results = [adam_update(masters[index], weight_grads[index] * factor, firsts[index], seconds[index], rates[index], decays[index]) for index in range(5)]
    momenta = tuple((item[0] for item in results))
    variances = tuple((item[1] for item in results))
    updated = tuple((item[2] for item in results))
    copies = tuple((item.astype(jnp.bfloat16) for item in updated))
    return (activations, input_grad, grad_norm.reshape(1), momenta[0], momenta[1], momenta[2], momenta[3], momenta[4], variances[0], variances[1], variances[2], variances[3], variances[4], updated[0], updated[1], updated[2], updated[3], updated[4], copies[0], copies[1], copies[2], copies[3], copies[4])
```

```python
import functools
import math

import jax
import jax.numpy as jnp
from jax import lax
from jax.experimental import pallas as pl
from jax.experimental.pallas import tpu as pltpu
from jax.sharding import PartitionSpec as P

D = 768
HEADS = 12
HEAD_DIM = 64
KEEP_GLOBAL = 98
KEEP_LOCAL = 18
KEEP = 268
PARAMS = 7087872
STEP = 5

norm_eps = 1e-06
clip_share = 0.05
matrix_rate = 0.04
vector_rate = 0.3
matrix_decay = 0.05
first_beta = 0.5
second_beta = 0.5
adam_eps = 1e-08

AXES = ("dp", "fsdp")
BF = jnp.bfloat16
F32 = jnp.float32
NT = (((1,), (1,)), ((), ()))
TN = (((0,), (0,)), ((), ()))
PAD = -(-KEEP // 16) * 16
PAIRS = HEADS // 2
PW = 2 * HEAD_DIM
GROUPS = 3
CHUNKS = 2
HIDDEN = 4 * D
HALF = HIDDEN // CHUNKS // 2
VMEM_LIMIT = 60 * 2**20
NEG = -1e30
SEGMENTS = (
    (0, 112, 0, KEEP_GLOBAL),
    (96, 112, KEEP_GLOBAL, 2 * KEEP_GLOBAL),
    (192, 80, 2 * KEEP_GLOBAL, KEEP),
)


def nn(left, right):
    return jnp.dot(left, right, preferred_element_type=F32)


def nt(left, right):
    return lax.dot_general(left, right, NT, preferred_element_type=F32)


def tn(left, right):
    return lax.dot_general(left, right, TN, preferred_element_type=F32)


def params(**more):
    return pltpu.CompilerParams(vmem_limit_bytes=VMEM_LIMIT, **more)


def cost(flops, moved, exps=0):
    return pl.CostEstimate(flops=int(flops), bytes_accessed=int(moved), transcendentals=int(exps))


def whole(shape):
    return pl.BlockSpec(shape, lambda *_: (0,) * len(shape))


ANY = pl.BlockSpec(memory_space=pl.ANY)
SMEM = pl.BlockSpec(memory_space=pltpu.SMEM)


def normalize(values):
    centred = values - jnp.mean(values, axis=-1, keepdims=True)
    spread = jnp.mean(centred * centred, axis=-1, keepdims=True)
    inverse = lax.rsqrt(spread + norm_eps)
    return centred * inverse, inverse


def norm_back(grad, normed, inverse, gain):
    pulled = grad * gain
    return inverse * (
        pulled
        - jnp.mean(pulled, axis=-1, keepdims=True)
        - normed * jnp.mean(pulled * normed, axis=-1, keepdims=True)
    )


def column_sum(values):
    return jnp.sum(values, axis=0, keepdims=True)


def window_start(image, image_tokens, rows, window):
    return jnp.minimum((image_tokens * image) // 16, (rows - window) // 16) * 16


def pick_kernel(image_tokens, rows, window, slots, vec, tokens, cot, picked, grads, normed, mlp):
    image = pl.program_id(0)
    shift = image_tokens * image - window_start(image, image_tokens, rows, window)
    place = slots[0] + shift
    hot = (lax.broadcasted_iota(jnp.int32, (PAD, window), 1) == place).astype(F32).astype(BF)
    values = nn(hot, tokens[...])
    grad_rows = nn(hot, cot[...])
    picked[...] = values.astype(BF)
    grads[...] = grad_rows.astype(BF)
    gain = vec[0:1, :].astype(F32)
    shift_one = vec[1:2, :].astype(F32)
    router = vec[8:9, :].astype(F32)
    unit, _ = normalize(values)
    normed[...] = (unit * gain + shift_one).astype(BF)
    routed = jnp.sum(values * router, axis=-1, keepdims=True)
    mlp[...] = (routed * grad_rows).astype(BF)


def pick(tokens, cot, slots, vec):
    rows = tokens.shape[0]
    count = slots.shape[0]
    image_tokens = rows // count
    window = -(-(image_tokens + 15) // 16) * 16
    start = functools.partial(
        window_start, image_tokens=image_tokens, rows=rows, window=window
    )
    source = pl.BlockSpec((pl.Element(window), pl.Element(D)), lambda i: (start(i), 0))
    block = pl.BlockSpec((PAD, D), lambda i: (i, 0))
    shape = jax.ShapeDtypeStruct((count * PAD, D), BF)
    return pl.pallas_call(
        functools.partial(pick_kernel, image_tokens, rows, window),
        grid=(count,),
        in_specs=[
            pl.BlockSpec((1, PAD, 1), lambda i: (i, 0, 0)),
            whole((16, D)),
            source,
            source,
        ],
        out_specs=(block,) * 4,
        out_shape=(shape,) * 4,
        compiler_params=params(),
        cost_estimate=cost(4 * count * PAD * window * D, 4 * rows * D + 8 * count * PAD * D),
        name="pick_rows",
    )(slots, vec, tokens, cot)


def local_mask():
    first, rows, low, high = SEGMENTS[2]
    slot = jnp.arange(rows) + first
    crop = jnp.where((slot >= low) & (slot < high), (slot - low) // KEEP_LOCAL, -1)
    same = (crop[:, None] == crop[None, :]) & (crop[:, None] >= 0)
    bias = jnp.where(same, 0.0, NEG).astype(F32)
    return jnp.concatenate([bias, bias], axis=1)


def lanes_of(rows):
    return lax.broadcasted_iota(jnp.int32, (rows, PW), 1) < HEAD_DIM


def split_heads(values):
    first = lanes_of(values.shape[0])
    zero = jnp.zeros_like(values)
    return jnp.concatenate(
        [jnp.where(first, values, zero), jnp.where(first, zero, values)], axis=0
    )


def join_heads(values):
    rows = values.shape[0] // 2
    return jnp.where(lanes_of(rows), values[:rows], values[rows:])


def probabilities(segment, mask, keys, queries):
    first, rows, low, high = segment
    scores = nt(keys, queries)
    if low == 2 * KEEP_GLOBAL:
        scores = scores + mask
    else:
        slot = lax.broadcasted_iota(jnp.int32, (rows, 1), 0) + first
        scores = jnp.where((slot >= low) & (slot < high), scores, NEG)
    grown = jnp.exp(scores - jnp.max(scores, axis=0, keepdims=True))
    return grown * (1.0 / jnp.sum(grown, axis=0, keepdims=True))


def attention(query, key_rows, value, mask, store):
    parts = []
    for segment in SEGMENTS:
        rows = slice(segment[0], segment[0] + segment[1])
        halves = split_heads(query[rows] * BF(HEAD_DIM**-0.5))
        probs = probabilities(segment, mask, key_rows[rows], halves).astype(BF)
        parts.append(join_heads(tn(probs, value[rows])))
    one, two, three = parts
    slot = lax.broadcasted_iota(jnp.int32, (16, 1), 0)
    store(0, one[:96])
    store(96, jnp.where(slot + 96 < KEEP_GLOBAL, one[96:], two[:16]))
    store(112, two[16:96])
    store(192, jnp.where(slot + 192 < 2 * KEEP_GLOBAL, two[96:], three[:16]))
    store(208, three[16:])


def attention_back(query, key_rows, value, grad, mask):
    results = []
    for segment in SEGMENTS:
        first, count, low, high = segment
        rows = slice(first, first + count)
        halves = split_heads(query[rows] * BF(HEAD_DIM**-0.5))
        slot = lax.broadcasted_iota(jnp.int32, (count, 1), 0) + first
        kept = jnp.where((slot >= low) & (slot < high), grad[rows], jnp.zeros((), BF))
        grads = split_heads(kept)
        probs = probabilities(segment, mask, key_rows[rows], halves)
        grad_probs = nt(value[rows], grads)
        weighted = jnp.sum(probs * grad_probs, axis=0, keepdims=True)
        grad_scores = (probs * (grad_probs - weighted)).astype(BF)
        grad_value = nn(probs.astype(BF), grads)
        grad_key = nn(grad_scores, halves)
        grad_query = join_heads(tn(grad_scores, key_rows[rows])) * HEAD_DIM**-0.5
        results.append((grad_query, grad_key, grad_value))
    joined = []
    for one, two, three in zip(*results):
        joined.append(
            jnp.concatenate(
                [
                    one[:96],
                    one[96:] + two[:16],
                    two[16:96],
                    two[96:] + three[:16],
                    three[16:],
                ],
                axis=0,
            )
        )
    return joined


def pair_lanes(place, group, own):
    core = place[2]
    pair = 2 * group + (core if own else 1 - core)
    return pl.ds(pl.multiple_of(pair * PW, PW), PW)


def heads_kernel(group, place, mask, vec, normed, own_w, other_w, *outs):
    rows = normed[...]
    for own, weight, mixed, heads in (
        (True, own_w, outs[0], outs[2]),
        (False, other_w, outs[1], outs[3]),
    ):
        lanes = pair_lanes(place, group, own)
        product = nn(rows, weight[...])
        query = (product[:, :PW] + vec[2:3, lanes].astype(F32)).astype(BF)
        key_rows = product[:, PW : 2 * PW].astype(BF)
        value = (product[:, 2 * PW :] + vec[3:4, lanes].astype(F32)).astype(BF)
        mixed[:, :PW] = query
        mixed[:, PW : 2 * PW] = key_rows
        mixed[:, 2 * PW :] = value

        def store(first, values, heads=heads):
            heads[first : first + values.shape[0], :] = values.astype(BF)

        attention(query, key_rows, value, mask[...], store)


def heads_forward(group, place, mask, vec, normed, own_w, other_w):
    rows = normed.shape[0]
    count = rows // PAD
    block = pl.BlockSpec((PAD, 3 * PW), lambda i: (i, 0))
    small = pl.BlockSpec((PAD, PW), lambda i: (i, 0))
    return pl.pallas_call(
        functools.partial(heads_kernel, group),
        grid=(count,),
        in_specs=[
            SMEM,
            whole(mask.shape),
            whole((16, D)),
            pl.BlockSpec((PAD, D), lambda i: (i, 0)),
            whole((D, 3 * PW)),
            whole((D, 3 * PW)),
        ],
        out_specs=(block, block, small, small),
        out_shape=(jax.ShapeDtypeStruct((rows, 3 * PW), BF),) * 2
        + (jax.ShapeDtypeStruct((rows, PW), BF),) * 2,
        compiler_params=params(),
        cost_estimate=cost(6 * 2 * rows * D * PW + rows * 2e5, 8 * rows * D, rows * 400),
        name=f"attention_{group}",
    )(place, mask, vec, normed, own_w, other_w)


def heads_back_kernel(
    group, count, place, mask, grad_attended, normed, w_out, mixed_own, mixed_other, *rest
):
    (gm_own, gm_other, gw_own, gw_other, sums_own, sums_other, kept_normed, kept_own, kept_other) = rest
    step = pl.program_id(0)

    @pl.when(step == 0)
    def _():
        sums_own[...] = jnp.zeros_like(sums_own)
        sums_other[...] = jnp.zeros_like(sums_other)

    @pl.when(step < count)
    def _():
        rows = pl.ds(pl.multiple_of(step * PAD, 16), PAD)
        kept_normed[rows, :] = normed[...]
        incoming = grad_attended[...]
        for own, mixed, out, kept, sums in (
            (False, mixed_other, gm_other, kept_other, sums_other),
            (True, mixed_own, gm_own, kept_own, sums_own),
        ):
            lanes = pair_lanes(place, group, own)
            grad_heads = nt(incoming, w_out[lanes, :]).astype(BF)
            parts = attention_back(
                mixed[:, :PW], mixed[:, PW : 2 * PW], mixed[:, 2 * PW :], grad_heads, mask[...]
            )
            for index, part in enumerate(parts):
                low = part.astype(BF)
                columns = slice(index * PW, (index + 1) * PW)
                out[:, columns] = low
                kept[rows, columns] = low
                sums[0:1, columns] += column_sum(low.astype(F32))

    @pl.when(step == count)
    def _():
        gw_other[...] = tn(kept_normed[...], kept_other[...]).astype(BF)
        gw_own[...] = tn(kept_normed[...], kept_own[...]).astype(BF)


def heads_backward(group, place, mask, grad_attended, normed, w_out, mixed_own, mixed_other):
    rows = normed.shape[0]
    count = rows // PAD
    last = count - 1
    wide = pl.BlockSpec((PAD, D), lambda i: (jnp.minimum(i, last), 0))
    block = pl.BlockSpec((PAD, 3 * PW), lambda i: (jnp.minimum(i, last), 0))
    mixed_shape = jax.ShapeDtypeStruct((rows, 3 * PW), BF)
    weight_shape = jax.ShapeDtypeStruct((D, 3 * PW), BF)
    sum_shape = jax.ShapeDtypeStruct((8, 3 * PW), F32)
    return pl.pallas_call(
        functools.partial(heads_back_kernel, group, count),
        grid=(count + 1,),
        in_specs=[SMEM, whole(mask.shape), wide, wide, whole((D, D)), block, block],
        out_specs=(block, block)
        + (whole((D, 3 * PW)),) * 2
        + (whole((8, 3 * PW)),) * 2,
        out_shape=(mixed_shape,) * 2 + (weight_shape,) * 2 + (sum_shape,) * 2,
        scratch_shapes=[
            pltpu.VMEM((rows, D), BF),
            pltpu.VMEM((rows, 3 * PW), BF),
            pltpu.VMEM((rows, 3 * PW), BF),
        ],
        compiler_params=params(),
        cost_estimate=cost(
            2 * rows * D * 2 * PW + 2 * rows * D * 6 * PW + rows * 5e5, 12 * rows * D, rows * 400
        ),
        name=f"attention_back_{group}",
    )(place, mask, grad_attended, normed, w_out, mixed_own, mixed_other)


def mix_kernel(place, vec, picked, own_w, other_w, *refs):
    heads = refs[: 2 * GROUPS]
    attended, normed, joined, w_full = refs[2 * GROUPS :]
    core = place[2]
    half = D // 2

    @pl.when(pl.program_id(0) == 0)
    def _():
        w_full[:, pl.ds(pl.multiple_of(core * half, 128), half)] = own_w[...]
        w_full[:, pl.ds(pl.multiple_of((1 - core) * half, 128), half)] = other_w[...]

    for group in range(GROUPS):
        joined[:, pair_lanes(place, group, True)] = heads[2 * group][...]
        joined[:, pair_lanes(place, group, False)] = heads[2 * group + 1][...]
    result = nn(joined[...], w_full[...]) + vec[4:5, :].astype(F32)
    attended[...] = result
    unit, _ = normalize(picked[...].astype(F32) + result)
    normed[...] = (unit * vec[5:6, :].astype(F32) + vec[6:7, :].astype(F32)).astype(BF)


def mix(place, vec, picked, own_w, other_w, heads):
    rows = picked.shape[0]
    size = 2 * PAD
    wide = pl.BlockSpec((size, D), lambda i: (i, 0))
    small = pl.BlockSpec((size, PW), lambda i: (i, 0))
    return pl.pallas_call(
        mix_kernel,
        grid=(rows // size,),
        in_specs=[SMEM, whole((16, D)), wide, whole((D, D // 2)), whole((D, D // 2))]
        + [small] * (2 * GROUPS),
        out_specs=(wide, wide, wide, whole((D, D))),
        out_shape=(
            jax.ShapeDtypeStruct((rows, D), F32),
            jax.ShapeDtypeStruct((rows, D), BF),
            jax.ShapeDtypeStruct((rows, D), BF),
            jax.ShapeDtypeStruct((D, D), BF),
        ),
        compiler_params=params(),
        cost_estimate=cost(2 * rows * D * D, 12 * rows * D),
        name="project_and_norm",
    )(place, vec, picked, own_w, other_w, *heads)


ERF_P = 0.3275911 / math.sqrt(2.0)
ERF_A = (0.254829592, -0.284496736, 1.421413741, -1.453152027, 1.061405429)


def gelu_and_slope(values):
    t = 1.0 / (1.0 + ERF_P * jnp.abs(values))
    bell = jnp.exp(-0.5 * values * values)
    tail = (0.5 * ERF_A[4]) * t + 0.5 * ERF_A[3]
    for factor in (ERF_A[2], ERF_A[1], ERF_A[0]):
        tail = tail * t + 0.5 * factor
    tail = tail * t * bell
    below = jnp.where(values >= 0, 1.0 - tail, tail)
    return values * below, below + values * bell * (1.0 / math.sqrt(2.0 * math.pi))


TILE = 256


def mlp_kernel(chunk, steps, size, place, bias, normed, grad, *refs):
    weights = refs[:4]
    refs = refs[4:]
    if chunk:
        out_before, back_before = refs[:2]
        refs = refs[2:]
    (out, back, gw1_other, gw2_other, gw1_own, gw2_own, sums) = refs[:7]
    kept_normed, kept_grad, kept_active, kept_before = refs[7:]
    step = pl.program_id(0)
    core = place[2]
    tiles = HALF // TILE

    @pl.when(step == 0)
    def _():
        sums[...] = jnp.zeros_like(sums)

    @pl.when(step < steps)
    def _():
        rows = pl.ds(pl.multiple_of(step * size, 16), size)
        left = normed[...]
        right = grad[...]
        kept_normed[rows, :] = left
        kept_grad[rows, :] = right
        for half in range(2):
            parity = core if half else 1 - core
            up, down = weights[2 * half], weights[2 * half + 1]
            for tile in range(tiles):
                columns = slice(tile * TILE, (tile + 1) * TILE)
                kept = slice(half * HALF + tile * TILE, half * HALF + (tile + 1) * TILE)
                before = nn(left, up[:, columns]) + bias[2 * chunk + parity, :, columns]
                active, slope = gelu_and_slope(before)
                kept_active[rows, kept] = active.astype(BF)
                low = (nt(right, down[columns, :]) * slope).astype(BF)
                kept_before[rows, kept] = low
                sums[parity, :, columns] += column_sum(low.astype(F32))
        result = nn(kept_active[rows, :HALF], weights[1][...])
        result += nn(kept_active[rows, HALF:], weights[3][...])
        pulled = nt(kept_before[rows, :HALF], weights[0][...])
        pulled += nt(kept_before[rows, HALF:], weights[2][...])
        if chunk:
            result += out_before[...]
            pulled += back_before[...]
        out[...] = result
        back[...] = pulled

    @pl.when(step >= steps)
    def _():
        tile = step - steps
        columns = pl.ds(pl.multiple_of(tile * TILE, TILE), TILE)
        for_up = tn(kept_normed[...], kept_before[:, columns]).astype(BF)
        for_down = tn(kept_active[:, columns], kept_grad[...]).astype(BF)

        @pl.when(tile < tiles)
        def _():
            gw1_other[...] = for_up
            gw2_other[...] = for_down

        @pl.when(tile >= tiles)
        def _():
            gw1_own[...] = for_up
            gw2_own[...] = for_down


def mlp(chunk, place, bias, normed, grad, weights, sums_before):
    rows = normed.shape[0]
    size = 2 * PAD
    steps = rows // size
    last = steps - 1
    tiles = HALF // TILE
    wide = pl.BlockSpec((size, D), lambda i: (jnp.minimum(i, last), 0))
    once = dict(pipeline_mode=pl.Buffered(1))
    up = pl.BlockSpec((D, HALF), lambda i: (0, 0), **once)
    down = pl.BlockSpec((HALF, D), lambda i: (0, 0), **once)

    def tile_of(i, first):
        return jnp.clip(i - steps - first, 0, tiles - 1)

    def gw1(first):
        return pl.BlockSpec((D, TILE), lambda i: (0, tile_of(i, first)))

    def gw2(first):
        return pl.BlockSpec((TILE, D), lambda i: (tile_of(i, first), 0))

    total = jax.ShapeDtypeStruct((rows, D), F32)
    up_shape = jax.ShapeDtypeStruct((D, HALF), BF)
    down_shape = jax.ShapeDtypeStruct((HALF, D), BF)
    return pl.pallas_call(
        functools.partial(mlp_kernel, chunk, steps, size),
        grid=(steps + 2 * tiles,),
        in_specs=[SMEM, whole(bias.shape), wide, wide, up, down, up, down]
        + [wide] * len(sums_before),
        out_specs=(wide, wide, gw1(0), gw2(0), gw1(tiles), gw2(tiles), whole((2, 1, HALF))),
        out_shape=(
            total,
            total,
            up_shape,
            down_shape,
            up_shape,
            down_shape,
            jax.ShapeDtypeStruct((2, 1, HALF), F32),
        ),
        scratch_shapes=[
            pltpu.VMEM((rows, D), BF),
            pltpu.VMEM((rows, D), BF),
            pltpu.VMEM((rows, 2 * HALF), BF),
            pltpu.VMEM((rows, 2 * HALF), BF),
        ],
        compiler_params=params(),
        cost_estimate=cost(
            24 * rows * D * HALF, 12 * rows * D + 16 * D * HALF, 4 * rows * HALF
        ),
        name=f"feed_forward_{chunk}",
    )(place, bias, normed, grad, *weights, *sums_before)


def turn_kernel(steps, size, place, vec, picked, grads, attended, out, back, heads, *refs):
    (grad_attended, carry, values, sums, gw_own, gw_other, kept_heads, kept_grad) = refs
    step = pl.program_id(0)
    core = place[2]
    half = D // 2

    @pl.when(step == 0)
    def _():
        sums[...] = jnp.zeros_like(sums)

    @pl.when(step < steps)
    def _():
        rows = pl.ds(pl.multiple_of(step * size, 16), size)
        inputs = picked[...].astype(F32)
        grad_rows = grads[...].astype(F32)
        router = vec[8:9, :].astype(F32)
        routed = jnp.sum(inputs * router, axis=-1, keepdims=True)
        mixed = attended[...]
        branch = mixed + out[...] + vec[7:8, :].astype(F32)
        values[...] = (inputs + routed * branch).astype(BF)
        grad_routed = jnp.sum(grad_rows * branch, axis=-1, keepdims=True)
        grad_branch = routed * grad_rows
        unit, inverse = normalize(inputs + mixed)
        pulled = back[...]
        residual = norm_back(pulled, unit, inverse, vec[5:6, :].astype(F32))
        low = (grad_branch + residual).astype(BF)
        grad_attended[...] = low
        kept_grad[rows, :] = low
        kept_heads[rows, :] = heads[...]
        carry[...] = residual + grad_routed * router
        sums[0:1, :] += column_sum(low.astype(F32))
        sums[1:2, :] += column_sum(pulled * unit)
        sums[2:3, :] += column_sum(pulled)
        sums[3:4, :] += column_sum(grad_branch.astype(BF).astype(F32))
        sums[4:5, :] += column_sum(inputs * grad_routed)

    @pl.when(step == steps)
    def _():
        own = pl.ds(pl.multiple_of(core * half, 128), half)
        other = pl.ds(pl.multiple_of((1 - core) * half, 128), half)
        gw_own[...] = tn(kept_heads[...], kept_grad[:, own]).astype(BF)
        gw_other[...] = tn(kept_heads[...], kept_grad[:, other]).astype(BF)


def turn(place, vec, picked, grads, attended, out, back, heads):
    rows = picked.shape[0]
    size = 2 * PAD
    steps = rows // size
    last = steps - 1
    wide = pl.BlockSpec((size, D), lambda i: (jnp.minimum(i, last), 0))
    return pl.pallas_call(
        functools.partial(turn_kernel, steps, size),
        grid=(steps + 1,),
        in_specs=[SMEM, whole((16, D))] + [wide] * 6,
        out_specs=(wide, wide, wide, whole((8, D)), whole((D, D // 2)), whole((D, D // 2))),
        out_shape=(
            jax.ShapeDtypeStruct((rows, D), BF),
            jax.ShapeDtypeStruct((rows, D), F32),
            jax.ShapeDtypeStruct((rows, D), BF),
            jax.ShapeDtypeStruct((8, D), F32),
            jax.ShapeDtypeStruct((D, D // 2), BF),
            jax.ShapeDtypeStruct((D, D // 2), BF),
        ),
        scratch_shapes=[pltpu.VMEM((rows, D), BF), pltpu.VMEM((rows, D), BF)],
        compiler_params=params(),
        cost_estimate=cost(2 * rows * D * D, 26 * rows * D),
        name="second_norm_back",
    )(place, vec, picked, grads, attended, out, back, heads)


def first_back_kernel(vec, picked, grads, carry, *refs):
    mixed = refs[: 2 * GROUPS]
    weights = refs[2 * GROUPS : 4 * GROUPS]
    values, sums = refs[4 * GROUPS :]

    @pl.when(pl.program_id(0) == 0)
    def _():
        sums[...] = jnp.zeros_like(sums)

    pulled = nt(mixed[0][...], weights[0][...])
    for left, right in zip(mixed[1:], weights[1:]):
        pulled += nt(left[...], right[...])
    unit, inverse = normalize(picked[...].astype(F32))
    grad = norm_back(pulled, unit, inverse, vec[0:1, :].astype(F32))
    values[...] = (grads[...].astype(F32) + grad + carry[...]).astype(BF)
    sums[0:1, :] += column_sum(pulled * unit)
    sums[1:2, :] += column_sum(pulled)


def first_back(vec, picked, grads, carry, mixed, weights):
    rows = picked.shape[0]
    size = 2 * PAD
    wide = pl.BlockSpec((size, D), lambda i: (i, 0))
    block = pl.BlockSpec((size, 3 * PW), lambda i: (i, 0))
    return pl.pallas_call(
        first_back_kernel,
        grid=(rows // size,),
        in_specs=[whole((16, D)), wide, wide, wide]
        + [block] * (2 * GROUPS)
        + [whole((D, 3 * PW))] * (2 * GROUPS),
        out_specs=(wide, whole((8, D))),
        out_shape=(jax.ShapeDtypeStruct((rows, D), BF), jax.ShapeDtypeStruct((8, D), F32)),
        compiler_params=params(),
        cost_estimate=cost(6 * rows * D * D, 16 * rows * D),
        name="first_norm_back",
    )(vec, picked, grads, carry, *mixed, *weights)


def put_kernel(span, places, *refs):
    half = len(refs) // 4
    sources, values, nexts, outs = (refs[i * half : (i + 1) * half] for i in range(4))
    width = places.shape[2]
    hot = lax.broadcasted_iota(jnp.int32, (span, width), 0) == places[0]
    hot = hot.astype(F32).astype(BF)
    kept = nn(hot, jnp.ones((width, 128), BF)) > 0.5
    for source, value, after, out in zip(sources, values, nexts, outs):
        moved = nn(hot[:, :PAD], value[...]) + nn(hot[:, PAD:], after[...])
        for tile in range(D // 128):
            lanes = slice(tile * 128, (tile + 1) * 128)
            out[:, lanes] = jnp.where(kept, moved[:, lanes].astype(BF), source[:, lanes])


def put(places, sources, values):
    rows = sources[0].shape[0]
    count = places.shape[0]
    span = -(-(rows // count) // 16) * 16
    block = pl.BlockSpec((span, D), lambda i: (i, 0))
    value = pl.BlockSpec((PAD, D), lambda i: (i, 0))
    after = pl.BlockSpec((16, D), lambda i: (jnp.minimum(i + 1, count - 1) * (PAD // 16), 0))
    kinds = len(sources)
    return pl.pallas_call(
        functools.partial(put_kernel, span),
        grid=(count,),
        in_specs=[pl.BlockSpec((1, 1, places.shape[2]), lambda i: (i, 0, 0))]
        + [block] * kinds
        + [value] * kinds
        + [after] * kinds,
        out_specs=(block,) * kinds,
        out_shape=(jax.ShapeDtypeStruct((rows, D), BF),) * kinds,
        compiler_params=params(),
        cost_estimate=cost(2 * kinds * rows * D * (PAD + 16), kinds * 6 * rows * D),
        name="put_rows",
    )(places, *sources, *values, *values)


def put_places(keep_slots, image_tokens):
    count = keep_slots.shape[0]
    span = -(-image_tokens // 16) * 16
    image = jnp.arange(count, dtype=jnp.int32)[:, None]
    own = keep_slots + image * (image_tokens - span)
    following = jnp.concatenate([keep_slots[1:, :16], jnp.full((1, 16), -span, jnp.int32)], axis=0)
    following = following + (image + 1) * image_tokens - image * span
    following = jnp.where(image < count - 1, following, -1)
    gap = jnp.full((count, PAD - KEEP), -1, jnp.int32)
    return jnp.concatenate([own, gap, following], axis=1)[:, None, :]


class Moves:
    def __init__(self, n_dp, n_fsdp):
        self.n_dp = n_dp
        self.n_fsdp = n_fsdp
        self.squares = n_fsdp // 2
        outer = lax.axis_index("dp")
        inner = lax.axis_index("fsdp")
        self.z = outer
        self.yx = inner // 2
        self.core = inner % 2
        self.place = jnp.stack([self.z, self.yx, self.core]).astype(jnp.int32)

    def swap(self, value, mask):
        total = self.n_dp * self.n_fsdp
        return lax.ppermute(value, AXES, [(i, i ^ mask) for i in range(total)])

    def over_z(self, values):
        return [self.swap(value, k * self.n_fsdp) for k, value in enumerate(values) if k]

    def over_yx(self, values):
        return [self.swap(value, 2 * k) for k, value in enumerate(values) if k]

    def over_core(self, value):
        return self.swap(value, 1)

    def sum_all(self, value):
        total = value
        for part in self.over_z([value] * self.n_dp):
            total = total + part
        value = total
        for part in self.over_yx([value] * self.squares):
            total = total + part
        return total + self.over_core(total)

    def along_z(self, piece):
        return place_blocks(self.place, 0, [piece] + self.over_z([piece] * self.n_dp))

    def along_yx(self, stacked):
        parts = [stacked] + self.over_yx([stacked] * self.squares)
        return place_blocks(self.place, 1, parts).reshape(-1, stacked.shape[2])


class Scatter:
    def __init__(self, moves, keeps, sends):
        self.moves = moves
        chips = moves.n_dp * moves.squares

        def shaped(value):
            return value.reshape(moves.n_dp, moves.squares, value.shape[0] // chips, value.shape[1])

        self.arrived = [shaped(moves.over_core(value)) for value in sends]
        self.keeps = [shaped(value) for value in keeps]

    def add_cores(self, place):
        blocks = add_pairs(place, self.keeps, self.arrived, self.moves.squares)
        self.squares = [[block[0]] + self.moves.over_yx(block) for block in blocks]
        return [block[0] for block in blocks]

    def add_squares(self, place):
        blocks = add_blocks(place, self.squares, self.moves.n_dp)
        self.lines = [[block[0]] + self.moves.over_z(block) for block in blocks]
        return [block[0] for block in blocks]

    def finish(self):
        results = []
        for line in self.lines:
            total = line[0].astype(F32)
            for part in line[1:]:
                total = total + part.astype(F32)
            results.append(total)
        return results


def after(value, *others):
    return lax.optimization_barrier((value, *others))[0]


def place_kernel(axis, count, place, *refs):
    out = refs[count]
    me = place[axis]
    for k in range(count):
        if axis == 0:
            out[me ^ k] = refs[k][...]
        else:
            out[:, me ^ k] = refs[k][...]


def place_blocks(place, axis, blocks):
    count = len(blocks)
    shape = blocks[0].shape
    stacked = shape[:axis] + (count,) + shape[axis:]
    return pl.pallas_call(
        functools.partial(place_kernel, axis, count),
        in_specs=[SMEM] + [pl.BlockSpec(memory_space=pltpu.VMEM)] * count,
        out_specs=pl.BlockSpec(memory_space=pltpu.VMEM),
        out_shape=jax.ShapeDtypeStruct(stacked, blocks[0].dtype),
        compiler_params=params(),
        cost_estimate=cost(0, 4 * count * math.prod(shape)),
        name="place_blocks",
    )(place, *blocks)


def add_pairs_kernel(count, place, *refs):
    for index in range(count):
        total = refs[index][...].astype(F32) + refs[count + index][...].astype(F32)
        refs[2 * count + index][...] = total[:, 0].astype(BF)


def add_pairs(place, keeps, arrived, squares):
    specs, outs, shapes, left, right = [], [], [], [], []
    for keep, other in zip(keeps, arrived):
        n_dp, _, m, n = keep.shape
        for k in range(squares):
            specs.append(
                pl.BlockSpec((n_dp, 1, m, n), lambda i, place, k=k: (0, place[1] ^ k, 0, 0))
            )
            outs.append(pl.BlockSpec((n_dp, m, n), lambda i, place: (0, 0, 0)))
            shapes.append(jax.ShapeDtypeStruct((n_dp, m, n), BF))
            left.append(keep)
            right.append(other)
    count = len(left)
    results = pl.pallas_call(
        functools.partial(add_pairs_kernel, count),
        grid_spec=pltpu.PrefetchScalarGridSpec(
            num_scalar_prefetch=1, grid=(1,), in_specs=specs + specs, out_specs=outs
        ),
        out_shape=shapes,
        compiler_params=params(),
        cost_estimate=cost(0, 6 * sum(math.prod(keep.shape) for keep in keeps)),
        name="add_cores",
    )(place, *left, *right)
    return [results[i * squares : (i + 1) * squares] for i in range(len(keeps))]


def add_blocks_kernel(count, terms, place, *refs):
    for index in range(count):
        total = refs[index * terms][...].astype(F32)
        for term in range(1, terms):
            total = total + refs[index * terms + term][...].astype(F32)
        refs[count * terms + index][...] = total[0].astype(BF)


def add_blocks(place, groups, n_dp):
    specs, outs, shapes, operands = [], [], [], []
    terms = len(groups[0])
    for arrays in groups:
        m, n = arrays[0].shape[1:]
        for k in range(n_dp):
            spec = pl.BlockSpec((1, m, n), lambda i, place, k=k: (place[0] ^ k, 0, 0))
            specs += [spec] * terms
            operands += arrays
            outs.append(pl.BlockSpec((m, n), lambda i, place: (0, 0)))
            shapes.append(jax.ShapeDtypeStruct((m, n), BF))
    results = pl.pallas_call(
        functools.partial(add_blocks_kernel, len(shapes), terms),
        grid_spec=pltpu.PrefetchScalarGridSpec(
            num_scalar_prefetch=1, grid=(1,), in_specs=specs, out_specs=outs
        ),
        out_shape=shapes,
        compiler_params=params(),
        cost_estimate=cost(0, 4 * sum(math.prod(a.shape) for g in groups for a in g)),
        name="add_squares",
    )(place, *operands)
    return [results[i * n_dp : (i + 1) * n_dp] for i in range(len(groups))]


def adam_update(master, grad, first, second, rate, decay):
    first_new = first_beta * first + (1.0 - first_beta) * grad
    second_new = second_beta * second + (1.0 - second_beta) * grad * grad
    first_hat = first_new / (1.0 - first_beta**STEP)
    second_hat = second_new / (1.0 - second_beta**STEP)
    updated = master - rate * (first_hat / (jnp.sqrt(second_hat) + adam_eps) + decay * master)
    return (first_new, second_new, updated)


def on_device(
    n_dp,
    n_fsdp,
    tokens,
    keep_slots,
    cotangent,
    project_in,
    project_out,
    expand,
    contract,
    vectors,
    first_in,
    first_out,
    first_expand,
    first_contract,
    first_vectors,
    second_in,
    second_out,
    second_expand,
    second_contract,
    second_vectors,
):
    moves = Moves(n_dp, n_fsdp)
    place, core = moves.place, moves.core
    total = n_dp * n_fsdp
    chips = total // 2
    rows_in = project_in.shape[0]
    units = contract.shape[0]
    per_chunk = units // CHUNKS
    owner = moves.z * n_fsdp + lax.axis_index("fsdp")

    columns = vectors.shape[1]
    padded = jnp.pad(vectors.astype(BF), ((0, 16 - vectors.shape[0]), (0, 0)))
    vec = lax.dynamic_update_slice(jnp.zeros((16, D), BF), padded, (0, owner * columns))
    vec = moves.sum_all(vec)

    def pair_columns(value, pair):
        return [value[:, part * D + pair * PW : part * D + (pair + 1) * PW] for part in range(3)]

    low_in = project_in.astype(BF)
    low_out = project_out.astype(BF)
    low_up = expand.astype(BF).reshape(rows_in, chips, 2, CHUNKS, per_chunk)
    low_up = low_up.transpose(0, 3, 2, 1, 4).reshape(rows_in, CHUNKS, 2, HALF)
    low_down = contract.astype(BF)
    halves = []
    for parity in range(2):
        parts = []
        for group in range(GROUPS):
            parts += pair_columns(low_in, 2 * group + parity)
        parts.append(low_out[:, parity * (D // 2) : (parity + 1) * (D // 2)])
        parts += [low_up[:, chunk, parity] for chunk in range(CHUNKS)]
        halves.append(jnp.concatenate(parts, axis=1))
    mine = jnp.where(core == 0, halves[0], halves[1])
    theirs = jnp.where(core == 0, halves[1], halves[0])
    arrived = moves.over_core(theirs)
    rows = jnp.where(
        core == 0,
        jnp.concatenate([mine, arrived], axis=0),
        jnp.concatenate([arrived, mine], axis=0),
    )

    step = 3 * PW
    at = GROUPS * step
    pieces = [rows[:, group * step : (group + 1) * step] for group in range(GROUPS - 1)]
    pieces.append(rows[:, (GROUPS - 1) * step : at + D // 2])
    at += D // 2
    for chunk in range(CHUNKS):
        pieces.append(rows[:, at + chunk * HALF : at + (chunk + 1) * HALF])
        pieces.append(low_down[chunk * per_chunk : (chunk + 1) * per_chunk])
    stacked = []
    for index, piece in enumerate(pieces):
        if index:
            piece = after(piece, stacked[-1])
        stacked.append(moves.along_z(piece))
    gathered = []
    for index, stack in enumerate(stacked):
        if index:
            stack = after(stack, gathered[-1][0])
        own = moves.along_yx(stack)
        gathered.append((own, moves.over_core(own)))
    w_in = gathered[: GROUPS - 1]
    w_in.append(tuple(value[:, :step] for value in gathered[GROUPS - 1]))
    w_out = tuple(value[:, step:] for value in gathered[GROUPS - 1])
    w_up = gathered[GROUPS::2]
    w_down = gathered[GROUPS + 1 :: 2]

    count = keep_slots.shape[0]
    image_tokens = tokens.shape[0] // count
    slots = jnp.pad(keep_slots, ((0, 0), (0, PAD - KEEP)), constant_values=-4 * image_tokens)
    picked, grad_rows, normed_one, grad_mlp = pick(tokens, cotangent, slots[:, :, None], vec)
    mask = local_mask()
    mixed, heads = [], []
    for group in range(GROUPS):
        mixed_own, mixed_other, heads_own, heads_other = heads_forward(
            group, after(place, *heads[-1:]), mask, vec, normed_one, *w_in[group]
        )
        mixed.append((mixed_own, mixed_other))
        heads += [heads_own, heads_other]
    attended, normed_two, heads_out, w_out_full = mix(place, vec, picked, *w_out, heads)

    bias = vec[9:13].astype(F32).reshape(chips, 2, CHUNKS, per_chunk)
    bias = bias.transpose(2, 1, 0, 3).reshape(CHUNKS * 2, 1, HALF)
    sums, up_down, bias_sums = (), [], []
    here = place
    for chunk in range(CHUNKS):
        own_up, other_up = w_up[chunk]
        own_down, other_down = w_down[chunk]
        result = mlp(
            chunk,
            here,
            bias,
            normed_two,
            grad_mlp,
            (other_up, other_down, own_up, own_down),
            sums,
        )
        sums = result[:2]
        gw1_other, gw2_other, gw1_own, gw2_own, hidden_sums = result[2:]
        up_down.append(Scatter(moves, [gw1_own, gw2_own], [gw1_other, gw2_other]))
        bias_sums.append(hidden_sums)
        if chunk == 0:
            here = after(place, *up_down[0].add_cores(place))

    here = after(place, *up_down[0].add_squares(after(place, sums[0])))
    grad_attended, carry, put_values, turn_sums, gw_own, gw_other = turn(
        here, vec, picked, grad_rows, attended, *sums, heads_out
    )
    here = after(place, *up_down[1].add_cores(after(place, grad_attended)))
    sum_in, grad_mixed, mixed_sums = [], [], []
    out_keep, out_send = gw_own, gw_other
    for group in range(GROUPS):
        gm_own, gm_other, gw_own, gw_other, sums_own, sums_other = heads_backward(
            group, here, mask, grad_attended, normed_one, w_out_full, *mixed[group]
        )
        grad_mixed += [gm_own, gm_other]
        if group == 0:
            sum_in.append(Scatter(moves, [out_keep, gw_own], [out_send, gw_other]))
            here = after(place, gm_own)
        else:
            sum_in.append(Scatter(moves, [gw_own], [gw_other]))
            done = sum_in[group - 1].add_cores(after(place, gm_own))
            if group == 1:
                done += up_down[1].add_squares(after(place, gm_own))
            else:
                done += sum_in[group - 2].add_squares(after(place, gm_own))
            here = after(place, *done)
        in_order = jnp.where(
            core == 0,
            jnp.stack([sums_own[0], sums_other[0]]),
            jnp.stack([sums_other[0], sums_own[0]]),
        )
        mixed_sums.append(in_order.reshape(2, 3, PW))
    grad_values, first_sums = first_back(
        after(vec, here),
        picked,
        grad_rows,
        carry,
        grad_mixed,
        [weight for pair in w_in for weight in pair],
    )
    done = sum_in[1].add_squares(after(place, grad_values))
    done += sum_in[2].add_cores(after(place, grad_values))
    places = put_places(keep_slots, image_tokens)
    (activations,) = put(after(places, *done), (tokens,), (put_values,))
    done = sum_in[2].add_squares(after(place, activations))
    (input_grad,) = put(after(places, *done), (cotangent,), (grad_values,))
    up_down = [part.finish() for part in up_down]
    sum_in = [part.finish() for part in sum_in]
    sum_out = sum_in[0][0]
    sum_in = [part[-1] for part in sum_in]

    mixed_sums = jnp.concatenate(mixed_sums, axis=0)
    grad_bias = jnp.concatenate(bias_sums, axis=0).reshape(CHUNKS, 2, chips, per_chunk)
    local_squares = jnp.zeros((), F32)
    for piece in sum_in + [sum_out] + [part for pair in up_down for part in pair]:
        local_squares = local_squares + jnp.sum(piece * piece)
    table = jnp.concatenate(
        [
            first_sums[0:2],
            mixed_sums[:, 0].reshape(1, D),
            mixed_sums[:, 2].reshape(1, D),
            turn_sums[0:5],
            grad_bias.transpose(2, 1, 0, 3).reshape(4, D),
            jnp.broadcast_to(local_squares, (3, D)),
        ],
        axis=0,
    )
    table = moves.sum_all(table)
    grad_vectors = table[:13]
    total_squares = table[13, 0] + jnp.sum(grad_vectors * grad_vectors)
    grad_norm = jnp.sqrt(total_squares)
    factor = jnp.minimum(1.0, clip_share * math.sqrt(PARAMS) / (grad_norm + 1e-06))

    def owned(value):
        return lax.dynamic_slice_in_dim(value, core * rows_in, rows_in, axis=0)

    def others(value):
        return lax.dynamic_slice_in_dim(value, (1 - core) * rows_in, rows_in, axis=0)

    def ordered(mine, theirs):
        return jnp.where(core == 0, jnp.stack([mine, theirs]), jnp.stack([theirs, mine]))

    ups = jnp.concatenate([pair[0] for pair in up_down], axis=1)
    ups = ordered(owned(ups), moves.over_core(others(ups)))
    ups = ups.reshape(2, rows_in, CHUNKS, chips, per_chunk)
    summed_expand = ups.transpose(1, 3, 0, 2, 4).reshape(rows_in, HIDDEN)
    summed_contract = jnp.concatenate([pair[1] for pair in up_down], axis=0)
    ins = jnp.concatenate(sum_in + [sum_out], axis=1)
    ins = ordered(owned(ins), moves.over_core(others(ins)))
    sum_ins = ins[:, :, : GROUPS * step].reshape(2, rows_in, GROUPS, 3, PW)
    summed_in = sum_ins.transpose(1, 3, 2, 0, 4).reshape(rows_in, 3 * D)
    summed_out = ins[:, :, GROUPS * step :].transpose(1, 0, 2).reshape(rows_in, D)
    summed_vectors = lax.dynamic_slice_in_dim(grad_vectors, owner * columns, columns, axis=1)

    summed = (summed_in, summed_out, summed_expand, summed_contract, summed_vectors)
    masters = (project_in, project_out, expand, contract, vectors)
    firsts = (first_in, first_out, first_expand, first_contract, first_vectors)
    seconds = (second_in, second_out, second_expand, second_contract, second_vectors)
    rates = (matrix_rate, matrix_rate, matrix_rate, matrix_rate, vector_rate)
    decays = (matrix_decay, matrix_decay, matrix_decay, matrix_decay, 0.0)
    results = [
        adam_update(
            masters[index],
            summed[index] * factor,
            firsts[index],
            seconds[index],
            rates[index],
            decays[index],
        )
        for index in range(5)
    ]
    momenta = tuple(item[0] for item in results)
    variances = tuple(item[1] for item in results)
    updated = tuple(item[2] for item in results)
    copies = tuple(item.astype(BF) for item in updated)
    return (
        (activations, input_grad, grad_norm.reshape(1)) + momenta + variances + updated + copies
    )


def solution(mesh):
    split = P(AXES, None)
    columns = P(None, AXES)
    weights = (split, split, split, split, columns)
    return jax.shard_map(
        functools.partial(on_device, mesh.shape["dp"], mesh.shape["fsdp"]),
        mesh=mesh,
        in_specs=(split, split, split) + weights * 3,
        out_specs=(split, split, P()) + weights * 4,
        check_vma=False,
    )
```

```python
import functools
import math

import jax
import jax.numpy as jnp
from jax import lax
from jax.experimental import pallas as pl
from jax.experimental.pallas import tpu as pltpu
from jax.sharding import PartitionSpec as P

D = 768
HEADS = 12
HEAD_DIM = 64
KEEP_GLOBAL = 98
KEEP_LOCAL = 18
KEEP = 268
PARAMS = 7087872
STEP = 5

norm_eps = 1e-06
clip_share = 0.05
matrix_rate = 0.04
vector_rate = 0.3
matrix_decay = 0.05
first_beta = 0.5
second_beta = 0.5
adam_eps = 1e-08

AXES = ("dp", "fsdp")
BF = jnp.bfloat16
F32 = jnp.float32
NT = (((1,), (1,)), ((), ()))
TN = (((0,), (0,)), ((), ()))
PAD = -(-KEEP // 16) * 16
PAIRS = HEADS // 2
PW = 2 * HEAD_DIM
SETS = ((0,), (1, 2))
CHUNKS = 2
QUARTERS = 2 * CHUNKS
HIDDEN = 4 * D
VMEM_LIMIT = 60 * 2**20
NEG = -1e30
SEGMENTS = (
    (0, 112, 0, KEEP_GLOBAL),
    (96, 112, KEEP_GLOBAL, 2 * KEEP_GLOBAL),
    (192, 80, 2 * KEEP_GLOBAL, KEEP),
)


def nn(left, right):
    return jnp.dot(left, right, preferred_element_type=F32)


def nt(left, right):
    return lax.dot_general(left, right, NT, preferred_element_type=F32)


def tn(left, right):
    return lax.dot_general(left, right, TN, preferred_element_type=F32)


def params(**more):
    return pltpu.CompilerParams(vmem_limit_bytes=VMEM_LIMIT, **more)


def cost(flops, moved, exps=0):
    return pl.CostEstimate(flops=int(flops), bytes_accessed=int(moved), transcendentals=int(exps))


def whole(shape):
    return pl.BlockSpec(shape, lambda *_: (0,) * len(shape))


ANY = pl.BlockSpec(memory_space=pl.ANY)
SMEM = pl.BlockSpec(memory_space=pltpu.SMEM)


def normalize(values):
    centred = values - jnp.mean(values, axis=-1, keepdims=True)
    spread = jnp.mean(centred * centred, axis=-1, keepdims=True)
    inverse = lax.rsqrt(spread + norm_eps)
    return centred * inverse, inverse


def norm_back(grad, normed, inverse, gain):
    pulled = grad * gain
    return inverse * (
        pulled
        - jnp.mean(pulled, axis=-1, keepdims=True)
        - normed * jnp.mean(pulled * normed, axis=-1, keepdims=True)
    )


def column_sum(values):
    return jnp.sum(values, axis=0, keepdims=True)


def window_start(image, image_tokens, rows, window):
    return jnp.minimum((image_tokens * image) // 16, (rows - window) // 16) * 16


def pick_kernel(image_tokens, rows, window, slots, source, picked):
    image = pl.program_id(0)
    shift = image_tokens * image - window_start(image, image_tokens, rows, window)
    place = slots[0] + shift
    hot = (lax.broadcasted_iota(jnp.int32, (PAD, window), 1) == place).astype(F32).astype(BF)
    picked[...] = nn(hot, source[...]).astype(BF)


def pick(source, slots):
    rows = source.shape[0]
    count = slots.shape[0]
    image_tokens = rows // count
    window = -(-(image_tokens + 15) // 16) * 16
    start = functools.partial(
        window_start, image_tokens=image_tokens, rows=rows, window=window
    )
    return pl.pallas_call(
        functools.partial(pick_kernel, image_tokens, rows, window),
        grid=(count,),
        in_specs=[
            pl.BlockSpec((1, PAD, 1), lambda i: (i, 0, 0)),
            pl.BlockSpec((pl.Element(window), pl.Element(D)), lambda i: (start(i), 0)),
        ],
        out_specs=pl.BlockSpec((PAD, D), lambda i: (i, 0)),
        out_shape=jax.ShapeDtypeStruct((count * PAD, D), BF),
        compiler_params=params(),
        cost_estimate=cost(2 * count * PAD * window * D, 2 * rows * D + 2 * count * PAD * D),
        name="pick_rows",
    )(slots, source)


def local_mask():
    first, rows, low, high = SEGMENTS[2]
    slot = jnp.arange(rows) + first
    crop = jnp.where((slot >= low) & (slot < high), (slot - low) // KEEP_LOCAL, -1)
    same = (crop[:, None] == crop[None, :]) & (crop[:, None] >= 0)
    bias = jnp.where(same, 0.0, NEG).astype(F32)
    return jnp.concatenate([bias, bias], axis=1)


def lanes_of(rows):
    return lax.broadcasted_iota(jnp.int32, (rows, PW), 1) < HEAD_DIM


def split_heads(values):
    first = lanes_of(values.shape[0])
    zero = jnp.zeros_like(values)
    return jnp.concatenate(
        [jnp.where(first, values, zero), jnp.where(first, zero, values)], axis=0
    )


def join_heads(values):
    rows = values.shape[0] // 2
    return jnp.where(lanes_of(rows), values[:rows], values[rows:])


def rows_of(segment):
    return slice(segment[0], segment[0] + segment[1])


def attention(jobs, mask):
    chains = [(job, segment) for job in jobs for segment in SEGMENTS]
    scores = []
    for (query, key_rows, _), segment in chains:
        rows = rows_of(segment)
        scores.append(nt(split_heads(query[rows] * HEAD_DIM**-0.5), key_rows[rows]))
    mask = jnp.concatenate([mask[:, : mask.shape[0]]] * 2, axis=0)
    probs = []
    for (_, segment), score in zip(chains, scores):
        first, count, low, high = segment
        if low == 2 * KEEP_GLOBAL:
            score = score + mask
        else:
            slot = lax.broadcasted_iota(jnp.int32, (1, count), 1) + first
            score = jnp.where((slot >= low) & (slot < high), score, NEG)
        grown = jnp.exp(score - jnp.max(score, axis=-1, keepdims=True))
        probs.append((grown * (1.0 / jnp.sum(grown, axis=-1, keepdims=True))).astype(BF))
    parts = []
    for ((_, _, value), segment), prob in zip(chains, probs):
        parts.append(join_heads(nn(prob, value[rows_of(segment)])))
    slot = lax.broadcasted_iota(jnp.int32, (16, 1), 0)
    results = []
    for index in range(len(jobs)):
        one, two, three = parts[3 * index : 3 * index + 3]
        results.append(
            jnp.concatenate(
                [
                    one[:96],
                    jnp.where(slot + 96 < KEEP_GLOBAL, one[96:], two[:16]),
                    two[16:96],
                    jnp.where(slot + 192 < 2 * KEEP_GLOBAL, two[96:], three[:16]),
                    three[16:],
                ],
                axis=0,
            ).astype(BF)
        )
    return results


def attention_back(jobs, mask):
    chains = [(job, segment) for job in jobs for segment in SEGMENTS]
    halves, grads = [], []
    for (query, _, _, grad), segment in chains:
        first, count, low, high = segment
        rows = rows_of(segment)
        halves.append(split_heads(query[rows] * HEAD_DIM**-0.5))
        slot = lax.broadcasted_iota(jnp.int32, (count, 1), 0) + first
        kept = jnp.where((slot >= low) & (slot < high), grad[rows], jnp.zeros((), BF))
        grads.append(split_heads(kept))
    scores, grad_probs = [], []
    for ((_, key_rows, value, _), segment), half, grad in zip(chains, halves, grads):
        rows = rows_of(segment)
        scores.append(nt(key_rows[rows], half))
        grad_probs.append(nt(value[rows], grad))
    probs, grad_scores = [], []
    for (_, segment), score, pulled in zip(chains, scores, grad_probs):
        first, count, low, high = segment
        if low == 2 * KEEP_GLOBAL:
            score = score + mask
        else:
            slot = lax.broadcasted_iota(jnp.int32, (count, 1), 0) + first
            score = jnp.where((slot >= low) & (slot < high), score, NEG)
        grown = jnp.exp(score - jnp.max(score, axis=0, keepdims=True))
        prob = grown * (1.0 / jnp.sum(grown, axis=0, keepdims=True))
        weighted = jnp.sum(prob * pulled, axis=0, keepdims=True)
        probs.append(prob.astype(BF))
        grad_scores.append((prob * (pulled - weighted)).astype(BF))
    parts = [[], [], []]
    for prob, grad in zip(probs, grads):
        parts[2].append(nn(prob, grad))
    for score, half in zip(grad_scores, halves):
        parts[1].append(nn(score, half))
    for ((_, key_rows, _, _), segment), score in zip(chains, grad_scores):
        parts[0].append(join_heads(tn(score, key_rows[rows_of(segment)])) * HEAD_DIM**-0.5)
    results = []
    for index in range(len(jobs)):
        joined = []
        for part in parts:
            one, two, three = part[3 * index : 3 * index + 3]
            joined.append(
                jnp.concatenate(
                    [
                        one[:96],
                        one[96:] + two[:16],
                        two[16:96],
                        two[96:] + three[:16],
                        three[16:],
                    ],
                    axis=0,
                ).astype(BF)
            )
        results.append(joined)
    return results


def pairs_of(place, groups):
    core = place[2]
    return [2 * group + core for group in groups] + [2 * group + 1 - core for group in groups]


def lane_block(index):
    return pl.ds(pl.multiple_of(index * PW, PW), PW)


IMAGES = 2


def heads_kernel(groups, place, mask, vec, source, own_w, other_w, *refs):
    if groups[0] == 0:
        mixed, heads, normed, weight = refs
        unit, _ = normalize(source[...].astype(F32))
        rows = (unit * vec[0:1, :].astype(F32) + vec[1:2, :].astype(F32)).astype(BF)
        normed[...] = rows
    else:
        mixed, heads, weight = refs
        rows = source[...]
    width = 3 * PW
    half = len(groups) * width

    @pl.when(pl.program_id(0) == 0)
    def _():
        weight[:, :half] = own_w[:, :half]
        weight[:, half:] = other_w[:, :half]

    product = nn(rows, weight[...])
    jobs, lanes = [], []
    for index, pair in enumerate(pairs_of(place, groups)):
        at = index * width
        block = lane_block(pair)
        query = (product[:, at : at + PW] + vec[2:3, block].astype(F32)).astype(BF)
        key_rows = product[:, at + PW : at + 2 * PW].astype(BF)
        value = (product[:, at + 2 * PW : at + width] + vec[3:4, block].astype(F32)).astype(BF)
        mixed[:, at : at + PW] = query
        mixed[:, at + PW : at + 2 * PW] = key_rows
        mixed[:, at + 2 * PW : at + width] = value
        for image in range(IMAGES):
            span = slice(image * PAD, (image + 1) * PAD)
            jobs.append((query[span], key_rows[span], value[span]))
            lanes.append((span, lane_block(pair - 2 * groups[0])))
    for (span, block), result in zip(lanes, attention(jobs, mask[...])):
        heads[span, block] = result


def heads_forward(groups, place, mask, vec, source, own_w, other_w):
    rows = source.shape[0]
    size = IMAGES * PAD
    width = 6 * PW * len(groups)
    wide = pl.BlockSpec((size, D), lambda i: (i, 0))
    weight = whole(own_w.shape)
    outs = [
        (pl.BlockSpec((size, width), lambda i: (i, 0)), jax.ShapeDtypeStruct((rows, width), BF)),
        (
            pl.BlockSpec((size, width // 3), lambda i: (i, 0)),
            jax.ShapeDtypeStruct((rows, width // 3), BF),
        ),
    ]
    if groups[0] == 0:
        outs.append((wide, jax.ShapeDtypeStruct((rows, D), BF)))
    return pl.pallas_call(
        functools.partial(heads_kernel, groups),
        grid=(rows // size,),
        in_specs=[SMEM, whole(mask.shape), whole((16, D)), wide, weight, weight],
        out_specs=tuple(out[0] for out in outs),
        out_shape=tuple(out[1] for out in outs),
        scratch_shapes=[pltpu.VMEM((D, width), BF)],
        compiler_params=params(),
        cost_estimate=cost(2 * rows * D * width + rows * 1e5 * len(groups), 8 * rows * D),
        name=f"attention_{groups[0]}",
    )(place, mask, vec, source, own_w, other_w)


def heads_back_kernel(
    groups, steps, place, mask, grad_attended, normed, w_out, mixed, *refs
):
    (grad_mixed, gw_own, gw_other, sums, kept_normed, kept_mixed) = refs
    step = pl.program_id(0)
    size = IMAGES * PAD
    width = 3 * PW
    half = len(groups) * width

    @pl.when(step == 0)
    def _():
        sums[...] = jnp.zeros_like(sums)

    @pl.when(step < steps)
    def _():
        rows = pl.ds(pl.multiple_of(step * size, 16), size)
        kept_normed[rows, :] = normed[...]
        incoming = grad_attended[...]
        jobs, places = [], []
        for index, pair in enumerate(pairs_of(place, groups)):
            at = index * width
            grad_heads = nt(incoming, w_out[lane_block(pair), :]).astype(BF)
            for image in range(IMAGES):
                span = slice(image * PAD, (image + 1) * PAD)
                jobs.append(
                    (
                        mixed[span, at : at + PW],
                        mixed[span, at + PW : at + 2 * PW],
                        mixed[span, at + 2 * PW : at + width],
                        grad_heads[span],
                    )
                )
                places.append((image, at))
        for (image, at), parts in zip(places, attention_back(jobs, mask[...])):
            for index, low in enumerate(parts):
                columns = slice(at + index * PW, at + (index + 1) * PW)
                grad_mixed[image * PAD : (image + 1) * PAD, columns] = low
                here = pl.ds(pl.multiple_of(step * size + image * PAD, 16), PAD)
                kept_mixed[here, columns] = low
                if index != 1:
                    sums[0:1, columns] += column_sum(low.astype(F32))

    @pl.when(step == steps)
    def _():
        gw_other[...] = tn(kept_normed[...], kept_mixed[:, half:]).astype(BF)
        gw_own[...] = tn(kept_normed[...], kept_mixed[:, :half]).astype(BF)


def heads_backward(groups, place, mask, grad_attended, normed, w_out, mixed):
    rows, width = mixed.shape
    size = IMAGES * PAD
    steps = rows // size
    last = steps - 1
    wide = pl.BlockSpec((size, D), lambda i: (jnp.minimum(i, last), 0))
    block = pl.BlockSpec((size, width), lambda i: (jnp.minimum(i, last), 0))
    weight_shape = jax.ShapeDtypeStruct((D, width // 2), BF)
    return pl.pallas_call(
        functools.partial(heads_back_kernel, groups, steps),
        grid=(steps + 1,),
        in_specs=[SMEM, whole(mask.shape), wide, wide, whole((D, D)), block],
        out_specs=(block,) + (whole((D, width // 2)),) * 2 + (whole((8, width)),),
        out_shape=(
            jax.ShapeDtypeStruct((rows, width), BF),
            weight_shape,
            weight_shape,
            jax.ShapeDtypeStruct((8, width), F32),
        ),
        scratch_shapes=[pltpu.VMEM((rows, D), BF), pltpu.VMEM((rows, width), BF)],
        compiler_params=params(),
        cost_estimate=cost(
            2 * rows * D * (width // 3 + width) + rows * 3e5 * len(groups), 12 * rows * D
        ),
        name=f"attention_back_{groups[0]}",
    )(place, mask, grad_attended, normed, w_out, mixed)


TILE = 256


def gelu_and_slope(values):
    below = 0.5 + 0.5 * lax.erf(values * math.sqrt(0.5))
    bell = jnp.exp(-0.5 * values * values) * (1.0 / math.sqrt(2.0 * math.pi))
    return values * below, below + values * bell


def both_ways(chunk, bias, weights, left, right, rows, kept_active, kept_before, sums):
    tiles = D // TILE
    for half in range(2):
        up, down = weights[2 * half], weights[2 * half + 1]
        for tile in range(tiles):
            columns = slice(tile * TILE, (tile + 1) * TILE)
            kept = slice(half * D + tile * TILE, half * D + (tile + 1) * TILE)
            before = nn(left, up[:, columns]) + bias[2 * chunk + half, :, columns]
            active, slope = gelu_and_slope(before)
            kept_active[rows, kept] = active.astype(BF)
            low = (nt(right, down[columns, :]) * slope).astype(BF)
            kept_before[rows, kept] = low
            sums[half, :, columns] += column_sum(low.astype(F32))
    result = nn(kept_active[rows, :D], weights[1][...])
    result += nn(kept_active[rows, D:], weights[3][...])
    pulled = nt(kept_before[rows, :D], weights[0][...])
    pulled += nt(kept_before[rows, D:], weights[2][...])
    return result, pulled


def hidden_grads(tile, blocks, kept, gw):
    kept_normed, kept_grad, kept_active, kept_before = kept

    def ordered(value):
        if blocks:
            value = jnp.concatenate([value[at : at + size] for at, size in blocks], axis=0)
        return value.astype(BF)

    for half in range(2):
        columns = slice(half * D, (half + 1) * D)

        @pl.when(tile == 2 * half)
        def _():
            gw[...] = ordered(tn(kept_normed[...], kept_before[:, columns]))

        @pl.when(tile == 2 * half + 1)
        def _():
            gw[...] = ordered(tn(kept_active[:, columns], kept_grad[...]))


def routed_rows(picked, grads, vec):
    inputs = picked[...].astype(F32)
    grad_rows = grads[...].astype(F32)
    routed = jnp.sum(inputs * vec[8:9, :].astype(F32), axis=-1, keepdims=True)
    return inputs, grad_rows, routed, routed * grad_rows


def first_mlp_kernel(steps, size, blocks, place, bias, vec, own_w, other_w, picked, grads, *refs):
    heads = refs[: len(SETS)]
    refs = refs[len(SETS) :]
    weights = refs[:4]
    attended, normed, out, back, gw, sums, w_full = refs[4:11]
    kept = refs[11:]
    kept_normed, kept_grad, kept_active, kept_before = kept
    step = pl.program_id(0)
    core = place[2]
    half = D // 2

    @pl.when(step == 0)
    def _():
        sums[...] = jnp.zeros_like(sums)
        w_full[:, pl.ds(pl.multiple_of(core * half, 128), half)] = own_w[...]
        w_full[:, pl.ds(pl.multiple_of((1 - core) * half, 128), half)] = other_w[...]

    @pl.when(step < steps)
    def _():
        rows = pl.ds(pl.multiple_of(step * size, 16), size)
        inputs, _, _, grad_branch = routed_rows(picked, grads, vec)
        right = grad_branch.astype(BF)
        joined = jnp.concatenate([part[...] for part in heads], axis=1)
        mixed = nn(joined, w_full[...]) + vec[4:5, :].astype(F32)
        attended[...] = mixed
        unit, _ = normalize(inputs + mixed)
        left = (unit * vec[5:6, :].astype(F32) + vec[6:7, :].astype(F32)).astype(BF)
        normed[...] = left
        kept_normed[rows, :] = left
        kept_grad[rows, :] = right
        out[...], back[...] = both_ways(
            0, bias, weights, left, right, rows, kept_active, kept_before, sums
        )

    @pl.when(step >= steps)
    def _():
        hidden_grads(step - steps, blocks, kept, gw)


def second_mlp_kernel(
    steps, size, blocks, place, bias, vec, picked, grads, normed, attended, out, back, *refs
):
    heads = refs[: len(SETS)]
    refs = refs[len(SETS) :]
    weights = refs[:4]
    (grad_attended, carry, values, turn_sums, sums, gw, gwo_own, gwo_other) = refs[4:12]
    kept, (kept_heads, kept_attended) = refs[12:16], refs[16:]
    kept_normed, kept_grad, kept_active, kept_before = kept
    step = pl.program_id(0)
    core = place[2]
    half = D // 2
    tiles = 4

    @pl.when(step == 0)
    def _():
        sums[...] = jnp.zeros_like(sums)
        turn_sums[...] = jnp.zeros_like(turn_sums)

    @pl.when(step < steps)
    def _():
        rows = pl.ds(pl.multiple_of(step * size, 16), size)
        inputs, grad_rows, routed, grad_branch = routed_rows(picked, grads, vec)
        left = normed[...]
        right = grad_branch.astype(BF)
        kept_normed[rows, :] = left
        kept_grad[rows, :] = right
        result, pulled = both_ways(
            1, bias, weights, left, right, rows, kept_active, kept_before, sums
        )
        pulled += back[...]
        router = vec[8:9, :].astype(F32)
        mixed = attended[...]
        branch = mixed + (result + out[...]) + vec[7:8, :].astype(F32)
        values[...] = (inputs + routed * branch).astype(BF)
        grad_routed = jnp.sum(grad_rows * branch, axis=-1, keepdims=True)
        unit, inverse = normalize(inputs + mixed)
        residual = norm_back(pulled, unit, inverse, vec[5:6, :].astype(F32))
        low = (grad_branch + residual).astype(BF)
        grad_attended[...] = low
        kept_attended[rows, :] = low
        at = 0
        for part in heads:
            kept_heads[rows, at : at + part.shape[1]] = part[...]
            at += part.shape[1]
        carry[...] = residual + grad_routed * router
        turn_sums[0:1, :] += column_sum(low.astype(F32))
        turn_sums[1:2, :] += column_sum(pulled * unit)
        turn_sums[2:3, :] += column_sum(pulled)
        turn_sums[3:4, :] += column_sum(right.astype(F32))
        turn_sums[4:5, :] += column_sum(inputs * grad_routed)

    @pl.when((step >= steps) & (step < steps + tiles))
    def _():
        hidden_grads(step - steps, blocks, kept, gw)

    @pl.when(step == steps + tiles)
    def _():
        own = pl.ds(pl.multiple_of(core * half, 128), half)
        other = pl.ds(pl.multiple_of((1 - core) * half, 128), half)
        gwo_own[...] = tn(kept_heads[...], kept_attended[:, own]).astype(BF)
        gwo_other[...] = tn(kept_heads[...], kept_attended[:, other]).astype(BF)


def mlp_specs(chunk, rows):
    size = (2 - chunk) * PAD
    steps = rows // size
    last = steps - 1

    def wide(width=D):
        return pl.BlockSpec((size, width), lambda i: (jnp.minimum(i, last), 0))

    weights = [
        pl.BlockSpec((D, D), lambda i, at=at: (0, at), pipeline_mode=pl.Buffered(1))
        for at in (0, 2, 1, 3)
    ]

    def gw_block(i):
        tile = jnp.clip(i - steps, 0, 3)
        return (0, tile // 2 + 2 * (tile % 2))

    scratch = [
        pltpu.VMEM((rows, D), BF),
        pltpu.VMEM((rows, D), BF),
        pltpu.VMEM((rows, 2 * D), BF),
        pltpu.VMEM((rows, 2 * D), BF),
    ]
    return size, steps, 4, wide, weights, pl.BlockSpec((D, D), gw_block), scratch


def first_mlp(blocks, place, bias, vec, w_out, picked, grads, heads, weights):
    rows = picked.shape[0]
    size, steps, tiles, wide, weight_specs, gw, scratch = mlp_specs(0, rows)
    total = jax.ShapeDtypeStruct((rows, D), F32)
    return pl.pallas_call(
        functools.partial(first_mlp_kernel, steps, size, blocks),
        grid=(steps + tiles,),
        in_specs=[SMEM, whole(bias.shape), whole((16, D))]
        + [pl.BlockSpec((D, D // 2), lambda i: (0, w_out[0].shape[1] * 2 // D - 1))] * 2
        + [wide()] * 2
        + [wide(part.shape[1]) for part in heads]
        + weight_specs,
        out_specs=(wide(),) * 4 + (gw, whole((2, 1, D)), whole((D, D))),
        out_shape=(
            total,
            jax.ShapeDtypeStruct((rows, D), BF),
            total,
            total,
            jax.ShapeDtypeStruct((D, 4 * D), BF),
            jax.ShapeDtypeStruct((2, 1, D), F32),
            jax.ShapeDtypeStruct((D, D), BF),
        ),
        scratch_shapes=scratch,
        compiler_params=params(),
        cost_estimate=cost(26 * rows * D * D, 30 * rows * D, 4 * rows * D),
        name="feed_forward_0",
    )(place, bias, vec, *w_out, picked, grads, *heads, *[weights] * 4)


def second_mlp(blocks, place, bias, vec, picked, grads, normed, attended, out, back, heads, weights):
    rows = picked.shape[0]
    size, steps, tiles, wide, weight_specs, gw, scratch = mlp_specs(1, rows)
    low = jax.ShapeDtypeStruct((rows, D), BF)
    column_half = jax.ShapeDtypeStruct((D, D // 2), BF)
    return pl.pallas_call(
        functools.partial(second_mlp_kernel, steps, size, blocks),
        grid=(steps + tiles + 1,),
        in_specs=[SMEM, whole(bias.shape), whole((16, D))]
        + [wide()] * 6
        + [wide(part.shape[1]) for part in heads]
        + weight_specs,
        out_specs=(wide(), wide(), wide(), whole((8, D)), whole((2, 1, D)), gw)
        + (whole((D, D // 2)),) * 2,
        out_shape=(
            low,
            jax.ShapeDtypeStruct((rows, D), F32),
            low,
            jax.ShapeDtypeStruct((8, D), F32),
            jax.ShapeDtypeStruct((2, 1, D), F32),
            jax.ShapeDtypeStruct((D, 4 * D), BF),
            column_half,
            column_half,
        ),
        scratch_shapes=scratch + [pltpu.VMEM((rows, D), BF), pltpu.VMEM((rows, D), BF)],
        compiler_params=params(),
        cost_estimate=cost(26 * rows * D * D, 40 * rows * D, 4 * rows * D),
        name="feed_forward_1",
    )(place, bias, vec, picked, grads, normed, attended, out, back, *heads, *[weights] * 4)


def first_back_kernel(count, vec, picked, grads, carry, *refs):
    mixed = refs[:count]
    weights = refs[count : 3 * count]
    values, sums = refs[3 * count : 3 * count + 2]
    kept = refs[3 * count + 2 :]

    @pl.when(pl.program_id(0) == 0)
    def _():
        sums[...] = jnp.zeros_like(sums)
        for index in range(count):
            half = mixed[index].shape[1] // 2
            kept[index][:, :half] = weights[2 * index][:, :half]
            kept[index][:, half:] = weights[2 * index + 1][:, :half]

    pulled = nt(mixed[0][...], kept[0][...])
    for index in range(1, count):
        pulled += nt(mixed[index][...], kept[index][...])
    unit, inverse = normalize(picked[...].astype(F32))
    grad = norm_back(pulled, unit, inverse, vec[0:1, :].astype(F32))
    values[...] = (grads[...].astype(F32) + grad + carry[...]).astype(BF)
    sums[0:1, :] += column_sum(pulled * unit)
    sums[1:2, :] += column_sum(pulled)


def first_back(vec, picked, grads, carry, mixed, weights):
    rows = picked.shape[0]
    size = 2 * PAD
    wide = pl.BlockSpec((size, D), lambda i: (i, 0))
    flat = [weight for pair in weights for weight in pair]
    return pl.pallas_call(
        functools.partial(first_back_kernel, len(mixed)),
        grid=(rows // size,),
        in_specs=[whole((16, D)), wide, wide, wide]
        + [pl.BlockSpec((size, part.shape[1]), lambda i: (i, 0)) for part in mixed]
        + [whole(weight.shape) for weight in flat],
        out_specs=(wide, whole((8, D))),
        out_shape=(jax.ShapeDtypeStruct((rows, D), BF), jax.ShapeDtypeStruct((8, D), F32)),
        scratch_shapes=[pltpu.VMEM((D, part.shape[1]), BF) for part in mixed],
        compiler_params=params(),
        cost_estimate=cost(6 * rows * D * D, 16 * rows * D),
        name="first_norm_back",
    )(vec, picked, grads, carry, *mixed, *flat)


def put_kernel(span, places, *refs):
    kinds = len(refs) // 5
    sources, values, nexts, outs, joined = (refs[i * kinds : (i + 1) * kinds] for i in range(5))
    width = places.shape[2]
    same = lax.broadcasted_iota(jnp.int32, (span, width), 0) == places[0]
    hot = same.astype(F32)
    kept = jnp.max(hot, axis=-1, keepdims=True) > 0.5
    hot = hot.astype(BF)
    for source, value, after, out, both in zip(sources, values, nexts, outs, joined):
        both[:PAD, :] = value[...]
        both[PAD:, :] = after[...]
        out[...] = jnp.where(kept, nn(hot, both[...]).astype(BF), source[...])


def put(places, sources, values):
    rows = sources[0].shape[0]
    count = places.shape[0]
    span = -(-(rows // count) // 16) * 16
    block = pl.BlockSpec((span, D), lambda i: (i, 0))
    value = pl.BlockSpec((PAD, D), lambda i: (i, 0))
    after = pl.BlockSpec((16, D), lambda i: (jnp.minimum(i + 1, count - 1) * (PAD // 16), 0))
    kinds = len(sources)
    return pl.pallas_call(
        functools.partial(put_kernel, span),
        grid=(count,),
        in_specs=[pl.BlockSpec((1, 1, places.shape[2]), lambda i: (i, 0, 0))]
        + [block] * kinds
        + [value] * kinds
        + [after] * kinds,
        out_specs=(block,) * kinds,
        out_shape=(jax.ShapeDtypeStruct((rows, D), BF),) * kinds,
        scratch_shapes=[pltpu.VMEM((PAD + 16, D), BF)] * kinds,
        compiler_params=params(),
        cost_estimate=cost(2 * kinds * rows * D * (PAD + 16), kinds * 6 * rows * D),
        name="put_rows",
    )(places, *sources, *values, *values)


def put_places(keep_slots, image_tokens):
    count = keep_slots.shape[0]
    span = -(-image_tokens // 16) * 16
    image = jnp.arange(count, dtype=jnp.int32)[:, None]
    own = keep_slots + image * (image_tokens - span)
    following = jnp.concatenate([keep_slots[1:, :16], jnp.full((1, 16), -span, jnp.int32)], axis=0)
    following = following + (image + 1) * image_tokens - image * span
    following = jnp.where(image < count - 1, following, -1)
    gap = jnp.full((count, PAD - KEEP), -1, jnp.int32)
    return jnp.concatenate([own, gap, following], axis=1)[:, None, :]


class Moves:
    def __init__(self, n_dp, n_fsdp):
        self.n_dp = n_dp
        self.n_fsdp = n_fsdp
        self.squares = n_fsdp // 2
        outer = lax.axis_index("dp")
        inner = lax.axis_index("fsdp")
        self.z = outer
        self.yx = inner // 2
        self.core = inner % 2
        self.place = jnp.stack([self.z, self.yx, self.core]).astype(jnp.int32)

    def swap(self, value, mask):
        total = self.n_dp * self.n_fsdp
        return lax.ppermute(value, AXES, [(i, i ^ mask) for i in range(total)])

    def over_z(self, values):
        return [values[0]] + [self.swap(values[k], k * self.n_fsdp) for k in range(1, self.n_dp)]

    def over_yx(self, values):
        return [values[0]] + [self.swap(values[k], 2 * k) for k in range(1, self.squares)]

    def over_core(self, value):
        return self.swap(value, 1)

    def sum_all(self, value):
        value = add_parts(self.over_z([value] * self.n_dp))
        value = add_parts(self.over_yx([value] * self.squares))
        return value + self.over_core(value)

    def square_blocks(self, size):
        return [
            ((z * self.n_fsdp + inner) * size, size)
            for inner in range(self.n_fsdp)
            for z in range(self.n_dp)
        ]

    def over_square(self, value, ordered):
        rows, n = value.shape
        if not ordered:
            value = value.reshape(self.n_dp, self.n_fsdp, -1, n).transpose(1, 0, 2, 3)
        value = value.reshape(rows, n)
        summed = lax.psum_scatter(value, "fsdp", scatter_dimension=0, tiled=True)
        return summed.reshape(self.n_dp, -1, n)

    def by_chip(self, value):
        chips = self.n_dp * self.squares
        return value.reshape(self.n_dp, self.squares, value.shape[0] // chips, value.shape[1])

    def add_cores(self, place, keeps, arrived):
        keeps = [self.by_chip(value) for value in keeps]
        arrived = [self.by_chip(value) for value in arrived]
        return add_pairs(place, keeps, arrived, self.squares)


def add_parts(parts):
    total = parts[0].astype(F32)
    for part in parts[1:]:
        total = total + part.astype(F32)
    return total


def together(*values):
    return lax.optimization_barrier(values)


def after(value, *others):
    return lax.optimization_barrier((value, *others))[0]


def place_kernel(axis, count, cuts, place, *refs):
    outs = refs[count:]
    me = place[axis]
    for k in range(count):
        for (first, width), out in zip(cuts, outs):
            if axis == 0:
                out[me ^ k] = refs[k][:, first : first + width]
            else:
                out[:, me ^ k] = refs[k][...]


def place_blocks(place, axis, blocks, widths):
    count = len(blocks)
    cuts, at = [], 0
    for width in widths:
        cuts.append((at, width))
        at += width
    shape = blocks[0].shape[:-1]
    shape = shape[:axis] + (count,) + shape[axis:]
    vmem = pl.BlockSpec(memory_space=pltpu.VMEM)
    return pl.pallas_call(
        functools.partial(place_kernel, axis, count, cuts),
        in_specs=[SMEM] + [vmem] * count,
        out_specs=[vmem] * len(widths),
        out_shape=[jax.ShapeDtypeStruct(shape + (width,), BF) for width in widths],
        compiler_params=params(),
        cost_estimate=cost(0, 4 * math.prod(shape) * at),
        name="place_blocks",
    )(place, *blocks)


def add_pairs_kernel(parts, squares, place, *refs):
    outs = refs[2 * parts * squares :]
    at = 0
    for part in range(parts):
        for k in range(squares):
            index = part * squares + k
            left, right = refs[index], refs[parts * squares + index]
            width = left.shape[3]
            total = left[...].astype(F32) + right[...].astype(F32)
            outs[k][:, :, at : at + width] = total[:, 0].astype(BF)
        at += width


def add_pairs(place, keeps, arrived, squares):
    specs, left, right = [], [], []
    n_dp, _, m, _ = keeps[0].shape
    for keep, other in zip(keeps, arrived):
        for k in range(squares):
            specs.append(
                pl.BlockSpec(
                    (n_dp, 1, m, keep.shape[3]), lambda i, place, k=k: (0, place[1] ^ k, 0, 0)
                )
            )
            left.append(keep)
            right.append(other)
    shape = (n_dp, m, sum(keep.shape[3] for keep in keeps))
    return pl.pallas_call(
        functools.partial(add_pairs_kernel, len(keeps), squares),
        grid_spec=pltpu.PrefetchScalarGridSpec(
            num_scalar_prefetch=1,
            grid=(1,),
            in_specs=specs + specs,
            out_specs=[pl.BlockSpec(shape, lambda i, place: (0, 0, 0))] * squares,
        ),
        out_shape=[jax.ShapeDtypeStruct(shape, BF)] * squares,
        compiler_params=params(),
        cost_estimate=cost(0, 6 * squares * math.prod(shape)),
        name="add_cores",
    )(place, *left, *right)


def add_blocks_kernel(count, rows, sizes, place, *refs):
    outs = refs[count * sum(sizes) :]
    at = 0
    for index in range(count):
        lane = 0
        for terms in sizes:
            total = refs[at][0].astype(F32)
            for term in range(1, terms):
                total = total + refs[at + term][0].astype(F32)
            at += terms
            for first in range(0, total.shape[0], rows):
                width = total.shape[1]
                outs[index][:, lane : lane + width] = total[first : first + rows].astype(BF)
                lane += width


def add_blocks(place, groups, n_dp, rows):
    specs, operands, lanes = [], [], 0
    for arrays in groups:
        _, m, n = arrays[0].shape
        lanes += n * (m // rows)
    for k in range(n_dp):
        for arrays in groups:
            _, m, n = arrays[0].shape
            spec = pl.BlockSpec((1, m, n), lambda i, place, k=k: (place[0] ^ k, 0, 0))
            specs += [spec] * len(arrays)
            operands += arrays
    sizes = [len(arrays) for arrays in groups]
    return pl.pallas_call(
        functools.partial(add_blocks_kernel, n_dp, rows, sizes),
        grid_spec=pltpu.PrefetchScalarGridSpec(
            num_scalar_prefetch=1,
            grid=(1,),
            in_specs=specs,
            out_specs=[pl.BlockSpec((rows, lanes), lambda i, place: (0, 0))] * n_dp,
        ),
        out_shape=[jax.ShapeDtypeStruct((rows, lanes), BF)] * n_dp,
        compiler_params=params(),
        cost_estimate=cost(0, 4 * n_dp * rows * lanes * max(sizes)),
        name="add_squares",
    )(place, *operands)


def adam_kernel(table, *refs):
    kinds = 5
    masters, firsts, seconds, grads = (refs[i * kinds : (i + 1) * kinds] for i in range(4))
    outs = refs[4 * kinds :]
    vector_rows = masters[4].shape[0]
    vectors = table[:vector_rows, :]
    squares = jnp.sum(vectors * vectors, keepdims=True) + table[vector_rows : vector_rows + 1, :1]
    grad_norm = jnp.sqrt(squares)
    factor = jnp.minimum(1.0, clip_share * math.sqrt(PARAMS) / (grad_norm + 1e-06))
    outs[0][...] = grad_norm
    for kind in range(kinds):
        rate = vector_rate if kind == 4 else matrix_rate
        decay = 0.0 if kind == 4 else matrix_decay
        master = masters[kind][...]
        grad = grads[kind][...] * factor
        first_new = first_beta * firsts[kind][...] + (1.0 - first_beta) * grad
        second_new = second_beta * seconds[kind][...] + (1.0 - second_beta) * grad * grad
        first_hat = first_new * (1.0 / (1.0 - first_beta**STEP))
        second_hat = second_new * (1.0 / (1.0 - second_beta**STEP))
        step = first_hat / (jnp.sqrt(second_hat) + adam_eps)
        updated = master - rate * (step + decay * master)
        outs[1 + kind][...] = first_new
        outs[1 + kinds + kind][...] = second_new
        outs[1 + 2 * kinds + kind][...] = updated
        outs[1 + 3 * kinds + kind][...] = updated.astype(BF)


def adam(table, masters, firsts, seconds, grads):
    vmem = pl.BlockSpec(memory_space=pltpu.VMEM)
    shapes = [master.shape for master in masters]
    states = [jax.ShapeDtypeStruct(shape, F32) for shape in shapes]
    outs = [jax.ShapeDtypeStruct((1, 1), F32)] + states * 3
    outs += [jax.ShapeDtypeStruct(shape, BF) for shape in shapes]
    elements = sum(math.prod(shape) for shape in shapes)
    return pl.pallas_call(
        adam_kernel,
        in_specs=[vmem] * 21,
        out_specs=[vmem] * len(outs),
        out_shape=outs,
        compiler_params=params(),
        cost_estimate=cost(20 * elements, 30 * elements),
        name="adam",
    )(table, *masters, *firsts, *seconds, *grads)


def on_device(
    n_dp,
    n_fsdp,
    tokens,
    keep_slots,
    cotangent,
    project_in,
    project_out,
    expand,
    contract,
    vectors,
    first_in,
    first_out,
    first_expand,
    first_contract,
    first_vectors,
    second_in,
    second_out,
    second_expand,
    second_contract,
    second_vectors,
):
    moves = Moves(n_dp, n_fsdp)
    place, core = moves.place, moves.core
    total = n_dp * n_fsdp
    rows_in = project_in.shape[0]
    part = contract.shape[0] // QUARTERS
    owner = moves.z * n_fsdp + lax.axis_index("fsdp")
    columns = vectors.shape[1]

    low_up = expand.astype(BF).reshape(rows_in, total, QUARTERS, part)
    low_up = low_up.transpose(0, 2, 1, 3).reshape(rows_in, HIDDEN)
    low_down = contract.astype(BF).reshape(QUARTERS, part, D)
    shards = [
        jnp.concatenate(
            [low_up[:, 2 * chunk * D : 2 * (chunk + 1) * D], low_down[2 * chunk], low_down[2 * chunk + 1]],
            axis=1,
        )
        for chunk in range(CHUNKS)
    ]
    w_hidden = [lax.all_gather(shards[0], AXES, axis=0, tiled=True)]

    def pair_columns(value, pair):
        return [value[:, at * D + pair * PW : at * D + (pair + 1) * PW] for at in range(3)]

    low_in = project_in.astype(BF)
    low_out = project_out.astype(BF)
    low_vec = jnp.pad(vectors.astype(BF).T, ((0, 0), (0, 128 - vectors.shape[0])))
    halves = []
    for parity in range(2):
        parts = []
        for index, groups in enumerate(SETS):
            for group in groups:
                parts += pair_columns(low_in, 2 * group + parity)
            if index == 0:
                parts.append(low_vec)
        parts.append(low_out[:, parity * (D // 2) : (parity + 1) * (D // 2)])
        halves.append(jnp.concatenate(parts, axis=1))
    mine = jnp.where(core == 0, halves[0], halves[1])
    theirs = jnp.where(core == 0, halves[1], halves[0])
    arrived = moves.over_core(theirs)
    rows = jnp.where(
        core == 0,
        jnp.concatenate([mine, arrived], axis=0),
        jnp.concatenate([arrived, mine], axis=0),
    )
    step = 3 * PW
    cut = len(SETS[0]) * step + 128
    widths = (cut, rows.shape[1] - cut)

    count = keep_slots.shape[0]
    image_tokens = tokens.shape[0] // count
    slots = jnp.pad(keep_slots, ((0, 0), (0, PAD - KEEP)), constant_values=-4 * image_tokens)
    slots = slots[:, :, None]
    parts = moves.over_z([rows] * n_dp)
    picked = pick(tokens, slots)
    picked, *parts = together(picked, *parts)
    first_stack, second_stack = place_blocks(place, 0, parts, widths)
    w_hidden.append(lax.all_gather(after(shards[1], first_stack), AXES, axis=0, tiled=True))
    parts = moves.over_yx([first_stack] * moves.squares)
    grad_rows = pick(cotangent, after(slots, first_stack))
    grad_rows, *parts = together(grad_rows, *parts)
    (first_own,) = place_blocks(place, 1, parts, widths[:1])
    first_own = first_own.reshape(D, widths[0])
    first_other = moves.over_core(first_own)
    vec = first_own[:, cut - 128 : cut - 112].T

    mask = local_mask()
    first_own, first_other, second_stack = together(first_own, first_other, second_stack)
    parts = moves.over_yx([second_stack] * moves.squares)
    mixed_0, heads_0, normed_one = heads_forward(
        SETS[0], place, mask, vec, picked, first_own, first_other
    )
    mixed_0, heads_0, normed_one, *parts = together(mixed_0, heads_0, normed_one, *parts)
    (second_own,) = place_blocks(place, 1, parts, widths[1:])
    second_own = second_own.reshape(D, widths[1])
    second_other = moves.over_core(second_own)
    w_in = [(first_own, first_other), (second_own, second_other)]
    w_out = w_in[1]
    mixed_1, heads_1 = heads_forward(SETS[1], place, mask, vec, normed_one, *w_in[1])
    heads = [heads_0, heads_1]

    bias = vec[9:13].astype(F32).reshape(total, QUARTERS, part)
    bias = bias.transpose(1, 0, 2).reshape(QUARTERS, 1, D)
    blocks = moves.square_blocks(rows_in) if rows_in % 8 == 0 else []
    attended, normed_two, out, back, gw_0, sums_0, w_out_full = first_mlp(
        blocks, place, bias, vec, w_out, picked, grad_rows, heads, w_hidden[0]
    )
    hidden_0 = moves.over_square(gw_0, blocks)
    (
        grad_attended,
        carry,
        put_values,
        turn_sums,
        sums_1,
        gw_1,
        gwo_own,
        gwo_other,
    ) = second_mlp(
        blocks,
        place,
        bias,
        vec,
        picked,
        grad_rows,
        normed_two,
        attended,
        out,
        back,
        heads,
        w_hidden[1],
    )
    hidden_1 = moves.over_square(gw_1, blocks)
    places = put_places(keep_slots, image_tokens)

    blocks = add_blocks(after(place, grad_attended), [[hidden_0]], n_dp, rows_in)
    parts = moves.over_z(blocks)
    arrived = moves.over_core(gwo_other)
    results = heads_backward(
        SETS[1],
        after(place, *blocks),
        mask,
        grad_attended,
        normed_one,
        w_out_full,
        mixed_1,
    )
    gm_1, gw_own, gw_other, sums_b, arrived, *hidden_0 = together(*results, arrived, *parts)
    blocks = moves.add_cores(
        place, [gwo_own, gw_own], [arrived, moves.over_core(gw_other)]
    )
    parts = moves.over_yx(blocks)
    results = heads_backward(
        SETS[0], after(place, *blocks), mask, grad_attended, normed_one, w_out_full, mixed_0
    )
    gm_0, gw_own, gw_other, sums_a, *parts = together(*results, *parts)
    blocks = add_blocks(place, [parts, [hidden_1]], n_dp, rows_in)
    parts = moves.over_z(blocks)
    arrived = moves.over_core(gw_other)
    results = first_back(
        after(vec, *blocks), picked, grad_rows, carry, [gm_0, gm_1], w_in
    )
    grad_values, first_sums, arrived, *later = together(*results, arrived, *parts)
    blocks = moves.add_cores(place, [gw_own], [arrived])
    parts = moves.over_yx(blocks)
    input_grad = put(after(places, *blocks), (cotangent,), (grad_values,))[0]
    input_grad, *parts = together(input_grad, *parts)
    blocks = add_blocks(place, [parts], n_dp, rows_in)
    parts = moves.over_z(blocks)
    activations = put(after(places, *blocks), (tokens,), (put_values,))[0]
    activations, *last = together(activations, *parts)
    hidden_0, later, last = add_parts(hidden_0), add_parts(later), add_parts(last)
    split = later.shape[1] - hidden_0.shape[1]
    later, hidden_1 = later[:, :split], later[:, split:]

    def in_pairs(sums, groups):
        own, other = sums[0].reshape(2, len(groups), 3, PW)
        pairs = jnp.stack([jnp.where(core == 0, own, other), jnp.where(core == 0, other, own)])
        return pairs.transpose(2, 1, 0, 3).reshape(3, 2 * len(groups) * PW)

    mixed_sums = jnp.concatenate([in_pairs(sums_a, SETS[0]), in_pairs(sums_b, SETS[1])], axis=1)
    grad_bias = jnp.concatenate([sums_0, sums_1], axis=0).reshape(QUARTERS, total, part)
    local_squares = jnp.zeros((), F32)
    for piece in (hidden_0, hidden_1, later, last):
        local_squares = local_squares + jnp.sum(piece * piece)
    table = jnp.concatenate(
        [
            first_sums[0:2],
            mixed_sums[0:1],
            mixed_sums[2:3],
            turn_sums[0:5],
            grad_bias.transpose(1, 0, 2).reshape(4, D),
            jnp.broadcast_to(local_squares, (3, D)),
        ],
        axis=0,
    )
    table = moves.sum_all(table)
    grad_vectors = table[:13]

    def complete(value):
        one, two = jnp.split(value, 2, axis=1)
        theirs = moves.over_core(jnp.where(core == 0, two, one))
        mine = jnp.where(core == 0, one, two)
        return jnp.where(core == 0, jnp.stack([mine, theirs]), jnp.stack([theirs, mine]))

    later, last = complete(later), complete(last)
    ups = jnp.concatenate([hidden_0[:, : 2 * D], hidden_1[:, : 2 * D]], axis=1)
    summed_expand = ups.reshape(rows_in, QUARTERS, total, part).transpose(0, 2, 1, 3)
    summed_expand = summed_expand.reshape(rows_in, HIDDEN)
    downs = [value[:, at * D : (at + 1) * D] for value in (hidden_0, hidden_1) for at in (2, 3)]
    summed_contract = jnp.concatenate(downs, axis=0)
    summed_out = jnp.concatenate([later[0, :, : D // 2], later[1, :, : D // 2]], axis=1)

    def in_columns(value, groups):
        value = value.reshape(2, rows_in, len(groups), 3, PW).transpose(1, 3, 2, 0, 4)
        return value.reshape(rows_in, 3, 2 * len(groups) * PW)

    summed_in = jnp.concatenate(
        [in_columns(last, SETS[0]), in_columns(later[:, :, D // 2 :], SETS[1])], axis=2
    ).reshape(rows_in, 3 * D)
    summed_vectors = lax.dynamic_slice_in_dim(grad_vectors, owner * columns, columns, axis=1)

    summed = (summed_in, summed_out, summed_expand, summed_contract, summed_vectors)
    masters = (project_in, project_out, expand, contract, vectors)
    firsts = (first_in, first_out, first_expand, first_contract, first_vectors)
    seconds = (second_in, second_out, second_expand, second_contract, second_vectors)
    grad_norm, *updates = adam(table, masters, firsts, seconds, summed)
    return (activations, input_grad, grad_norm.reshape(1), *updates)


def solution(mesh):
    split = P(AXES, None)
    columns = P(None, AXES)
    weights = (split, split, split, split, columns)
    return jax.shard_map(
        functools.partial(on_device, mesh.shape["dp"], mesh.shape["fsdp"]),
        mesh=mesh,
        in_specs=(split, split, split) + weights * 3,
        out_specs=(split, split, P()) + weights * 4,
        check_vma=False,
    )
```

```python
import functools
import math

import jax
import jax.numpy as jnp
from jax import lax
from jax.experimental import pallas as pl
from jax.experimental.pallas import tpu as pltpu
from jax.sharding import PartitionSpec as P

D = 768
HEADS = 12
HEAD_DIM = 64
KEEP_GLOBAL = 98
KEEP_LOCAL = 18
KEEP = 268
PARAMS = 7087872
STEP = 5

norm_eps = 1e-06
clip_share = 0.05
matrix_rate = 0.04
vector_rate = 0.3
matrix_decay = 0.05
first_beta = 0.5
second_beta = 0.5
adam_eps = 1e-08

AXES = ("dp", "fsdp")
BF = jnp.bfloat16
F32 = jnp.float32
NT = (((1,), (1,)), ((), ()))
TN = (((0,), (0,)), ((), ()))
PAD = -(-KEEP // 16) * 16
PAIRS = HEADS // 2
PW = 2 * HEAD_DIM
SETS = ((0,), (1, 2))
CHUNKS = 2
QUARTERS = 2 * CHUNKS
HIDDEN = 4 * D
IMAGES = 2
NEG = -1e30
SEGMENTS = (
    (0, 112, 0, KEEP_GLOBAL),
    (96, 112, KEEP_GLOBAL, 2 * KEEP_GLOBAL),
    (192, 80, 2 * KEEP_GLOBAL, KEEP),
)


def nn(left, right):
    return jnp.dot(left, right, preferred_element_type=F32)


def nt(left, right):
    return lax.dot_general(left, right, NT, preferred_element_type=F32)


def tn(left, right):
    return lax.dot_general(left, right, TN, preferred_element_type=F32)


def params(limit=60):
    return pltpu.CompilerParams(vmem_limit_bytes=limit * 2**20)


def cost(flops, moved, exps=0):
    return pl.CostEstimate(flops=int(flops), bytes_accessed=int(moved), transcendentals=int(exps))


def whole(shape):
    return pl.BlockSpec(shape, lambda *_: (0,) * len(shape))


ANY = pl.BlockSpec(memory_space=pl.ANY)
SMEM = pl.BlockSpec(memory_space=pltpu.SMEM)


def normalize(values):
    centred = values - jnp.mean(values, axis=-1, keepdims=True)
    spread = jnp.mean(centred * centred, axis=-1, keepdims=True)
    inverse = lax.rsqrt(spread + norm_eps)
    return centred * inverse, inverse


def norm_back(grad, normed, inverse, gain):
    pulled = grad * gain
    return inverse * (
        pulled
        - jnp.mean(pulled, axis=-1, keepdims=True)
        - normed * jnp.mean(pulled * normed, axis=-1, keepdims=True)
    )


def column_sum(values):
    return jnp.sum(values, axis=0, keepdims=True)


def window_start(step, image_tokens, rows, window):
    return jnp.minimum((IMAGES * image_tokens * step) // 16, (rows - window) // 16) * 16


def pick_kernel(image_tokens, rows, window, part, place, slots, source, picked):
    step = pl.program_id(0)
    shift = IMAGES * image_tokens * step - window_start(step, image_tokens, rows, window)
    for image in range(IMAGES):
        first = (image * image_tokens) // 16 * 16
        span = min(part, window - first)
        target = slots[image] + shift + image * image_tokens - first
        hot = lax.broadcasted_iota(jnp.int32, (PAD, span), 1) == target
        values = nn(hot.astype(F32).astype(BF), source[first : first + span, :])
        picked[image * PAD : (image + 1) * PAD, :] = values.astype(BF)


def pick(place, source, slots):
    rows = source.shape[0]
    count = slots.shape[0]
    image_tokens = rows // count
    window = -(-(IMAGES * image_tokens + 15) // 16) * 16
    part = -(-(image_tokens + 32) // 16) * 16
    start = functools.partial(
        window_start, image_tokens=image_tokens, rows=rows, window=window
    )
    return pl.pallas_call(
        functools.partial(pick_kernel, image_tokens, rows, window, part),
        grid=(count // IMAGES,),
        in_specs=[
            SMEM,
            pl.BlockSpec((IMAGES, PAD, 1), lambda i: (i, 0, 0)),
            pl.BlockSpec((pl.Element(window), pl.Element(D)), lambda i: (start(i), 0)),
        ],
        out_specs=pl.BlockSpec((IMAGES * PAD, D), lambda i: (i, 0)),
        out_shape=jax.ShapeDtypeStruct((count * PAD, D), BF),
        compiler_params=params(20),
        cost_estimate=cost(2 * count * PAD * window * D, 2 * rows * D + 2 * count * PAD * D),
        name="pick_rows",
    )(place, slots, source)


def local_mask():
    first, rows, low, high = SEGMENTS[2]
    slot = jnp.arange(rows) + first
    crop = jnp.where((slot >= low) & (slot < high), (slot - low) // KEEP_LOCAL, -1)
    same = (crop[:, None] == crop[None, :]) & (crop[:, None] >= 0)
    bias = jnp.where(same, 0.0, NEG).astype(F32)
    return jnp.concatenate([bias, bias], axis=1)


def lanes_of(rows):
    return lax.broadcasted_iota(jnp.int32, (rows, PW), 1) < HEAD_DIM


def split_heads(values):
    first = lanes_of(values.shape[0])
    zero = jnp.zeros_like(values)
    return jnp.concatenate(
        [jnp.where(first, values, zero), jnp.where(first, zero, values)], axis=0
    )


def join_heads(values):
    rows = values.shape[0] // 2
    return jnp.where(lanes_of(rows), values[:rows], values[rows:])


def rows_of(segment):
    return slice(segment[0], segment[0] + segment[1])


def attention(jobs, mask):
    chains = [(job, segment) for job in jobs for segment in SEGMENTS]
    scores = []
    for (query, key_rows, _), segment in chains:
        rows = rows_of(segment)
        scores.append(nt(split_heads(query[rows] * HEAD_DIM**-0.5), key_rows[rows]))
    mask = jnp.concatenate([mask[:, : mask.shape[0]]] * 2, axis=0)
    probs = []
    for (_, segment), score in zip(chains, scores):
        first, count, low, high = segment
        if low == 2 * KEEP_GLOBAL:
            score = score + mask
        else:
            slot = lax.broadcasted_iota(jnp.int32, (1, count), 1) + first
            score = jnp.where((slot >= low) & (slot < high), score, NEG)
        grown = jnp.exp(score - jnp.max(score, axis=-1, keepdims=True))
        probs.append((grown * (1.0 / jnp.sum(grown, axis=-1, keepdims=True))).astype(BF))
    parts = []
    for ((_, _, value), segment), prob in zip(chains, probs):
        parts.append(join_heads(nn(prob, value[rows_of(segment)])))
    slot = lax.broadcasted_iota(jnp.int32, (16, 1), 0)
    results = []
    for index in range(len(jobs)):
        one, two, three = parts[3 * index : 3 * index + 3]
        results.append(
            jnp.concatenate(
                [
                    one[:96],
                    jnp.where(slot + 96 < KEEP_GLOBAL, one[96:], two[:16]),
                    two[16:96],
                    jnp.where(slot + 192 < 2 * KEEP_GLOBAL, two[96:], three[:16]),
                    three[16:],
                ],
                axis=0,
            ).astype(BF)
        )
    return results


def attention_back(jobs, mask):
    chains = [(job, segment) for job in jobs for segment in SEGMENTS]
    halves, grads = [], []
    for (query, _, _, grad), segment in chains:
        first, count, low, high = segment
        rows = rows_of(segment)
        halves.append(split_heads(query[rows] * HEAD_DIM**-0.5))
        slot = lax.broadcasted_iota(jnp.int32, (count, 1), 0) + first
        kept = jnp.where((slot >= low) & (slot < high), grad[rows], jnp.zeros((), BF))
        grads.append(split_heads(kept))
    scores, grad_probs = [], []
    for ((_, key_rows, value, _), segment), half, grad in zip(chains, halves, grads):
        rows = rows_of(segment)
        scores.append(nt(key_rows[rows], half))
        grad_probs.append(nt(value[rows], grad))
    probs, grad_scores = [], []
    for (_, segment), score, pulled in zip(chains, scores, grad_probs):
        first, count, low, high = segment
        if low == 2 * KEEP_GLOBAL:
            score = score + mask
        else:
            slot = lax.broadcasted_iota(jnp.int32, (count, 1), 0) + first
            score = jnp.where((slot >= low) & (slot < high), score, NEG)
        grown = jnp.exp(score - jnp.max(score, axis=0, keepdims=True))
        prob = grown * (1.0 / jnp.sum(grown, axis=0, keepdims=True))
        weighted = jnp.sum(prob * pulled, axis=0, keepdims=True)
        probs.append(prob.astype(BF))
        grad_scores.append((prob * (pulled - weighted)).astype(BF))
    parts = [[], [], []]
    for prob, grad in zip(probs, grads):
        parts[2].append(nn(prob, grad))
    for score, half in zip(grad_scores, halves):
        parts[1].append(nn(score, half))
    for ((_, key_rows, _, _), segment), score in zip(chains, grad_scores):
        parts[0].append(join_heads(tn(score, key_rows[rows_of(segment)])) * HEAD_DIM**-0.5)
    results = []
    for index in range(len(jobs)):
        joined = []
        for part in parts:
            one, two, three = part[3 * index : 3 * index + 3]
            joined.append(
                jnp.concatenate(
                    [
                        one[:96],
                        one[96:] + two[:16],
                        two[16:96],
                        two[96:] + three[:16],
                        three[16:],
                    ],
                    axis=0,
                ).astype(BF)
            )
        results.append(joined)
    return results


def pairs_of(place, groups):
    core = place[2]
    return [2 * group + core for group in groups] + [2 * group + 1 - core for group in groups]


def lane_block(index):
    return pl.ds(pl.multiple_of(index * PW, PW), PW)


def heads_kernel(groups, place, mask, vec, source, own_w, other_w, *refs):
    if groups[0] == 0:
        mixed, heads, normed, weight = refs
        unit, _ = normalize(source[...].astype(F32))
        rows = (unit * vec[0:1, :].astype(F32) + vec[1:2, :].astype(F32)).astype(BF)
        normed[...] = rows
    else:
        mixed, heads, weight = refs
        rows = source[...]
    width = 3 * PW
    half = len(groups) * width

    @pl.when(pl.program_id(0) == 0)
    def _():
        weight[:, :half] = own_w[:, :half]
        weight[:, half:] = other_w[:, :half]

    product = nn(rows, weight[...])
    jobs, lanes = [], []
    for index, pair in enumerate(pairs_of(place, groups)):
        at = index * width
        block = lane_block(pair)
        query = (product[:, at : at + PW] + vec[2:3, block].astype(F32)).astype(BF)
        key_rows = product[:, at + PW : at + 2 * PW].astype(BF)
        value = (product[:, at + 2 * PW : at + width] + vec[3:4, block].astype(F32)).astype(BF)
        mixed[:, at : at + PW] = query
        mixed[:, at + PW : at + 2 * PW] = key_rows
        mixed[:, at + 2 * PW : at + width] = value
        for image in range(IMAGES):
            span = slice(image * PAD, (image + 1) * PAD)
            jobs.append((query[span], key_rows[span], value[span]))
            lanes.append((span, lane_block(pair - 2 * groups[0])))
    for (span, block), result in zip(lanes, attention(jobs, mask[...])):
        heads[span, block] = result


def heads_forward(groups, place, mask, vec, source, own_w, other_w):
    rows = source.shape[0]
    size = IMAGES * PAD
    width = 6 * PW * len(groups)
    wide = pl.BlockSpec((size, D), lambda i: (i, 0))
    weight = whole(own_w.shape)
    outs = [
        (pl.BlockSpec((size, width), lambda i: (i, 0)), jax.ShapeDtypeStruct((rows, width), BF)),
        (
            pl.BlockSpec((size, width // 3), lambda i: (i, 0)),
            jax.ShapeDtypeStruct((rows, width // 3), BF),
        ),
    ]
    if groups[0] == 0:
        outs.append((wide, jax.ShapeDtypeStruct((rows, D), BF)))
    return pl.pallas_call(
        functools.partial(heads_kernel, groups),
        grid=(rows // size,),
        in_specs=[SMEM, whole(mask.shape), whole((16, D)), wide, weight, weight],
        out_specs=tuple(out[0] for out in outs),
        out_shape=tuple(out[1] for out in outs),
        scratch_shapes=[pltpu.VMEM((D, width), BF)],
        compiler_params=params(32),
        cost_estimate=cost(2 * rows * D * width + rows * 1e5 * len(groups), 8 * rows * D),
        name=f"attention_{groups[0]}",
    )(place, mask, vec, source, own_w, other_w)


def heads_back_kernel(groups, steps, place, mask, grad_attended, normed, w_out, mixed, *refs):
    heads = refs[:-6] if len(refs) == 6 else refs[: -8]
    (grad_mixed, gw_own, gw_other, sums, kept_normed, kept_mixed) = refs[len(heads) :][:6]
    kept_heads, kept_grad = refs[len(heads) + 6 :] if heads else (None, None)
    step = pl.program_id(0)
    size = IMAGES * PAD
    width = 3 * PW
    half = len(groups) * width

    @pl.when(step == 0)
    def _():
        sums[...] = jnp.zeros_like(sums)

    @pl.when(step < steps)
    def _():
        rows = pl.ds(pl.multiple_of(step * size, 16), size)
        kept_normed[rows, :] = normed[...]
        incoming = grad_attended[...]
        if heads:
            kept_grad[rows, :] = incoming
            at = 0
            for part in heads:
                kept_heads[rows, at : at + part.shape[1]] = part[...]
                at += part.shape[1]
        jobs, places = [], []
        for index, pair in enumerate(pairs_of(place, groups)):
            at = index * width
            grad_heads = nt(incoming, w_out[lane_block(pair), :]).astype(BF)
            for image in range(IMAGES):
                span = slice(image * PAD, (image + 1) * PAD)
                jobs.append(
                    (
                        mixed[span, at : at + PW],
                        mixed[span, at + PW : at + 2 * PW],
                        mixed[span, at + 2 * PW : at + width],
                        grad_heads[span],
                    )
                )
                places.append((image, at))
        for (image, at), parts in zip(places, attention_back(jobs, mask[...])):
            for index, low in enumerate(parts):
                columns = slice(at + index * PW, at + (index + 1) * PW)
                grad_mixed[image * PAD : (image + 1) * PAD, columns] = low
                here = pl.ds(pl.multiple_of(step * size + image * PAD, 16), PAD)
                kept_mixed[here, columns] = low
                if index != 1:
                    sums[0:1, columns] += column_sum(low.astype(F32))

    @pl.when(step == steps)
    def _():
        first = 0
        if heads:
            first = D // 2
            core = place[2]
            own = pl.ds(pl.multiple_of(core * first, 128), first)
            other = pl.ds(pl.multiple_of((1 - core) * first, 128), first)
            gw_own[:, :first] = tn(kept_heads[...], kept_grad[:, own]).astype(BF)
            gw_other[:, :first] = tn(kept_heads[...], kept_grad[:, other]).astype(BF)
        gw_other[:, first:] = tn(kept_normed[...], kept_mixed[:, half:]).astype(BF)
        gw_own[:, first:] = tn(kept_normed[...], kept_mixed[:, :half]).astype(BF)


def heads_backward(groups, place, mask, grad_attended, normed, w_out, mixed, heads=()):
    rows, width = mixed.shape
    size = IMAGES * PAD
    steps = rows // size
    last = steps - 1

    def block(width):
        return pl.BlockSpec((size, width), lambda i: (jnp.minimum(i, last), 0))

    weight = (D, width // 2 + (D // 2 if heads else 0))
    kept = [D, width] + [D, D] * bool(heads)
    return pl.pallas_call(
        functools.partial(heads_back_kernel, groups, steps),
        grid=(steps + 1,),
        in_specs=[SMEM, whole(mask.shape), block(D), block(D)]
        + [pl.BlockSpec((D, D), lambda i: (0, w_out.shape[1] // D - 1)), block(width)]
        + [block(part.shape[1]) for part in heads],
        out_specs=(block(width), whole(weight), whole(weight), whole((8, width))),
        out_shape=(
            jax.ShapeDtypeStruct((rows, width), BF),
            jax.ShapeDtypeStruct(weight, BF),
            jax.ShapeDtypeStruct(weight, BF),
            jax.ShapeDtypeStruct((8, width), F32),
        ),
        scratch_shapes=[pltpu.VMEM((rows, lanes), BF) for lanes in kept],
        compiler_params=params(60 if heads else 40),
        cost_estimate=cost(
            2 * rows * D * (width // 3 + width) + rows * 3e5 * len(groups), 12 * rows * D
        ),
        name=f"attention_back_{groups[0]}",
    )(place, mask, grad_attended, normed, w_out, mixed, *heads)


TILE = 256


def gelu_and_slope(values):
    below = 0.5 + 0.5 * lax.erf(values * math.sqrt(0.5))
    bell = jnp.exp(-0.5 * values * values) * (1.0 / math.sqrt(2.0 * math.pi))
    return values * below, below + values * bell


def both_ways(chunk, bias, weights, left, right, rows, kept_active, kept_before, sums):
    tiles = D // TILE
    for half in range(2):
        up, down = weights[2 * half], weights[2 * half + 1]
        for tile in range(tiles):
            columns = slice(tile * TILE, (tile + 1) * TILE)
            kept = slice(half * D + tile * TILE, half * D + (tile + 1) * TILE)
            before = nn(left, up[:, columns]) + bias[2 * chunk + half, :, columns]
            active, slope = gelu_and_slope(before)
            kept_active[rows, kept] = active.astype(BF)
            low = (nt(right, down[columns, :]) * slope).astype(BF)
            kept_before[rows, kept] = low
            sums[half, :, columns] += column_sum(low.astype(F32))
    result = nn(kept_active[rows, :D], weights[1][...])
    result += nn(kept_active[rows, D:], weights[3][...])
    pulled = nt(kept_before[rows, :D], weights[0][...])
    pulled += nt(kept_before[rows, D:], weights[2][...])
    return result, pulled


def hidden_grads(tile, blocks, kept, gw):
    kept_normed, kept_grad, kept_active, kept_before = kept

    def ordered(value):
        if blocks:
            value = jnp.concatenate([value[at : at + size] for at, size in blocks], axis=0)
        return value.astype(BF)

    for half in range(2):
        columns = slice(half * D, (half + 1) * D)

        @pl.when(tile == 2 * half)
        def _():
            gw[...] = ordered(tn(kept_normed[...], kept_before[:, columns]))

        @pl.when(tile == 2 * half + 1)
        def _():
            gw[...] = ordered(tn(kept_active[:, columns], kept_grad[...]))


def routed_rows(picked, grads, vec):
    inputs = picked[...].astype(F32)
    grad_rows = grads[...].astype(F32)
    routed = jnp.sum(inputs * vec[8:9, :].astype(F32), axis=-1, keepdims=True)
    return inputs, grad_rows, routed, routed * grad_rows


def first_mlp_kernel(steps, size, blocks, bias, vec, w_out, picked, grads, *refs):
    heads = refs[: len(SETS)]
    refs = refs[len(SETS) :]
    weights = refs[:4]
    attended, normed, out, back, gw, sums = refs[4:10]
    kept = refs[10:]
    kept_normed, kept_grad, kept_active, kept_before = kept
    step = pl.program_id(0)

    @pl.when(step == 0)
    def _():
        sums[...] = jnp.zeros_like(sums)

    @pl.when(step < steps)
    def _():
        rows = pl.ds(pl.multiple_of(step * size, 16), size)
        inputs, _, _, grad_branch = routed_rows(picked, grads, vec)
        right = grad_branch.astype(BF)
        joined = jnp.concatenate([part[...] for part in heads], axis=1)
        mixed = nn(joined, w_out[...]) + vec[4:5, :].astype(F32)
        attended[...] = mixed
        unit, _ = normalize(inputs + mixed)
        left = (unit * vec[5:6, :].astype(F32) + vec[6:7, :].astype(F32)).astype(BF)
        normed[...] = left
        kept_normed[rows, :] = left
        kept_grad[rows, :] = right
        out[...], back[...] = both_ways(
            0, bias, weights, left, right, rows, kept_active, kept_before, sums
        )

    @pl.when(step >= steps)
    def _():
        hidden_grads(step - steps, blocks, kept, gw)


def second_mlp_kernel(
    steps, size, blocks, place, bias, vec, picked, grads, normed, attended, out, back, *refs
):
    weights = refs[:4]
    (grad_attended, carry, values, turn_sums, sums, gw) = refs[4:10]
    kept = refs[10:]
    kept_normed, kept_grad, kept_active, kept_before = kept
    step = pl.program_id(0)

    @pl.when(step == 0)
    def _():
        sums[...] = jnp.zeros_like(sums)
        turn_sums[...] = jnp.zeros_like(turn_sums)

    @pl.when(step < steps)
    def _():
        rows = pl.ds(pl.multiple_of(step * size, 16), size)
        inputs, grad_rows, routed, grad_branch = routed_rows(picked, grads, vec)
        left = normed[...]
        right = grad_branch.astype(BF)
        kept_normed[rows, :] = left
        kept_grad[rows, :] = right
        result, pulled = both_ways(
            1, bias, weights, left, right, rows, kept_active, kept_before, sums
        )
        pulled += back[...]
        router = vec[8:9, :].astype(F32)
        mixed = attended[...]
        branch = mixed + (result + out[...]) + vec[7:8, :].astype(F32)
        values[...] = (inputs + routed * branch).astype(BF)
        grad_routed = jnp.sum(grad_rows * branch, axis=-1, keepdims=True)
        unit, inverse = normalize(inputs + mixed)
        residual = norm_back(pulled, unit, inverse, vec[5:6, :].astype(F32))
        low = (grad_branch + residual).astype(BF)
        grad_attended[...] = low
        carry[...] = residual + grad_routed * router
        turn_sums[0:1, :] += column_sum(low.astype(F32))
        turn_sums[1:2, :] += column_sum(pulled * unit)
        turn_sums[2:3, :] += column_sum(pulled)
        turn_sums[3:4, :] += column_sum(right.astype(F32))
        turn_sums[4:5, :] += column_sum(inputs * grad_routed)

    @pl.when(step >= steps)
    def _():
        hidden_grads(step - steps, blocks, kept, gw)


def mlp_specs(chunk, rows):
    size = (2 - chunk) * PAD
    steps = rows // size
    last = steps - 1

    def wide(width=D):
        return pl.BlockSpec((size, width), lambda i: (jnp.minimum(i, last), 0))

    weights = [
        pl.BlockSpec((D, D), lambda i, at=at: (0, at), pipeline_mode=pl.Buffered(1))
        for at in (0, 2, 1, 3)
    ]

    def gw_block(i):
        tile = jnp.clip(i - steps, 0, 3)
        return (0, tile // 2 + 2 * (tile % 2))

    scratch = [
        pltpu.VMEM((rows, D), BF),
        pltpu.VMEM((rows, D), BF),
        pltpu.VMEM((rows, 2 * D), BF),
        pltpu.VMEM((rows, 2 * D), BF),
    ]
    return size, steps, 4, wide, weights, pl.BlockSpec((D, D), gw_block), scratch


def first_mlp(blocks, bias, vec, picked, grads, heads, weights):
    rows = picked.shape[0]
    size, steps, tiles, wide, weight_specs, gw, scratch = mlp_specs(0, rows)
    total = jax.ShapeDtypeStruct((rows, D), F32)
    return pl.pallas_call(
        functools.partial(first_mlp_kernel, steps, size, blocks),
        grid=(steps + tiles,),
        in_specs=[whole(bias.shape), whole((16, D))]
        + [pl.BlockSpec((D, D), lambda i: (0, 4), pipeline_mode=pl.Buffered(1))]
        + [wide()] * 2
        + [wide(part.shape[1]) for part in heads]
        + weight_specs,
        out_specs=(wide(),) * 4 + (gw, whole((2, 1, D))),
        out_shape=(
            total,
            jax.ShapeDtypeStruct((rows, D), BF),
            total,
            total,
            jax.ShapeDtypeStruct((D, 4 * D), BF),
            jax.ShapeDtypeStruct((2, 1, D), F32),
        ),
        scratch_shapes=scratch,
        compiler_params=params(),
        cost_estimate=cost(26 * rows * D * D, 30 * rows * D, 4 * rows * D),
        name="feed_forward_0",
    )(bias, vec, weights, picked, grads, *heads, *[weights] * 4)


def second_mlp(blocks, place, bias, vec, picked, grads, normed, attended, out, back, weights):
    rows = picked.shape[0]
    size, steps, tiles, wide, weight_specs, gw, scratch = mlp_specs(1, rows)
    low = jax.ShapeDtypeStruct((rows, D), BF)
    return pl.pallas_call(
        functools.partial(second_mlp_kernel, steps, size, blocks),
        grid=(steps + tiles,),
        in_specs=[SMEM, whole(bias.shape), whole((16, D))]
        + [wide()] * 6
        + weight_specs,
        out_specs=(wide(), wide(), wide(), whole((8, D)), whole((2, 1, D)), gw),
        out_shape=(
            low,
            jax.ShapeDtypeStruct((rows, D), F32),
            low,
            jax.ShapeDtypeStruct((8, D), F32),
            jax.ShapeDtypeStruct((2, 1, D), F32),
            jax.ShapeDtypeStruct((D, 4 * D), BF),
        ),
        scratch_shapes=scratch,
        compiler_params=params(),
        cost_estimate=cost(26 * rows * D * D, 40 * rows * D, 4 * rows * D),
        name="feed_forward_1",
    )(place, bias, vec, picked, grads, normed, attended, out, back, *[weights] * 4)


def first_back_kernel(count, vec, picked, grads, carry, *refs):
    mixed = refs[:count]
    weights = refs[count : 3 * count]
    values, sums = refs[3 * count : 3 * count + 2]
    kept = refs[3 * count + 2 :]

    @pl.when(pl.program_id(0) == 0)
    def _():
        sums[...] = jnp.zeros_like(sums)
        for index in range(count):
            half = mixed[index].shape[1] // 2
            kept[index][:, :half] = weights[2 * index][:, :half]
            kept[index][:, half:] = weights[2 * index + 1][:, :half]

    pulled = nt(mixed[0][...], kept[0][...])
    for index in range(1, count):
        pulled += nt(mixed[index][...], kept[index][...])
    unit, inverse = normalize(picked[...].astype(F32))
    grad = norm_back(pulled, unit, inverse, vec[0:1, :].astype(F32))
    values[...] = (grads[...].astype(F32) + grad + carry[...]).astype(BF)
    sums[0:1, :] += column_sum(pulled * unit)
    sums[1:2, :] += column_sum(pulled)


def first_back(vec, picked, grads, carry, mixed, weights):
    rows = picked.shape[0]
    size = 2 * PAD
    wide = pl.BlockSpec((size, D), lambda i: (i, 0))
    flat = [weight for pair in weights for weight in pair]
    return pl.pallas_call(
        functools.partial(first_back_kernel, len(mixed)),
        grid=(rows // size,),
        in_specs=[whole((16, D)), wide, wide, wide]
        + [pl.BlockSpec((size, part.shape[1]), lambda i: (i, 0)) for part in mixed]
        + [whole(weight.shape) for weight in flat],
        out_specs=(wide, whole((8, D))),
        out_shape=(jax.ShapeDtypeStruct((rows, D), BF), jax.ShapeDtypeStruct((8, D), F32)),
        scratch_shapes=[pltpu.VMEM((D, part.shape[1]), BF) for part in mixed],
        compiler_params=params(44),
        cost_estimate=cost(6 * rows * D * D, 16 * rows * D),
        name="first_norm_back",
    )(vec, picked, grads, carry, *mixed, *flat)


def put_kernel(span, places, source, value, after, out, both):
    width = places.shape[2]
    for image in range(IMAGES):
        rows = slice(image * span, (image + 1) * span)
        both[:PAD, :] = value[image * PAD : (image + 1) * PAD, :]
        if image + 1 < IMAGES:
            both[PAD:, :] = value[(image + 1) * PAD : (image + 1) * PAD + 16, :]
        else:
            both[PAD:, :] = after[...]
        same = lax.broadcasted_iota(jnp.int32, (span, width), 0) == places[image]
        hot = same.astype(F32)
        kept = jnp.max(hot, axis=-1, keepdims=True) > 0.5
        moved = nn(hot.astype(BF), both[...])
        out[rows, :] = jnp.where(kept, moved, source[rows, :].astype(F32)).astype(BF)


def put(places, source, values):
    rows = source.shape[0]
    count = places.shape[0]
    span = -(-(rows // count) // 16) * 16
    steps = count // IMAGES
    block = pl.BlockSpec((IMAGES * span, D), lambda i: (i, 0))
    return pl.pallas_call(
        functools.partial(put_kernel, span),
        grid=(steps,),
        in_specs=[
            pl.BlockSpec((IMAGES, 1, places.shape[2]), lambda i: (i, 0, 0)),
            block,
            pl.BlockSpec((IMAGES * PAD, D), lambda i: (i, 0)),
            pl.BlockSpec(
                (16, D), lambda i: (jnp.minimum(i + 1, steps - 1) * (IMAGES * PAD // 16), 0)
            ),
        ],
        out_specs=block,
        out_shape=jax.ShapeDtypeStruct((rows, D), BF),
        scratch_shapes=[pltpu.VMEM((PAD + 16, D), BF)],
        compiler_params=params(24),
        cost_estimate=cost(2 * rows * D * (PAD + 16), 6 * rows * D),
        name="put_rows",
    )(places, source, values, values)


def put_places(keep_slots, image_tokens):
    count = keep_slots.shape[0]
    span = -(-image_tokens // 16) * 16
    image = jnp.arange(count, dtype=jnp.int32)[:, None]
    own = keep_slots + image * (image_tokens - span)
    following = jnp.concatenate([keep_slots[1:, :16], jnp.full((1, 16), -span, jnp.int32)], axis=0)
    following = following + (image + 1) * image_tokens - image * span
    following = jnp.where(image < count - 1, following, -1)
    gap = jnp.full((count, PAD - KEEP), -1, jnp.int32)
    return jnp.concatenate([own, gap, following], axis=1)[:, None, :]


class Moves:
    def __init__(self, n_dp, n_fsdp):
        self.n_dp = n_dp
        self.n_fsdp = n_fsdp
        self.squares = n_fsdp // 2
        outer = lax.axis_index("dp")
        inner = lax.axis_index("fsdp")
        self.z = outer
        self.yx = inner // 2
        self.core = inner % 2
        self.place = jnp.stack([self.z, self.yx, self.core]).astype(jnp.int32)

    def swap(self, value, mask):
        total = self.n_dp * self.n_fsdp
        return lax.ppermute(value, AXES, [(i, i ^ mask) for i in range(total)])

    def over_z(self, values):
        return [values[0]] + [self.swap(values[k], k * self.n_fsdp) for k in range(1, self.n_dp)]

    def over_yx(self, values):
        return [values[0]] + [self.swap(values[k], 2 * k) for k in range(1, self.squares)]

    def over_core(self, value):
        return self.swap(value, 1)

    def square_blocks(self, size):
        return [
            ((z * self.n_fsdp + inner) * size, size)
            for inner in range(self.n_fsdp)
            for z in range(self.n_dp)
        ]

    def over_square(self, value, ordered):
        rows, n = value.shape
        if not ordered:
            value = value.reshape(self.n_dp, self.n_fsdp, -1, n).transpose(1, 0, 2, 3)
        value = value.reshape(rows, n)
        return lax.psum_scatter(value, "fsdp", scatter_dimension=0, tiled=True)

    def by_chip(self, value):
        chips = self.n_dp * self.squares
        return value.reshape(self.n_dp, self.squares, value.shape[0] // chips, value.shape[1])

    def add_cores(self, place, keeps, arrived):
        keeps = [self.by_chip(value) for value in keeps]
        arrived = [self.by_chip(value) for value in arrived]
        return add_pairs(place, keeps, arrived, self.squares)


def add_parts(parts):
    total = parts[0].astype(F32)
    for part in parts[1:]:
        total = total + part.astype(F32)
    return total


def together(*values):
    return lax.optimization_barrier(values)


def after(value, *others):
    return lax.optimization_barrier((value, *others))[0]


def place_kernel(axis, count, cuts, place, *refs):
    outs = refs[count:]
    me = place[axis]
    for k in range(count):
        for (first, width), out in zip(cuts, outs):
            if axis == 0:
                out[me ^ k] = refs[k][:, first : first + width]
            else:
                out[:, me ^ k] = refs[k][...]


def place_blocks(place, axis, blocks, widths):
    count = len(blocks)
    cuts, at = [], 0
    for width in widths:
        cuts.append((at, width))
        at += width
    shape = blocks[0].shape[:-1]
    shape = shape[:axis] + (count,) + shape[axis:]
    vmem = pl.BlockSpec(memory_space=pltpu.VMEM)
    return pl.pallas_call(
        functools.partial(place_kernel, axis, count, cuts),
        in_specs=[SMEM] + [vmem] * count,
        out_specs=[vmem] * len(widths),
        out_shape=[jax.ShapeDtypeStruct(shape + (width,), BF) for width in widths],
        compiler_params=params(24),
        cost_estimate=cost(0, 4 * math.prod(shape) * at),
        name="place_blocks",
    )(place, *blocks)


def add_pairs_kernel(parts, squares, place, *refs):
    outs = refs[2 * parts * squares :]
    at = 0
    for part in range(parts):
        for k in range(squares):
            index = part * squares + k
            left, right = refs[index], refs[parts * squares + index]
            width = left.shape[3]
            total = left[...].astype(F32) + right[...].astype(F32)
            outs[k][:, :, at : at + width] = total[:, 0].astype(BF)
        at += width


def add_pairs(place, keeps, arrived, squares):
    specs, left, right = [], [], []
    n_dp, _, m, _ = keeps[0].shape
    for keep, other in zip(keeps, arrived):
        for k in range(squares):
            specs.append(
                pl.BlockSpec(
                    (n_dp, 1, m, keep.shape[3]), lambda i, place, k=k: (0, place[1] ^ k, 0, 0)
                )
            )
            left.append(keep)
            right.append(other)
    shape = (n_dp, m, sum(keep.shape[3] for keep in keeps))
    return pl.pallas_call(
        functools.partial(add_pairs_kernel, len(keeps), squares),
        grid_spec=pltpu.PrefetchScalarGridSpec(
            num_scalar_prefetch=1,
            grid=(1,),
            in_specs=specs + specs,
            out_specs=[pl.BlockSpec(shape, lambda i, place: (0, 0, 0))] * squares,
        ),
        out_shape=[jax.ShapeDtypeStruct(shape, BF)] * squares,
        compiler_params=params(24),
        cost_estimate=cost(0, 6 * squares * math.prod(shape)),
        name="add_cores",
    )(place, *left, *right)


def add_blocks_kernel(count, rows, sizes, place, *refs):
    outs = refs[count * sum(sizes) :]
    at = 0
    for index in range(count):
        lane = 0
        for terms in sizes:
            total = refs[at][0].astype(F32)
            for term in range(1, terms):
                total = total + refs[at + term][0].astype(F32)
            at += terms
            for first in range(0, total.shape[0], rows):
                width = total.shape[1]
                outs[index][:, lane : lane + width] = total[first : first + rows].astype(BF)
                lane += width


def add_blocks(place, groups, n_dp, rows):
    specs, operands, lanes = [], [], 0
    for arrays in groups:
        _, m, n = arrays[0].shape
        lanes += n * (m // rows)
    for k in range(n_dp):
        for arrays in groups:
            _, m, n = arrays[0].shape
            spec = pl.BlockSpec((1, m, n), lambda i, place, k=k: (place[0] ^ k, 0, 0))
            specs += [spec] * len(arrays)
            operands += arrays
    sizes = [len(arrays) for arrays in groups]
    return pl.pallas_call(
        functools.partial(add_blocks_kernel, n_dp, rows, sizes),
        grid_spec=pltpu.PrefetchScalarGridSpec(
            num_scalar_prefetch=1,
            grid=(1,),
            in_specs=specs,
            out_specs=[pl.BlockSpec((rows, lanes), lambda i, place: (0, 0))] * n_dp,
        ),
        out_shape=[jax.ShapeDtypeStruct((rows, lanes), BF)] * n_dp,
        compiler_params=params(24),
        cost_estimate=cost(0, 4 * n_dp * rows * lanes * max(sizes)),
        name="add_squares",
    )(place, *operands)


def planes_kernel(count, place, *refs):
    rows = refs[0].shape[1]
    out = refs[-1]
    lane = 0
    for ref in refs[:count]:
        out[0, :, lane : lane + ref.shape[2]] = ref[0]
        lane += ref.shape[2]
    total = refs[count][0].astype(F32)
    for ref in refs[count + 1 : -1]:
        total = total + ref[0].astype(F32)
    width = total.shape[1]
    for first in range(0, total.shape[0], rows):
        out[0, :, lane : lane + width] = total[first : first + rows].astype(BF)
        lane += width


def planes(place, ready, parts):
    n_dp, rows, _ = ready[0].shape
    arrays = ready + parts
    lanes = sum(value.shape[2] for value in ready) + parts[0].shape[1] // rows * parts[0].shape[2]
    return pl.pallas_call(
        functools.partial(planes_kernel, len(ready)),
        grid=(n_dp,),
        in_specs=[SMEM] + [pl.BlockSpec((1,) + a.shape[1:], lambda i: (i, 0, 0)) for a in arrays],
        out_specs=pl.BlockSpec((1, rows, lanes), lambda i: (i, 0, 0)),
        out_shape=jax.ShapeDtypeStruct((n_dp, rows, lanes), BF),
        compiler_params=params(),
        cost_estimate=cost(0, 4 * n_dp * rows * lanes),
        name="planes",
    )(place, *arrays)


def quarters_kernel(total, part, up, down, project_out, *outs):
    outs[0][:, 4 * D :] = project_out[...].astype(BF)
    for chunk, out in enumerate(outs):
        for half in range(2):
            quarter = 2 * chunk + half
            pieces = [
                up[:, (owner * QUARTERS + quarter) * part : (owner * QUARTERS + quarter + 1) * part]
                for owner in range(total)
            ]
            out[:, half * D : (half + 1) * D] = jnp.concatenate(pieces, axis=1).astype(BF)
            rows = slice(quarter * part, (quarter + 1) * part)
            out[:, (2 + half) * D : (3 + half) * D] = down[rows, :].astype(BF)


def to_quarters(total, up, down, project_out):
    rows = up.shape[0]
    part = down.shape[0] // QUARTERS
    shape = jax.ShapeDtypeStruct((rows, 4 * D), BF)
    if part % 8:
        ups = up.astype(BF).reshape(rows, total, QUARTERS, part).transpose(2, 0, 1, 3)
        ups = ups.reshape(QUARTERS, rows, D)
        downs = down.astype(BF).reshape(QUARTERS, part, D)
        first = [ups[0], ups[1], downs[0], downs[1], project_out.astype(BF)]
        second = [ups[2], ups[3], downs[2], downs[3]]
        return [jnp.concatenate(first, axis=1), jnp.concatenate(second, axis=1)]
    vmem = pl.BlockSpec(memory_space=pltpu.VMEM)
    return pl.pallas_call(
        functools.partial(quarters_kernel, total, part),
        in_specs=[vmem] * 3,
        out_specs=[vmem] * 2,
        out_shape=[jax.ShapeDtypeStruct((rows, 5 * D), BF), shape],
        compiler_params=params(),
        cost_estimate=cost(0, 12 * rows * 4 * D),
        name="to_quarters",
    )(up, down, project_out)


def hidden_kernel(total, part, value, up, down):
    pieces = []
    for owner in range(total):
        for quarter in range(QUARTERS):
            at = (4 * (quarter // 2) + quarter % 2) * D + owner * part
            pieces.append(value[:, at : at + part].astype(F32))
    up[...] = jnp.concatenate(pieces, axis=1)
    for quarter in range(QUARTERS):
        at = (4 * (quarter // 2) + 2 + quarter % 2) * D
        down[quarter * part : (quarter + 1) * part, :] = value[:, at : at + D].astype(F32)


def from_quarters(total, value):
    rows = value.shape[0]
    part = D // total
    if part % 8:
        quarters = value.astype(F32).reshape(rows, CHUNKS, 2, 2, D)
        ups = quarters[:, :, 0].reshape(rows, QUARTERS, total, part).transpose(0, 2, 1, 3)
        downs = quarters[:, :, 1].reshape(rows, QUARTERS, D).transpose(1, 0, 2)
        return ups.reshape(rows, HIDDEN), downs.reshape(QUARTERS * part, D)
    vmem = pl.BlockSpec(memory_space=pltpu.VMEM)
    return pl.pallas_call(
        functools.partial(hidden_kernel, total, part),
        in_specs=[vmem],
        out_specs=[vmem] * 2,
        out_shape=[
            jax.ShapeDtypeStruct((rows, HIDDEN), F32),
            jax.ShapeDtypeStruct((QUARTERS * part, D), F32),
        ],
        compiler_params=params(16),
        cost_estimate=cost(0, 6 * rows * 8 * D),
        name="from_quarters",
    )(value)


def unit_pieces(total):
    part = D // total
    for quarter in range(QUARTERS):
        for owner in range(total):
            first = (owner * QUARTERS + quarter) * part
            yield quarter, owner * part, first // D, first % D


def vectors_kernel(total, source, vec, bias):
    rows = source[...].astype(F32).T[:16, :]
    vec[...] = rows.astype(BF)
    part = D // total
    pieces = [[] for _ in range(QUARTERS)]
    for quarter, _, row, lane in unit_pieces(total):
        pieces[quarter].append(rows[9 + row : 10 + row, lane : lane + part])
    for quarter in range(QUARTERS):
        bias[quarter] = jnp.concatenate(pieces[quarter], axis=1)


def vectors_of(total, gathered):
    if D // total % 8:
        vec = gathered[:, -128:-112].T
        bias = vec[9:13].astype(F32).reshape(total, QUARTERS, -1).transpose(1, 0, 2)
        return vec, bias.reshape(QUARTERS, 1, D)
    return pl.pallas_call(
        functools.partial(vectors_kernel, total),
        grid=(1,),
        in_specs=[pl.BlockSpec((D, 128), lambda i: (0, gathered.shape[1] // 128 - 1))],
        out_specs=[whole((16, D)), whole((QUARTERS, 1, D))],
        out_shape=[
            jax.ShapeDtypeStruct((16, D), BF),
            jax.ShapeDtypeStruct((QUARTERS, 1, D), F32),
        ],
        compiler_params=params(16),
        cost_estimate=cost(0, 4 * D * 128),
        name="vectors",
    )(gathered)


def pair_sums(core, sums, groups, part):
    width = 3 * PW
    half = len(groups) * width
    pieces = []
    for index in range(len(groups)):
        at = index * width + part * PW
        own = sums[0:1, at : at + PW]
        other = sums[0:1, half + at : half + at + PW]
        pieces += [jnp.where(core == 0, own, other), jnp.where(core == 0, other, own)]
    return pieces


def table_kernel(total, place, *refs):
    (first, sums_a, sums_b, turn, sums_0, sums_1, summed) = refs[:7]
    parts, (table, mine, send) = refs[7:-3], refs[-3:]
    core = place[2]
    table[...] = jnp.zeros_like(table)
    table[0:2, :] = first[0:2, :]
    for row, part in ((2, 0), (3, 2)):
        pieces = pair_sums(core, sums_a, SETS[0], part) + pair_sums(core, sums_b, SETS[1], part)
        table[row : row + 1, :] = jnp.concatenate(pieces, axis=1)
    table[4:9, :] = turn[0:5, :]
    size = D // total
    pieces = sorted((row, lane, quarter, at) for quarter, at, row, lane in unit_pieces(total))
    for row in range(4):
        values = []
        for _, _, quarter, at in pieces[row * len(pieces) // 4 : (row + 1) * len(pieces) // 4]:
            source = sums_1 if quarter // 2 else sums_0
            values.append(source[quarter % 2][:, at : at + size])
        table[9 + row : 10 + row, :] = jnp.concatenate(values, axis=1)
    last = parts[0][...].astype(F32)
    for part in parts[1:]:
        last = last + part[...].astype(F32)
    hidden = 8 * D
    half = (summed.shape[1] - hidden) // 2
    squares = jnp.sum(last * last, keepdims=True)
    for at in range(0, summed.shape[1], 2 * D):
        piece = summed[:, at : min(at + 2 * D, summed.shape[1])].astype(F32)
        squares = squares + jnp.sum(piece * piece, keepdims=True)
    table[13:14, :] = jnp.broadcast_to(squares, (1, D))
    later = summed[:, hidden:].astype(F32)
    for at, value in ((0, later), (half, last)):
        width = value.shape[1] // 2
        one, two = value[:, :width], value[:, width:]
        mine[:, at : at + width] = jnp.where(core == 0, one, two)
        send[:, at : at + width] = jnp.where(core == 0, two, one)


def make_table(total, place, first, sums_a, sums_b, turn, sums_0, sums_1, summed, parts):
    rows = summed.shape[0]
    lanes = (summed.shape[1] - 8 * D + parts[0].shape[1]) // 2
    vmem = pl.BlockSpec(memory_space=pltpu.VMEM)
    half = jax.ShapeDtypeStruct((rows, lanes), F32)
    return pl.pallas_call(
        functools.partial(table_kernel, total),
        in_specs=[SMEM] + [vmem] * (7 + len(parts)),
        out_specs=[vmem] * 3,
        out_shape=[jax.ShapeDtypeStruct((16, D), F32), half, half],
        compiler_params=params(),
        cost_estimate=cost(0, 20 * rows * lanes),
        name="table",
    )(place, first, sums_a, sums_b, turn, sums_0, sums_1, summed, *parts)


def whole_rows(core, mine, theirs):
    ordered = (
        jnp.where(core == 0, mine[...], theirs[...]),
        jnp.where(core == 0, theirs[...], mine[...]),
    )
    half = D // 2
    outs = jnp.concatenate([value[:, :half] for value in ordered], axis=1)
    pieces = []
    for part in range(3):
        at = half
        for groups in SETS:
            for index in range(len(groups)):
                lane = at + (3 * index + part) * PW
                pieces += [value[:, lane : lane + PW] for value in ordered]
            at += 3 * PW * len(groups)
    return jnp.concatenate(pieces, axis=1), outs


def adam_kernel(place, table, mine, theirs, up, down, own, *refs):
    kinds = 5
    masters, firsts, seconds = (refs[i * kinds : (i + 1) * kinds] for i in range(3))
    outs = refs[3 * kinds :]
    grads = whole_rows(place[2], mine, theirs) + (up[...], down[...], own[...])
    vector_rows = masters[4].shape[0]
    vectors = table[:vector_rows, :]
    squares = jnp.sum(vectors * vectors, keepdims=True) + table[vector_rows : vector_rows + 1, :1]
    grad_norm = jnp.sqrt(squares)
    factor = jnp.minimum(1.0, clip_share * math.sqrt(PARAMS) / (grad_norm + 1e-06))
    outs[0][...] = grad_norm
    for kind in range(kinds):
        rate = vector_rate if kind == 4 else matrix_rate
        decay = 0.0 if kind == 4 else matrix_decay
        master = masters[kind][...]
        grad = grads[kind] * factor
        first_new = first_beta * firsts[kind][...] + (1.0 - first_beta) * grad
        second_new = second_beta * seconds[kind][...] + (1.0 - second_beta) * grad * grad
        first_hat = first_new * (1.0 / (1.0 - first_beta**STEP))
        second_hat = second_new * (1.0 / (1.0 - second_beta**STEP))
        step = first_hat / (jnp.sqrt(second_hat) + adam_eps)
        updated = master - rate * (step + decay * master)
        outs[1 + kind][...] = first_new
        outs[1 + kinds + kind][...] = second_new
        outs[1 + 2 * kinds + kind][...] = updated
        outs[1 + 3 * kinds + kind][...] = updated.astype(BF)


def adam(place, table, mine, theirs, up, down, own, masters, firsts, seconds):
    vmem = pl.BlockSpec(memory_space=pltpu.VMEM)
    shapes = [master.shape for master in masters]
    states = [jax.ShapeDtypeStruct(shape, F32) for shape in shapes]
    outs = [jax.ShapeDtypeStruct((1, 1), F32)] + states * 3
    outs += [jax.ShapeDtypeStruct(shape, BF) for shape in shapes]
    elements = sum(math.prod(shape) for shape in shapes)
    return pl.pallas_call(
        adam_kernel,
        in_specs=[SMEM] + [vmem] * 21,
        out_specs=[vmem] * len(outs),
        out_shape=outs,
        compiler_params=params(),
        cost_estimate=cost(20 * elements, 30 * elements),
        name="adam",
    )(place, table, mine, theirs, up, down, own, *masters, *firsts, *seconds)


def on_device(
    n_dp,
    n_fsdp,
    tokens,
    keep_slots,
    cotangent,
    project_in,
    project_out,
    expand,
    contract,
    vectors,
    first_in,
    first_out,
    first_expand,
    first_contract,
    first_vectors,
    second_in,
    second_out,
    second_expand,
    second_contract,
    second_vectors,
):
    moves = Moves(n_dp, n_fsdp)
    place, core = moves.place, moves.core
    total = n_dp * n_fsdp
    rows_in = project_in.shape[0]
    part = contract.shape[0] // QUARTERS
    owner = moves.z * n_fsdp + lax.axis_index("fsdp")
    columns = vectors.shape[1]

    shards = to_quarters(total, expand, contract, project_out)
    w_hidden = [lax.all_gather(shards[0], AXES, axis=0, tiled=True)]

    def pair_columns(value, pair):
        return [value[:, at * D + pair * PW : at * D + (pair + 1) * PW] for at in range(3)]

    low_in = project_in.astype(BF)
    low_vec = jnp.pad(vectors.astype(BF).T, ((0, 0), (0, 128 - vectors.shape[0])))
    halves = []
    for parity in range(2):
        parts = []
        for index, groups in enumerate(SETS):
            for group in groups:
                parts += pair_columns(low_in, 2 * group + parity)
            if index == 0:
                parts.append(low_vec)
        halves.append(jnp.concatenate(parts, axis=1))
    mine = jnp.where(core == 0, halves[0], halves[1])
    theirs = jnp.where(core == 0, halves[1], halves[0])
    arrived = moves.over_core(theirs)
    rows = jnp.where(
        core == 0,
        jnp.concatenate([mine, arrived], axis=0),
        jnp.concatenate([arrived, mine], axis=0),
    )
    step = 3 * PW
    cut = len(SETS[0]) * step + 128
    widths = (cut, rows.shape[1] - cut)

    count = keep_slots.shape[0]
    image_tokens = tokens.shape[0] // count
    slots = jnp.pad(keep_slots, ((0, 0), (0, PAD - KEEP)), constant_values=-4 * image_tokens)
    slots = slots[:, :, None]
    parts = moves.over_z([rows] * n_dp)
    picked = pick(place, tokens, slots)
    picked, *parts = together(picked, *parts)
    first_stack, second_stack = place_blocks(place, 0, parts, widths)
    parts = moves.over_yx([first_stack] * moves.squares)
    (first_own,) = place_blocks(place, 1, parts, widths[:1])
    first_own = first_own.reshape(D, widths[0])
    first_other = moves.over_core(first_own)
    vec, bias = vectors_of(total, first_own)

    mask = local_mask()
    first_own, first_other, second_stack = together(first_own, first_other, second_stack)
    parts = moves.over_yx([second_stack] * moves.squares)
    mixed_0, heads_0, normed_one = heads_forward(
        SETS[0], place, mask, vec, picked, first_own, first_other
    )
    grad_rows = pick(after(place, heads_0), cotangent, slots)
    mixed_0, heads_0, normed_one, grad_rows, *parts = together(
        mixed_0, heads_0, normed_one, grad_rows, *parts
    )
    (second_own,) = place_blocks(place, 1, parts, widths[1:])
    second_own = second_own.reshape(D, widths[1])
    second_other = moves.over_core(second_own)
    w_in = [(first_own, first_other), (second_own, second_other)]
    shard = after(shards[1], second_own)
    parts = moves.over_z([shard] * n_dp)
    mixed_1, heads_1 = heads_forward(SETS[1], place, mask, vec, normed_one, *w_in[1])
    mixed_1, heads_1, *parts = together(mixed_1, heads_1, *parts)
    (stack,) = place_blocks(place, 0, parts, [shard.shape[1]])
    gathered = lax.all_gather(stack, "fsdp", axis=1, tiled=True)
    w_hidden.append(gathered.reshape(D, shard.shape[1]))
    heads = [heads_0, heads_1]

    blocks = moves.square_blocks(rows_in) if rows_in % 8 == 0 else []
    attended, normed_two, out, back, gw_0, sums_0 = first_mlp(
        blocks, bias, vec, picked, grad_rows, heads, w_hidden[0]
    )
    hidden_0 = moves.over_square(gw_0, blocks)
    (
        grad_attended,
        carry,
        put_values,
        turn_sums,
        sums_1,
        gw_1,
    ) = second_mlp(
        blocks,
        place,
        bias,
        vec,
        picked,
        grad_rows,
        normed_two,
        attended,
        out,
        back,
        w_hidden[1],
    )
    hidden_1 = moves.over_square(gw_1, blocks)
    places = put_places(keep_slots, image_tokens)

    results = heads_backward(
        SETS[0], place, mask, grad_attended, normed_one, w_hidden[0], mixed_0, heads
    )
    gm_0, gw_own, gw_other, sums_a, hidden_0 = together(*results, hidden_0)
    blocks = moves.add_cores(place, [gw_own], [moves.over_core(gw_other)])
    later = moves.over_yx(blocks)
    results = heads_backward(
        SETS[1], after(place, *blocks), mask, grad_attended, normed_one, w_hidden[0], mixed_1
    )
    gm_1, gw_own, gw_other, sums_b, *later = together(*results, *later)
    blocks = moves.add_cores(place, [gw_own], [moves.over_core(gw_other)])
    last = moves.over_yx(blocks)
    hidden = [value.reshape(n_dp, rows_in, -1) for value in (hidden_0, hidden_1)]
    plane_sums = planes(after(place, *blocks), hidden, later)
    summed = lax.psum_scatter(
        plane_sums.reshape(n_dp * rows_in, -1), "dp", scatter_dimension=0, tiled=True
    )
    results = first_back(
        after(vec, plane_sums), picked, grad_rows, carry, [gm_0, gm_1], w_in
    )
    grad_values, first_sums, *last = together(*results, *last)
    blocks = add_blocks(place, [last], n_dp, rows_in)
    last = moves.over_z(blocks)
    input_grad = put(after(places, *blocks), cotangent, grad_values)
    input_grad, *last = together(input_grad, *last)
    table, mine, send = make_table(
        total,
        place,
        first_sums,
        sums_a,
        sums_b,
        turn_sums,
        sums_0,
        sums_1,
        summed,
        last,
    )
    parts = moves.over_z([table] * n_dp)
    theirs = moves.over_core(send)
    activations = put(after(places, table), tokens, put_values)
    activations, theirs, *parts = together(activations, theirs, *parts)
    table = add_parts(moves.over_yx([add_parts(parts)] * moves.squares))
    table = table + moves.over_core(table)

    summed_expand, summed_contract = from_quarters(total, summed[:, : 8 * D])
    own = lax.dynamic_slice_in_dim(table[:13], owner * columns, columns, axis=1)
    masters = (project_in, project_out, expand, contract, vectors)
    firsts = (first_in, first_out, first_expand, first_contract, first_vectors)
    seconds = (second_in, second_out, second_expand, second_contract, second_vectors)
    grad_norm, *updates = adam(
        place,
        table,
        mine,
        theirs,
        summed_expand,
        summed_contract,
        own,
        masters,
        firsts,
        seconds,
    )
    return (activations, input_grad, grad_norm.reshape(1), *updates)


def solution(mesh):
    split = P(AXES, None)
    columns = P(None, AXES)
    weights = (split, split, split, split, columns)
    return jax.shard_map(
        functools.partial(on_device, mesh.shape["dp"], mesh.shape["fsdp"]),
        mesh=mesh,
        in_specs=(split, split, split) + weights * 3,
        out_specs=(split, split, P()) + weights * 4,
        check_vma=False,
    )
```

```python
import functools
import math

import jax
import jax.numpy as jnp
from jax import lax
from jax.experimental import pallas as pl
from jax.experimental.pallas import tpu as pltpu
from jax.sharding import PartitionSpec as P

D = 768
HEADS = 12
HEAD_DIM = 64
KEEP_GLOBAL = 98
KEEP_LOCAL = 18
KEEP = 268
PARAMS = 7087872
STEP = 5

norm_eps = 1e-06
clip_share = 0.05
matrix_rate = 0.04
vector_rate = 0.3
matrix_decay = 0.05
first_beta = 0.5
second_beta = 0.5
adam_eps = 1e-08

AXES = ("dp", "fsdp")
BF = jnp.bfloat16
F32 = jnp.float32
NT = (((1,), (1,)), ((), ()))
TN = (((0,), (0,)), ((), ()))
PAD = -(-KEEP // 16) * 16
PAIRS = HEADS // 2
PW = 2 * HEAD_DIM
SETS = ((0,), (1, 2))
CHUNKS = 2
QUARTERS = 2 * CHUNKS
HIDDEN = 4 * D
IMAGES = 2
NEG = -1e30
SEGMENTS = (
    (0, 112, 0, KEEP_GLOBAL),
    (96, 112, KEEP_GLOBAL, 2 * KEEP_GLOBAL),
    (192, 80, 2 * KEEP_GLOBAL, KEEP),
)


def nn(left, right):
    return jnp.dot(left, right, preferred_element_type=F32)


def nt(left, right):
    return lax.dot_general(left, right, NT, preferred_element_type=F32)


def tn(left, right):
    return lax.dot_general(left, right, TN, preferred_element_type=F32)


def params(limit=60):
    return pltpu.CompilerParams(vmem_limit_bytes=limit * 2**20)


def cost(flops, moved, exps=0):
    return pl.CostEstimate(flops=int(flops), bytes_accessed=int(moved), transcendentals=int(exps))


def whole(shape):
    return pl.BlockSpec(shape, lambda *_: (0,) * len(shape))


ANY = pl.BlockSpec(memory_space=pl.ANY)
SMEM = pl.BlockSpec(memory_space=pltpu.SMEM)


def normalize(values):
    centred = values - jnp.mean(values, axis=-1, keepdims=True)
    spread = jnp.mean(centred * centred, axis=-1, keepdims=True)
    inverse = lax.rsqrt(spread + norm_eps)
    return centred * inverse, inverse


def norm_back(grad, normed, inverse, gain):
    pulled = grad * gain
    return inverse * (
        pulled
        - jnp.mean(pulled, axis=-1, keepdims=True)
        - normed * jnp.mean(pulled * normed, axis=-1, keepdims=True)
    )


def column_sum(values):
    return jnp.sum(values, axis=0, keepdims=True)


def window_start(step, image_tokens, rows, window):
    return jnp.minimum((IMAGES * image_tokens * step) // 16, (rows - window) // 16) * 16


def pick_kernel(image_tokens, rows, window, part, place, slots, source, picked):
    step = pl.program_id(0)
    shift = IMAGES * image_tokens * step - window_start(step, image_tokens, rows, window)
    for image in range(IMAGES):
        first = (image * image_tokens) // 16 * 16
        span = min(part, window - first)
        target = slots[image] + shift + image * image_tokens - first
        hot = lax.broadcasted_iota(jnp.int32, (PAD, span), 1) == target
        values = nn(hot.astype(F32).astype(BF), source[first : first + span, :])
        picked[image * PAD : (image + 1) * PAD, :] = values.astype(BF)


def pick(place, source, slots):
    rows = source.shape[0]
    count = slots.shape[0]
    image_tokens = rows // count
    window = -(-(IMAGES * image_tokens + 15) // 16) * 16
    part = -(-(image_tokens + 32) // 16) * 16
    start = functools.partial(
        window_start, image_tokens=image_tokens, rows=rows, window=window
    )
    return pl.pallas_call(
        functools.partial(pick_kernel, image_tokens, rows, window, part),
        grid=(count // IMAGES,),
        in_specs=[
            SMEM,
            pl.BlockSpec((IMAGES, PAD, 1), lambda i: (i, 0, 0)),
            pl.BlockSpec((pl.Element(window), pl.Element(D)), lambda i: (start(i), 0)),
        ],
        out_specs=pl.BlockSpec((IMAGES * PAD, D), lambda i: (i, 0)),
        out_shape=jax.ShapeDtypeStruct((count * PAD, D), BF),
        compiler_params=params(20),
        cost_estimate=cost(2 * count * PAD * window * D, 2 * rows * D + 2 * count * PAD * D),
        name="pick_rows",
    )(place, slots, source)


def local_mask():
    first, rows, low, high = SEGMENTS[2]
    slot = jnp.arange(rows) + first
    crop = jnp.where((slot >= low) & (slot < high), (slot - low) // KEEP_LOCAL, -1)
    same = (crop[:, None] == crop[None, :]) & (crop[:, None] >= 0)
    bias = jnp.where(same, 0.0, NEG).astype(F32)
    return jnp.concatenate([bias, bias], axis=1)


def lanes_of(rows):
    return lax.broadcasted_iota(jnp.int32, (rows, PW), 1) < HEAD_DIM


def split_heads(values):
    first = lanes_of(values.shape[0])
    zero = jnp.zeros_like(values)
    return jnp.concatenate(
        [jnp.where(first, values, zero), jnp.where(first, zero, values)], axis=0
    )


def join_heads(values):
    rows = values.shape[0] // 2
    return jnp.where(lanes_of(rows), values[:rows], values[rows:])


def rows_of(segment):
    return slice(segment[0], segment[0] + segment[1])


def attention(jobs, mask):
    chains = [(job, segment) for job in jobs for segment in SEGMENTS]
    scores = []
    for (query, key_rows, _), segment in chains:
        rows = rows_of(segment)
        scores.append(nt(split_heads(query[rows] * HEAD_DIM**-0.5), key_rows[rows]))
    mask = jnp.concatenate([mask[:, : mask.shape[0]]] * 2, axis=0)
    probs = []
    for (_, segment), score in zip(chains, scores):
        first, count, low, high = segment
        if low == 2 * KEEP_GLOBAL:
            score = score + mask
        else:
            slot = lax.broadcasted_iota(jnp.int32, (1, count), 1) + first
            score = jnp.where((slot >= low) & (slot < high), score, NEG)
        grown = jnp.exp(score - jnp.max(score, axis=-1, keepdims=True))
        probs.append((grown * (1.0 / jnp.sum(grown, axis=-1, keepdims=True))).astype(BF))
    parts = []
    for ((_, _, value), segment), prob in zip(chains, probs):
        parts.append(join_heads(nn(prob, value[rows_of(segment)])))
    slot = lax.broadcasted_iota(jnp.int32, (16, 1), 0)
    results = []
    for index in range(len(jobs)):
        one, two, three = parts[3 * index : 3 * index + 3]
        results.append(
            jnp.concatenate(
                [
                    one[:96],
                    jnp.where(slot + 96 < KEEP_GLOBAL, one[96:], two[:16]),
                    two[16:96],
                    jnp.where(slot + 192 < 2 * KEEP_GLOBAL, two[96:], three[:16]),
                    three[16:],
                ],
                axis=0,
            ).astype(BF)
        )
    return results


def attention_back(jobs, mask):
    chains = [(job, segment) for job in jobs for segment in SEGMENTS]
    halves, grads = [], []
    for (query, _, _, grad), segment in chains:
        first, count, low, high = segment
        rows = rows_of(segment)
        halves.append(split_heads(query[rows] * HEAD_DIM**-0.5))
        slot = lax.broadcasted_iota(jnp.int32, (count, 1), 0) + first
        kept = jnp.where((slot >= low) & (slot < high), grad[rows], jnp.zeros((), BF))
        grads.append(split_heads(kept))
    scores, grad_probs = [], []
    for ((_, key_rows, value, _), segment), half, grad in zip(chains, halves, grads):
        rows = rows_of(segment)
        scores.append(nt(key_rows[rows], half))
        grad_probs.append(nt(value[rows], grad))
    probs, grad_scores = [], []
    for (_, segment), score, pulled in zip(chains, scores, grad_probs):
        first, count, low, high = segment
        if low == 2 * KEEP_GLOBAL:
            score = score + mask
        else:
            slot = lax.broadcasted_iota(jnp.int32, (count, 1), 0) + first
            score = jnp.where((slot >= low) & (slot < high), score, NEG)
        grown = jnp.exp(score - jnp.max(score, axis=0, keepdims=True))
        prob = grown * (1.0 / jnp.sum(grown, axis=0, keepdims=True))
        weighted = jnp.sum(prob * pulled, axis=0, keepdims=True)
        probs.append(prob.astype(BF))
        grad_scores.append((prob * (pulled - weighted)).astype(BF))
    parts = [[], [], []]
    for prob, grad in zip(probs, grads):
        parts[2].append(nn(prob, grad))
    for score, half in zip(grad_scores, halves):
        parts[1].append(nn(score, half))
    for ((_, key_rows, _, _), segment), score in zip(chains, grad_scores):
        parts[0].append(join_heads(tn(score, key_rows[rows_of(segment)])) * HEAD_DIM**-0.5)
    results = []
    for index in range(len(jobs)):
        joined = []
        for part in parts:
            one, two, three = part[3 * index : 3 * index + 3]
            joined.append(
                jnp.concatenate(
                    [
                        one[:96],
                        one[96:] + two[:16],
                        two[16:96],
                        two[96:] + three[:16],
                        three[16:],
                    ],
                    axis=0,
                ).astype(BF)
            )
        results.append(joined)
    return results


def pairs_of(place, groups):
    core = place[2]
    return [2 * group + core for group in groups] + [2 * group + 1 - core for group in groups]


def lane_block(index):
    return pl.ds(pl.multiple_of(index * PW, PW), PW)


def heads_kernel(groups, place, mask, vec, source, own_w, other_w, *refs):
    if groups[0] == 0:
        mixed, heads, normed, weight = refs
        unit, _ = normalize(source[...].astype(F32))
        rows = (unit * vec[0:1, :].astype(F32) + vec[1:2, :].astype(F32)).astype(BF)
        normed[...] = rows
    else:
        mixed, heads, weight = refs
        rows = source[...]
    width = 3 * PW
    half = len(groups) * width

    @pl.when(pl.program_id(0) == 0)
    def _():
        weight[:, :half] = own_w[:, :half]
        weight[:, half:] = other_w[:, :half]

    product = nn(rows, weight[...])
    jobs, lanes = [], []
    for index, pair in enumerate(pairs_of(place, groups)):
        at = index * width
        block = lane_block(pair)
        query = (product[:, at : at + PW] + vec[2:3, block].astype(F32)).astype(BF)
        key_rows = product[:, at + PW : at + 2 * PW].astype(BF)
        value = (product[:, at + 2 * PW : at + width] + vec[3:4, block].astype(F32)).astype(BF)
        mixed[:, at : at + PW] = query
        mixed[:, at + PW : at + 2 * PW] = key_rows
        mixed[:, at + 2 * PW : at + width] = value
        for image in range(IMAGES):
            span = slice(image * PAD, (image + 1) * PAD)
            jobs.append((query[span], key_rows[span], value[span]))
            lanes.append((span, lane_block(pair - 2 * groups[0])))
    for (span, block), result in zip(lanes, attention(jobs, mask[...])):
        heads[span, block] = result


def heads_forward(groups, place, mask, vec, source, own_w, other_w):
    rows = source.shape[0]
    size = IMAGES * PAD
    width = 6 * PW * len(groups)
    wide = pl.BlockSpec((size, D), lambda i: (i, 0))
    weight = whole(own_w.shape)
    outs = [
        (pl.BlockSpec((size, width), lambda i: (i, 0)), jax.ShapeDtypeStruct((rows, width), BF)),
        (
            pl.BlockSpec((size, width // 3), lambda i: (i, 0)),
            jax.ShapeDtypeStruct((rows, width // 3), BF),
        ),
    ]
    if groups[0] == 0:
        outs.append((wide, jax.ShapeDtypeStruct((rows, D), BF)))
    return pl.pallas_call(
        functools.partial(heads_kernel, groups),
        grid=(rows // size,),
        in_specs=[SMEM, whole(mask.shape), whole((16, D)), wide, weight, weight],
        out_specs=tuple(out[0] for out in outs),
        out_shape=tuple(out[1] for out in outs),
        scratch_shapes=[pltpu.VMEM((D, width), BF)],
        compiler_params=params(32),
        cost_estimate=cost(2 * rows * D * width + rows * 1e5 * len(groups), 8 * rows * D),
        name=f"attention_{groups[0]}",
    )(place, mask, vec, source, own_w, other_w)


def heads_back_kernel(groups, steps, place, mask, grad_attended, normed, w_out, mixed, *refs):
    heads = refs[:-6] if len(refs) == 6 else refs[: -8]
    (grad_mixed, gw_own, gw_other, sums, kept_normed, kept_mixed) = refs[len(heads) :][:6]
    kept_heads, kept_grad = refs[len(heads) + 6 :] if heads else (None, None)
    step = pl.program_id(0)
    size = IMAGES * PAD
    width = 3 * PW
    half = len(groups) * width

    @pl.when(step == 0)
    def _():
        sums[...] = jnp.zeros_like(sums)

    @pl.when(step < steps)
    def _():
        rows = pl.ds(pl.multiple_of(step * size, 16), size)
        kept_normed[rows, :] = normed[...]
        incoming = grad_attended[...]
        if heads:
            kept_grad[rows, :] = incoming
            at = 0
            for part in heads:
                kept_heads[rows, at : at + part.shape[1]] = part[...]
                at += part.shape[1]
        jobs, places = [], []
        for index, pair in enumerate(pairs_of(place, groups)):
            at = index * width
            grad_heads = nt(incoming, w_out[lane_block(pair), :]).astype(BF)
            for image in range(IMAGES):
                span = slice(image * PAD, (image + 1) * PAD)
                jobs.append(
                    (
                        mixed[span, at : at + PW],
                        mixed[span, at + PW : at + 2 * PW],
                        mixed[span, at + 2 * PW : at + width],
                        grad_heads[span],
                    )
                )
                places.append((image, at))
        for (image, at), parts in zip(places, attention_back(jobs, mask[...])):
            for index, low in enumerate(parts):
                columns = slice(at + index * PW, at + (index + 1) * PW)
                grad_mixed[image * PAD : (image + 1) * PAD, columns] = low
                here = pl.ds(pl.multiple_of(step * size + image * PAD, 16), PAD)
                kept_mixed[here, columns] = low
                if index != 1:
                    sums[0:1, columns] += column_sum(low.astype(F32))

    @pl.when(step == steps)
    def _():
        first = 0
        if heads:
            first = D // 2
            core = place[2]
            own = pl.ds(pl.multiple_of(core * first, 128), first)
            other = pl.ds(pl.multiple_of((1 - core) * first, 128), first)
            gw_own[:, :first] = tn(kept_heads[...], kept_grad[:, own]).astype(BF)
            gw_other[:, :first] = tn(kept_heads[...], kept_grad[:, other]).astype(BF)
        gw_other[:, first:] = tn(kept_normed[...], kept_mixed[:, half:]).astype(BF)
        gw_own[:, first:] = tn(kept_normed[...], kept_mixed[:, :half]).astype(BF)


def heads_backward(groups, place, mask, grad_attended, normed, w_out, mixed, heads=()):
    rows, width = mixed.shape
    size = IMAGES * PAD
    steps = rows // size
    last = steps - 1

    def block(width):
        return pl.BlockSpec((size, width), lambda i: (jnp.minimum(i, last), 0))

    weight = (D, width // 2 + (D // 2 if heads else 0))
    kept = [D, width] + [D, D] * bool(heads)
    return pl.pallas_call(
        functools.partial(heads_back_kernel, groups, steps),
        grid=(steps + 1,),
        in_specs=[SMEM, whole(mask.shape), block(D), block(D)]
        + [pl.BlockSpec((D, D), lambda i: (0, w_out.shape[1] // D - 1)), block(width)]
        + [block(part.shape[1]) for part in heads],
        out_specs=(block(width), whole(weight), whole(weight), whole((8, width))),
        out_shape=(
            jax.ShapeDtypeStruct((rows, width), BF),
            jax.ShapeDtypeStruct(weight, BF),
            jax.ShapeDtypeStruct(weight, BF),
            jax.ShapeDtypeStruct((8, width), F32),
        ),
        scratch_shapes=[pltpu.VMEM((rows, lanes), BF) for lanes in kept],
        compiler_params=params(60 if heads else 40),
        cost_estimate=cost(
            2 * rows * D * (width // 3 + width) + rows * 3e5 * len(groups), 12 * rows * D
        ),
        name=f"attention_back_{groups[0]}",
    )(place, mask, grad_attended, normed, w_out, mixed, *heads)


TILE = 256


def gelu_and_slope(values):
    below = 0.5 + 0.5 * lax.erf(values * math.sqrt(0.5))
    bell = jnp.exp(-0.5 * values * values) * (1.0 / math.sqrt(2.0 * math.pi))
    return values * below, below + values * bell


def both_ways(chunk, bias, weights, left, right, rows, kept_active, kept_before, sums):
    tiles = D // TILE
    for half in range(2):
        up, down = weights[2 * half], weights[2 * half + 1]
        for tile in range(tiles):
            columns = slice(tile * TILE, (tile + 1) * TILE)
            kept = slice(half * D + tile * TILE, half * D + (tile + 1) * TILE)
            before = nn(left, up[:, columns]) + bias[2 * chunk + half, :, columns]
            active, slope = gelu_and_slope(before)
            kept_active[rows, kept] = active.astype(BF)
            low = (nt(right, down[columns, :]) * slope).astype(BF)
            kept_before[rows, kept] = low
            sums[half, :, columns] += column_sum(low.astype(F32))
    result = nn(kept_active[rows, :D], weights[1][...])
    result += nn(kept_active[rows, D:], weights[3][...])
    pulled = nt(kept_before[rows, :D], weights[0][...])
    pulled += nt(kept_before[rows, D:], weights[2][...])
    return result, pulled


def hidden_grads(tile, blocks, kept, gw):
    kept_normed, kept_grad, kept_active, kept_before = kept

    def ordered(value):
        if blocks:
            value = jnp.concatenate([value[at : at + size] for at, size in blocks], axis=0)
        return value.astype(BF)

    for half in range(2):
        columns = slice(half * D, (half + 1) * D)

        @pl.when(tile == 2 * half)
        def _():
            gw[...] = ordered(tn(kept_normed[...], kept_before[:, columns]))

        @pl.when(tile == 2 * half + 1)
        def _():
            gw[...] = ordered(tn(kept_active[:, columns], kept_grad[...]))


def routed_rows(picked, grads, vec):
    inputs = picked[...].astype(F32)
    grad_rows = grads[...].astype(F32)
    routed = jnp.sum(inputs * vec[8:9, :].astype(F32), axis=-1, keepdims=True)
    return inputs, grad_rows, routed, routed * grad_rows


def first_mlp_kernel(steps, size, blocks, bias, vec, w_out, picked, grads, *refs):
    heads = refs[: len(SETS)]
    refs = refs[len(SETS) :]
    weights = refs[:4]
    attended, normed, out, back, gw, sums = refs[4:10]
    kept = refs[10:]
    kept_normed, kept_grad, kept_active, kept_before = kept
    step = pl.program_id(0)

    @pl.when(step == 0)
    def _():
        sums[...] = jnp.zeros_like(sums)

    @pl.when(step < steps)
    def _():
        rows = pl.ds(pl.multiple_of(step * size, 16), size)
        inputs, _, _, grad_branch = routed_rows(picked, grads, vec)
        right = grad_branch.astype(BF)
        joined = jnp.concatenate([part[...] for part in heads], axis=1)
        mixed = nn(joined, w_out[...]) + vec[4:5, :].astype(F32)
        attended[...] = mixed
        unit, _ = normalize(inputs + mixed)
        left = (unit * vec[5:6, :].astype(F32) + vec[6:7, :].astype(F32)).astype(BF)
        normed[...] = left
        kept_normed[rows, :] = left
        kept_grad[rows, :] = right
        out[...], back[...] = both_ways(
            0, bias, weights, left, right, rows, kept_active, kept_before, sums
        )

    @pl.when(step >= steps)
    def _():
        hidden_grads(step - steps, blocks, kept, gw)


def second_mlp_kernel(
    steps, size, blocks, place, bias, vec, picked, grads, normed, attended, out, back, *refs
):
    weights = refs[:4]
    (grad_attended, carry, values, turn_sums, sums, gw) = refs[4:10]
    kept = refs[10:]
    kept_normed, kept_grad, kept_active, kept_before = kept
    step = pl.program_id(0)

    @pl.when(step == 0)
    def _():
        sums[...] = jnp.zeros_like(sums)
        turn_sums[...] = jnp.zeros_like(turn_sums)

    @pl.when(step < steps)
    def _():
        rows = pl.ds(pl.multiple_of(step * size, 16), size)
        inputs, grad_rows, routed, grad_branch = routed_rows(picked, grads, vec)
        left = normed[...]
        right = grad_branch.astype(BF)
        kept_normed[rows, :] = left
        kept_grad[rows, :] = right
        result, pulled = both_ways(
            1, bias, weights, left, right, rows, kept_active, kept_before, sums
        )
        pulled += back[...]
        router = vec[8:9, :].astype(F32)
        mixed = attended[...]
        branch = mixed + (result + out[...]) + vec[7:8, :].astype(F32)
        values[...] = (inputs + routed * branch).astype(BF)
        grad_routed = jnp.sum(grad_rows * branch, axis=-1, keepdims=True)
        unit, inverse = normalize(inputs + mixed)
        residual = norm_back(pulled, unit, inverse, vec[5:6, :].astype(F32))
        low = (grad_branch + residual).astype(BF)
        grad_attended[...] = low
        carry[...] = residual + grad_routed * router
        turn_sums[0:1, :] += column_sum(low.astype(F32))
        turn_sums[1:2, :] += column_sum(pulled * unit)
        turn_sums[2:3, :] += column_sum(pulled)
        turn_sums[3:4, :] += column_sum(right.astype(F32))
        turn_sums[4:5, :] += column_sum(inputs * grad_routed)

    @pl.when(step >= steps)
    def _():
        hidden_grads(step - steps, blocks, kept, gw)


def mlp_specs(chunk, rows):
    size = PAD
    steps = rows // size
    last = steps - 1

    def wide(width=D):
        return pl.BlockSpec((size, width), lambda i: (jnp.minimum(i, last), 0))

    weights = [
        pl.BlockSpec((D, D), lambda i, at=at: (0, at), pipeline_mode=pl.Buffered(1))
        for at in (0, 2, 1, 3)
    ]

    def gw_block(i):
        tile = jnp.clip(i - steps, 0, 3)
        return (0, tile // 2 + 2 * (tile % 2))

    scratch = [
        pltpu.VMEM((rows, D), BF),
        pltpu.VMEM((rows, D), BF),
        pltpu.VMEM((rows, 2 * D), BF),
        pltpu.VMEM((rows, 2 * D), BF),
    ]
    return size, steps, 4, wide, weights, pl.BlockSpec((D, D), gw_block), scratch


def first_mlp(blocks, bias, vec, picked, grads, heads, weights):
    rows = picked.shape[0]
    size, steps, tiles, wide, weight_specs, gw, scratch = mlp_specs(0, rows)
    total = jax.ShapeDtypeStruct((rows, D), F32)
    return pl.pallas_call(
        functools.partial(first_mlp_kernel, steps, size, blocks),
        grid=(steps + tiles,),
        in_specs=[whole(bias.shape), whole((16, D))]
        + [pl.BlockSpec((D, D), lambda i: (0, 4), pipeline_mode=pl.Buffered(1))]
        + [wide()] * 2
        + [wide(part.shape[1]) for part in heads]
        + weight_specs,
        out_specs=(wide(),) * 4 + (gw, whole((2, 1, D))),
        out_shape=(
            total,
            jax.ShapeDtypeStruct((rows, D), BF),
            total,
            total,
            jax.ShapeDtypeStruct((D, 4 * D), BF),
            jax.ShapeDtypeStruct((2, 1, D), F32),
        ),
        scratch_shapes=scratch,
        compiler_params=params(),
        cost_estimate=cost(26 * rows * D * D, 30 * rows * D, 4 * rows * D),
        name="feed_forward_0",
    )(bias, vec, weights, picked, grads, *heads, *[weights] * 4)


def second_mlp(blocks, place, bias, vec, picked, grads, normed, attended, out, back, weights):
    rows = picked.shape[0]
    size, steps, tiles, wide, weight_specs, gw, scratch = mlp_specs(1, rows)
    low = jax.ShapeDtypeStruct((rows, D), BF)
    return pl.pallas_call(
        functools.partial(second_mlp_kernel, steps, size, blocks),
        grid=(steps + tiles,),
        in_specs=[SMEM, whole(bias.shape), whole((16, D))]
        + [wide()] * 6
        + weight_specs,
        out_specs=(wide(), wide(), wide(), whole((8, D)), whole((2, 1, D)), gw),
        out_shape=(
            low,
            jax.ShapeDtypeStruct((rows, D), F32),
            low,
            jax.ShapeDtypeStruct((8, D), F32),
            jax.ShapeDtypeStruct((2, 1, D), F32),
            jax.ShapeDtypeStruct((D, 4 * D), BF),
        ),
        scratch_shapes=scratch,
        compiler_params=params(),
        cost_estimate=cost(26 * rows * D * D, 40 * rows * D, 4 * rows * D),
        name="feed_forward_1",
    )(place, bias, vec, picked, grads, normed, attended, out, back, *[weights] * 4)


def first_back_kernel(count, vec, picked, grads, carry, *refs):
    mixed = refs[:count]
    weights = refs[count : 3 * count]
    values, sums = refs[3 * count : 3 * count + 2]
    kept = refs[3 * count + 2 :]

    @pl.when(pl.program_id(0) == 0)
    def _():
        sums[...] = jnp.zeros_like(sums)
        for index in range(count):
            half = mixed[index].shape[1] // 2
            kept[index][:, :half] = weights[2 * index][:, :half]
            kept[index][:, half:] = weights[2 * index + 1][:, :half]

    pulled = nt(mixed[0][...], kept[0][...])
    for index in range(1, count):
        pulled += nt(mixed[index][...], kept[index][...])
    unit, inverse = normalize(picked[...].astype(F32))
    grad = norm_back(pulled, unit, inverse, vec[0:1, :].astype(F32))
    values[...] = (grads[...].astype(F32) + grad + carry[...]).astype(BF)
    sums[0:1, :] += column_sum(pulled * unit)
    sums[1:2, :] += column_sum(pulled)


def first_back(vec, picked, grads, carry, mixed, weights):
    rows = picked.shape[0]
    size = 2 * PAD
    wide = pl.BlockSpec((size, D), lambda i: (i, 0))
    flat = [weight for pair in weights for weight in pair]
    return pl.pallas_call(
        functools.partial(first_back_kernel, len(mixed)),
        grid=(rows // size,),
        in_specs=[whole((16, D)), wide, wide, wide]
        + [pl.BlockSpec((size, part.shape[1]), lambda i: (i, 0)) for part in mixed]
        + [whole(weight.shape) for weight in flat],
        out_specs=(wide, whole((8, D))),
        out_shape=(jax.ShapeDtypeStruct((rows, D), BF), jax.ShapeDtypeStruct((8, D), F32)),
        scratch_shapes=[pltpu.VMEM((D, part.shape[1]), BF) for part in mixed],
        compiler_params=params(44),
        cost_estimate=cost(6 * rows * D * D, 16 * rows * D),
        name="first_norm_back",
    )(vec, picked, grads, carry, *mixed, *flat)


def put_kernel(span, places, source, value, after, out, both):
    width = places.shape[2]
    for image in range(IMAGES):
        rows = slice(image * span, (image + 1) * span)
        both[:PAD, :] = value[image * PAD : (image + 1) * PAD, :]
        if image + 1 < IMAGES:
            both[PAD:, :] = value[(image + 1) * PAD : (image + 1) * PAD + 16, :]
        else:
            both[PAD:, :] = after[...]
        same = lax.broadcasted_iota(jnp.int32, (span, width), 0) == places[image]
        hot = same.astype(F32)
        kept = jnp.max(hot, axis=-1, keepdims=True) > 0.5
        moved = nn(hot.astype(BF), both[...])
        out[rows, :] = jnp.where(kept, moved, source[rows, :].astype(F32)).astype(BF)


def put(places, source, values):
    rows = source.shape[0]
    count = places.shape[0]
    span = -(-(rows // count) // 16) * 16
    steps = count // IMAGES
    block = pl.BlockSpec((IMAGES * span, D), lambda i: (i, 0))
    return pl.pallas_call(
        functools.partial(put_kernel, span),
        grid=(steps,),
        in_specs=[
            pl.BlockSpec((IMAGES, 1, places.shape[2]), lambda i: (i, 0, 0)),
            block,
            pl.BlockSpec((IMAGES * PAD, D), lambda i: (i, 0)),
            pl.BlockSpec(
                (16, D), lambda i: (jnp.minimum(i + 1, steps - 1) * (IMAGES * PAD // 16), 0)
            ),
        ],
        out_specs=block,
        out_shape=jax.ShapeDtypeStruct((rows, D), BF),
        scratch_shapes=[pltpu.VMEM((PAD + 16, D), BF)],
        compiler_params=params(24),
        cost_estimate=cost(2 * rows * D * (PAD + 16), 6 * rows * D),
        name="put_rows",
    )(places, source, values, values)


def put_places(keep_slots, image_tokens):
    count = keep_slots.shape[0]
    span = -(-image_tokens // 16) * 16
    image = jnp.arange(count, dtype=jnp.int32)[:, None]
    own = keep_slots + image * (image_tokens - span)
    following = jnp.concatenate([keep_slots[1:, :16], jnp.full((1, 16), -span, jnp.int32)], axis=0)
    following = following + (image + 1) * image_tokens - image * span
    following = jnp.where(image < count - 1, following, -1)
    gap = jnp.full((count, PAD - KEEP), -1, jnp.int32)
    return jnp.concatenate([own, gap, following], axis=1)[:, None, :]


class Moves:
    def __init__(self, n_dp, n_fsdp):
        self.n_dp = n_dp
        self.n_fsdp = n_fsdp
        self.squares = n_fsdp // 2
        outer = lax.axis_index("dp")
        inner = lax.axis_index("fsdp")
        self.z = outer
        self.yx = inner // 2
        self.core = inner % 2
        self.place = jnp.stack([self.z, self.yx, self.core]).astype(jnp.int32)

    def swap(self, value, mask):
        total = self.n_dp * self.n_fsdp
        return lax.ppermute(value, AXES, [(i, i ^ mask) for i in range(total)])

    def over_z(self, values):
        return [values[0]] + [self.swap(values[k], k * self.n_fsdp) for k in range(1, self.n_dp)]

    def over_yx(self, values):
        return [values[0]] + [self.swap(values[k], 2 * k) for k in range(1, self.squares)]

    def over_core(self, value):
        return self.swap(value, 1)

    def square_blocks(self, size):
        return [
            ((z * self.n_fsdp + inner) * size, size)
            for inner in range(self.n_fsdp)
            for z in range(self.n_dp)
        ]

    def over_square(self, value, ordered):
        rows, n = value.shape
        if not ordered:
            value = value.reshape(self.n_dp, self.n_fsdp, -1, n).transpose(1, 0, 2, 3)
        value = value.reshape(rows, n)
        return lax.psum_scatter(value, "fsdp", scatter_dimension=0, tiled=True)

    def by_chip(self, value):
        chips = self.n_dp * self.squares
        return value.reshape(self.n_dp, self.squares, value.shape[0] // chips, value.shape[1])

    def add_cores(self, place, keeps, arrived):
        keeps = [self.by_chip(value) for value in keeps]
        arrived = [self.by_chip(value) for value in arrived]
        return add_pairs(place, keeps, arrived, self.squares)


def add_parts(parts):
    total = parts[0].astype(F32)
    for part in parts[1:]:
        total = total + part.astype(F32)
    return total


def together(*values):
    return lax.optimization_barrier(values)


def after(value, *others):
    return lax.optimization_barrier((value, *others))[0]


def place_kernel(axis, count, cuts, place, *refs):
    outs = refs[count:]
    me = place[axis]
    for k in range(count):
        for (first, width), out in zip(cuts, outs):
            if axis == 0:
                out[me ^ k] = refs[k][:, first : first + width]
            else:
                out[:, me ^ k] = refs[k][...]


def place_blocks(place, axis, blocks, widths):
    count = len(blocks)
    cuts, at = [], 0
    for width in widths:
        cuts.append((at, width))
        at += width
    shape = blocks[0].shape[:-1]
    shape = shape[:axis] + (count,) + shape[axis:]
    vmem = pl.BlockSpec(memory_space=pltpu.VMEM)
    return pl.pallas_call(
        functools.partial(place_kernel, axis, count, cuts),
        in_specs=[SMEM] + [vmem] * count,
        out_specs=[vmem] * len(widths),
        out_shape=[jax.ShapeDtypeStruct(shape + (width,), BF) for width in widths],
        compiler_params=params(24),
        cost_estimate=cost(0, 4 * math.prod(shape) * at),
        name="place_blocks",
    )(place, *blocks)


def add_pairs_kernel(parts, squares, place, *refs):
    outs = refs[2 * parts * squares :]
    at = 0
    for part in range(parts):
        for k in range(squares):
            index = part * squares + k
            left, right = refs[index], refs[parts * squares + index]
            width = left.shape[3]
            total = left[...].astype(F32) + right[...].astype(F32)
            outs[k][:, :, at : at + width] = total[:, 0].astype(BF)
        at += width


def add_pairs(place, keeps, arrived, squares):
    specs, left, right = [], [], []
    n_dp, _, m, _ = keeps[0].shape
    for keep, other in zip(keeps, arrived):
        for k in range(squares):
            specs.append(
                pl.BlockSpec(
                    (n_dp, 1, m, keep.shape[3]), lambda i, place, k=k: (0, place[1] ^ k, 0, 0)
                )
            )
            left.append(keep)
            right.append(other)
    shape = (n_dp, m, sum(keep.shape[3] for keep in keeps))
    return pl.pallas_call(
        functools.partial(add_pairs_kernel, len(keeps), squares),
        grid_spec=pltpu.PrefetchScalarGridSpec(
            num_scalar_prefetch=1,
            grid=(1,),
            in_specs=specs + specs,
            out_specs=[pl.BlockSpec(shape, lambda i, place: (0, 0, 0))] * squares,
        ),
        out_shape=[jax.ShapeDtypeStruct(shape, BF)] * squares,
        compiler_params=params(24),
        cost_estimate=cost(0, 6 * squares * math.prod(shape)),
        name="add_cores",
    )(place, *left, *right)


def add_blocks_kernel(count, rows, sizes, place, *refs):
    outs = refs[count * sum(sizes) :]
    at = 0
    for index in range(count):
        lane = 0
        for terms in sizes:
            total = refs[at][0].astype(F32)
            for term in range(1, terms):
                total = total + refs[at + term][0].astype(F32)
            at += terms
            for first in range(0, total.shape[0], rows):
                width = total.shape[1]
                outs[index][:, lane : lane + width] = total[first : first + rows].astype(BF)
                lane += width


def add_blocks(place, groups, n_dp, rows):
    specs, operands, lanes = [], [], 0
    for arrays in groups:
        _, m, n = arrays[0].shape
        lanes += n * (m // rows)
    for k in range(n_dp):
        for arrays in groups:
            _, m, n = arrays[0].shape
            spec = pl.BlockSpec((1, m, n), lambda i, place, k=k: (place[0] ^ k, 0, 0))
            specs += [spec] * len(arrays)
            operands += arrays
    sizes = [len(arrays) for arrays in groups]
    return pl.pallas_call(
        functools.partial(add_blocks_kernel, n_dp, rows, sizes),
        grid_spec=pltpu.PrefetchScalarGridSpec(
            num_scalar_prefetch=1,
            grid=(1,),
            in_specs=specs,
            out_specs=[pl.BlockSpec((rows, lanes), lambda i, place: (0, 0))] * n_dp,
        ),
        out_shape=[jax.ShapeDtypeStruct((rows, lanes), BF)] * n_dp,
        compiler_params=params(24),
        cost_estimate=cost(0, 4 * n_dp * rows * lanes * max(sizes)),
        name="add_squares",
    )(place, *operands)


def planes_kernel(count, place, *refs):
    rows = refs[0].shape[1]
    out = refs[-1]
    lane = 0
    for ref in refs[:count]:
        out[0, :, lane : lane + ref.shape[2]] = ref[0]
        lane += ref.shape[2]
    total = refs[count][0].astype(F32)
    for ref in refs[count + 1 : -1]:
        total = total + ref[0].astype(F32)
    width = total.shape[1]
    for first in range(0, total.shape[0], rows):
        out[0, :, lane : lane + width] = total[first : first + rows].astype(BF)
        lane += width


def planes(place, ready, parts):
    n_dp, rows, _ = ready[0].shape
    arrays = ready + parts
    lanes = sum(value.shape[2] for value in ready) + parts[0].shape[1] // rows * parts[0].shape[2]
    return pl.pallas_call(
        functools.partial(planes_kernel, len(ready)),
        grid=(n_dp,),
        in_specs=[SMEM] + [pl.BlockSpec((1,) + a.shape[1:], lambda i: (i, 0, 0)) for a in arrays],
        out_specs=pl.BlockSpec((1, rows, lanes), lambda i: (i, 0, 0)),
        out_shape=jax.ShapeDtypeStruct((n_dp, rows, lanes), BF),
        compiler_params=params(),
        cost_estimate=cost(0, 4 * n_dp * rows * lanes),
        name="planes",
    )(place, *arrays)


def quarters_kernel(total, part, up, down, project_out, *outs):
    outs[0][:, 4 * D :] = project_out[...].astype(BF)
    for chunk, out in enumerate(outs):
        for half in range(2):
            quarter = 2 * chunk + half
            pieces = [
                up[:, (owner * QUARTERS + quarter) * part : (owner * QUARTERS + quarter + 1) * part]
                for owner in range(total)
            ]
            out[:, half * D : (half + 1) * D] = jnp.concatenate(pieces, axis=1).astype(BF)
            rows = slice(quarter * part, (quarter + 1) * part)
            out[:, (2 + half) * D : (3 + half) * D] = down[rows, :].astype(BF)


def to_quarters(total, up, down, project_out):
    rows = up.shape[0]
    part = down.shape[0] // QUARTERS
    shape = jax.ShapeDtypeStruct((rows, 4 * D), BF)
    if part % 8:
        ups = up.astype(BF).reshape(rows, total, QUARTERS, part).transpose(2, 0, 1, 3)
        ups = ups.reshape(QUARTERS, rows, D)
        downs = down.astype(BF).reshape(QUARTERS, part, D)
        first = [ups[0], ups[1], downs[0], downs[1], project_out.astype(BF)]
        second = [ups[2], ups[3], downs[2], downs[3]]
        return [jnp.concatenate(first, axis=1), jnp.concatenate(second, axis=1)]
    vmem = pl.BlockSpec(memory_space=pltpu.VMEM)
    return pl.pallas_call(
        functools.partial(quarters_kernel, total, part),
        in_specs=[vmem] * 3,
        out_specs=[vmem] * 2,
        out_shape=[jax.ShapeDtypeStruct((rows, 5 * D), BF), shape],
        compiler_params=params(),
        cost_estimate=cost(0, 12 * rows * 4 * D),
        name="to_quarters",
    )(up, down, project_out)


def hidden_kernel(total, part, value, up, down):
    pieces = []
    for owner in range(total):
        for quarter in range(QUARTERS):
            at = (4 * (quarter // 2) + quarter % 2) * D + owner * part
            pieces.append(value[:, at : at + part].astype(F32))
    up[...] = jnp.concatenate(pieces, axis=1)
    for quarter in range(QUARTERS):
        at = (4 * (quarter // 2) + 2 + quarter % 2) * D
        down[quarter * part : (quarter + 1) * part, :] = value[:, at : at + D].astype(F32)


def from_quarters(total, value):
    rows = value.shape[0]
    part = D // total
    if part % 8:
        quarters = value[:, : 8 * D].astype(F32).reshape(rows, CHUNKS, 2, 2, D)
        ups = quarters[:, :, 0].reshape(rows, QUARTERS, total, part).transpose(0, 2, 1, 3)
        downs = quarters[:, :, 1].reshape(rows, QUARTERS, D).transpose(1, 0, 2)
        return ups.reshape(rows, HIDDEN), downs.reshape(QUARTERS * part, D)
    vmem = pl.BlockSpec(memory_space=pltpu.VMEM)
    return pl.pallas_call(
        functools.partial(hidden_kernel, total, part),
        in_specs=[vmem],
        out_specs=[vmem] * 2,
        out_shape=[
            jax.ShapeDtypeStruct((rows, HIDDEN), F32),
            jax.ShapeDtypeStruct((QUARTERS * part, D), F32),
        ],
        compiler_params=params(16),
        cost_estimate=cost(0, 6 * rows * 8 * D),
        name="from_quarters",
    )(value)


def unit_pieces(total):
    part = D // total
    for quarter in range(QUARTERS):
        for owner in range(total):
            first = (owner * QUARTERS + quarter) * part
            yield quarter, owner * part, first // D, first % D


def vectors_kernel(total, source, vec, bias):
    rows = source[...].astype(F32).T[:16, :]
    vec[...] = rows.astype(BF)
    part = D // total
    pieces = [[] for _ in range(QUARTERS)]
    for quarter, _, row, lane in unit_pieces(total):
        pieces[quarter].append(rows[9 + row : 10 + row, lane : lane + part])
    for quarter in range(QUARTERS):
        bias[quarter] = jnp.concatenate(pieces[quarter], axis=1)


def vectors_of(total, gathered):
    if D // total % 8:
        vec = gathered[:, -128:-112].T
        bias = vec[9:13].astype(F32).reshape(total, QUARTERS, -1).transpose(1, 0, 2)
        return vec, bias.reshape(QUARTERS, 1, D)
    return pl.pallas_call(
        functools.partial(vectors_kernel, total),
        grid=(1,),
        in_specs=[pl.BlockSpec((D, 128), lambda i: (0, gathered.shape[1] // 128 - 1))],
        out_specs=[whole((16, D)), whole((QUARTERS, 1, D))],
        out_shape=[
            jax.ShapeDtypeStruct((16, D), BF),
            jax.ShapeDtypeStruct((QUARTERS, 1, D), F32),
        ],
        compiler_params=params(16),
        cost_estimate=cost(0, 4 * D * 128),
        name="vectors",
    )(gathered)


def pair_sums(core, sums, groups, part):
    width = 3 * PW
    half = len(groups) * width
    pieces = []
    for index in range(len(groups)):
        at = index * width + part * PW
        own = sums[0:1, at : at + PW]
        other = sums[0:1, half + at : half + at + PW]
        pieces += [jnp.where(core == 0, own, other), jnp.where(core == 0, other, own)]
    return pieces


def table_kernel(total, place, *refs):
    (first, sums_a, sums_b, turn, sums_0, sums_1, summed) = refs[:7]
    parts, (table, mine, send) = refs[7:-3], refs[-3:]
    core = place[2]
    table[...] = jnp.zeros_like(table)
    table[0:2, :] = first[0:2, :]
    for row, part in ((2, 0), (3, 2)):
        pieces = pair_sums(core, sums_a, SETS[0], part) + pair_sums(core, sums_b, SETS[1], part)
        table[row : row + 1, :] = jnp.concatenate(pieces, axis=1)
    table[4:9, :] = turn[0:5, :]
    size = D // total
    pieces = sorted((row, lane, quarter, at) for quarter, at, row, lane in unit_pieces(total))
    for row in range(4):
        values = []
        for _, _, quarter, at in pieces[row * len(pieces) // 4 : (row + 1) * len(pieces) // 4]:
            source = sums_1 if quarter // 2 else sums_0
            values.append(source[quarter % 2][:, at : at + size])
        table[9 + row : 10 + row, :] = jnp.concatenate(values, axis=1)
    last = parts[0][...].astype(F32)
    for part in parts[1:]:
        last = last + part[...].astype(F32)
    hidden = 8 * D
    half = (summed.shape[1] - hidden) // 2
    squares = jnp.sum(last * last, keepdims=True)
    for at in range(0, summed.shape[1], 2 * D):
        piece = summed[:, at : min(at + 2 * D, summed.shape[1])].astype(F32)
        squares = squares + jnp.sum(piece * piece, keepdims=True)
    table[13:14, :] = jnp.broadcast_to(squares, (1, D))
    later = summed[:, hidden:].astype(F32)
    for at, value in ((0, later), (half, last)):
        width = value.shape[1] // 2
        one, two = value[:, :width], value[:, width:]
        mine[:, at : at + width] = jnp.where(core == 0, one, two)
        send[:, at : at + width] = jnp.where(core == 0, two, one)


def make_table(total, place, first, sums_a, sums_b, turn, sums_0, sums_1, summed, parts):
    rows = summed.shape[0]
    lanes = (summed.shape[1] - 8 * D + parts[0].shape[1]) // 2
    vmem = pl.BlockSpec(memory_space=pltpu.VMEM)
    half = jax.ShapeDtypeStruct((rows, lanes), F32)
    return pl.pallas_call(
        functools.partial(table_kernel, total),
        in_specs=[SMEM] + [vmem] * (7 + len(parts)),
        out_specs=[vmem] * 3,
        out_shape=[jax.ShapeDtypeStruct((16, D), F32), half, half],
        compiler_params=params(),
        cost_estimate=cost(0, 20 * rows * lanes),
        name="table",
    )(place, first, sums_a, sums_b, turn, sums_0, sums_1, summed, *parts)


def whole_rows(core, mine, theirs):
    ordered = (
        jnp.where(core == 0, mine[...], theirs[...]),
        jnp.where(core == 0, theirs[...], mine[...]),
    )
    half = D // 2
    outs = jnp.concatenate([value[:, :half] for value in ordered], axis=1)
    pieces = []
    for part in range(3):
        at = half
        for groups in SETS:
            for index in range(len(groups)):
                lane = at + (3 * index + part) * PW
                pieces += [value[:, lane : lane + PW] for value in ordered]
            at += 3 * PW * len(groups)
    return jnp.concatenate(pieces, axis=1), outs


def adam_kernel(place, table, mine, theirs, up, down, own, *refs):
    kinds = 5
    masters, firsts, seconds = (refs[i * kinds : (i + 1) * kinds] for i in range(3))
    outs = refs[3 * kinds :]
    grads = whole_rows(place[2], mine, theirs) + (up[...], down[...], own[...])
    vector_rows = masters[4].shape[0]
    vectors = table[:vector_rows, :]
    squares = jnp.sum(vectors * vectors, keepdims=True) + table[vector_rows : vector_rows + 1, :1]
    grad_norm = jnp.sqrt(squares)
    factor = jnp.minimum(1.0, clip_share * math.sqrt(PARAMS) / (grad_norm + 1e-06))
    outs[0][...] = grad_norm
    for kind in range(kinds):
        rate = vector_rate if kind == 4 else matrix_rate
        decay = 0.0 if kind == 4 else matrix_decay
        master = masters[kind][...]
        grad = grads[kind] * factor
        first_new = first_beta * firsts[kind][...] + (1.0 - first_beta) * grad
        second_new = second_beta * seconds[kind][...] + (1.0 - second_beta) * grad * grad
        first_hat = first_new * (1.0 / (1.0 - first_beta**STEP))
        second_hat = second_new * (1.0 / (1.0 - second_beta**STEP))
        step = first_hat / (jnp.sqrt(second_hat) + adam_eps)
        updated = master - rate * (step + decay * master)
        outs[1 + kind][...] = first_new
        outs[1 + kinds + kind][...] = second_new
        outs[1 + 2 * kinds + kind][...] = updated
        outs[1 + 3 * kinds + kind][...] = updated.astype(BF)


def adam(place, table, mine, theirs, up, down, own, masters, firsts, seconds):
    vmem = pl.BlockSpec(memory_space=pltpu.VMEM)
    shapes = [master.shape for master in masters]
    states = [jax.ShapeDtypeStruct(shape, F32) for shape in shapes]
    outs = [jax.ShapeDtypeStruct((1, 1), F32)] + states * 3
    outs += [jax.ShapeDtypeStruct(shape, BF) for shape in shapes]
    elements = sum(math.prod(shape) for shape in shapes)
    return pl.pallas_call(
        adam_kernel,
        in_specs=[SMEM] + [vmem] * 21,
        out_specs=[vmem] * len(outs),
        out_shape=outs,
        compiler_params=params(),
        cost_estimate=cost(20 * elements, 30 * elements),
        name="adam",
    )(place, table, mine, theirs, up, down, own, *masters, *firsts, *seconds)


def on_device(
    n_dp,
    n_fsdp,
    tokens,
    keep_slots,
    cotangent,
    project_in,
    project_out,
    expand,
    contract,
    vectors,
    first_in,
    first_out,
    first_expand,
    first_contract,
    first_vectors,
    second_in,
    second_out,
    second_expand,
    second_contract,
    second_vectors,
):
    moves = Moves(n_dp, n_fsdp)
    place, core = moves.place, moves.core
    total = n_dp * n_fsdp
    rows_in = project_in.shape[0]
    part = contract.shape[0] // QUARTERS
    owner = moves.z * n_fsdp + lax.axis_index("fsdp")
    columns = vectors.shape[1]

    shards = to_quarters(total, expand, contract, project_out)
    w_hidden = [lax.all_gather(shards[0], AXES, axis=0, tiled=True)]

    def pair_columns(value, pair):
        return [value[:, at * D + pair * PW : at * D + (pair + 1) * PW] for at in range(3)]

    low_in = project_in.astype(BF)
    low_vec = jnp.pad(vectors.astype(BF).T, ((0, 0), (0, 128 - vectors.shape[0])))
    halves = []
    for parity in range(2):
        parts = []
        for index, groups in enumerate(SETS):
            for group in groups:
                parts += pair_columns(low_in, 2 * group + parity)
            if index == 0:
                parts.append(low_vec)
        halves.append(jnp.concatenate(parts, axis=1))
    mine = jnp.where(core == 0, halves[0], halves[1])
    theirs = jnp.where(core == 0, halves[1], halves[0])
    arrived = moves.over_core(theirs)
    rows = jnp.where(
        core == 0,
        jnp.concatenate([mine, arrived], axis=0),
        jnp.concatenate([arrived, mine], axis=0),
    )
    step = 3 * PW
    cut = len(SETS[0]) * step + 128
    widths = (cut, rows.shape[1] - cut)

    count = keep_slots.shape[0]
    image_tokens = tokens.shape[0] // count
    slots = jnp.pad(keep_slots, ((0, 0), (0, PAD - KEEP)), constant_values=-4 * image_tokens)
    slots = slots[:, :, None]
    parts = moves.over_z([rows] * n_dp)
    picked = pick(place, tokens, slots)
    picked, *parts = together(picked, *parts)
    first_stack, second_stack = place_blocks(place, 0, parts, widths)
    parts = moves.over_yx([first_stack] * moves.squares)
    (first_own,) = place_blocks(place, 1, parts, widths[:1])
    first_own = first_own.reshape(D, widths[0])
    first_other = moves.over_core(first_own)
    vec, bias = vectors_of(total, first_own)

    mask = local_mask()
    first_own, first_other, second_stack = together(first_own, first_other, second_stack)
    parts = moves.over_yx([second_stack] * moves.squares)
    mixed_0, heads_0, normed_one = heads_forward(
        SETS[0], place, mask, vec, picked, first_own, first_other
    )
    grad_rows = pick(after(place, heads_0), cotangent, slots)
    mixed_0, heads_0, normed_one, grad_rows, *parts = together(
        mixed_0, heads_0, normed_one, grad_rows, *parts
    )
    (second_own,) = place_blocks(place, 1, parts, widths[1:])
    second_own = second_own.reshape(D, widths[1])
    second_other = moves.over_core(second_own)
    w_in = [(first_own, first_other), (second_own, second_other)]
    shard = after(shards[1], second_own)
    parts = moves.over_z([shard] * n_dp)
    mixed_1, heads_1 = heads_forward(SETS[1], place, mask, vec, normed_one, *w_in[1])
    mixed_1, heads_1, *parts = together(mixed_1, heads_1, *parts)
    (stack,) = place_blocks(place, 0, parts, [shard.shape[1]])
    gathered = lax.all_gather(stack, "fsdp", axis=1, tiled=True)
    w_hidden.append(gathered.reshape(D, shard.shape[1]))
    heads = [heads_0, heads_1]

    blocks = moves.square_blocks(rows_in) if rows_in % 8 == 0 else []
    attended, normed_two, out, back, gw_0, sums_0 = first_mlp(
        blocks, bias, vec, picked, grad_rows, heads, w_hidden[0]
    )
    hidden_0 = moves.over_square(gw_0, blocks)
    (
        grad_attended,
        carry,
        put_values,
        turn_sums,
        sums_1,
        gw_1,
    ) = second_mlp(
        blocks,
        place,
        bias,
        vec,
        picked,
        grad_rows,
        normed_two,
        attended,
        out,
        back,
        w_hidden[1],
    )
    hidden_1 = moves.over_square(gw_1, blocks)
    places = put_places(keep_slots, image_tokens)

    results = heads_backward(
        SETS[0], place, mask, grad_attended, normed_one, w_hidden[0], mixed_0, heads
    )
    gm_0, gw_own, gw_other, sums_a, hidden_0 = together(*results, hidden_0)
    blocks = moves.add_cores(place, [gw_own], [moves.over_core(gw_other)])
    later = moves.over_yx(blocks)
    results = heads_backward(
        SETS[1], after(place, *blocks), mask, grad_attended, normed_one, w_hidden[0], mixed_1
    )
    gm_1, gw_own, gw_other, sums_b, *later = together(*results, *later)
    blocks = moves.add_cores(place, [gw_own], [moves.over_core(gw_other)])
    last = moves.over_yx(blocks)
    hidden = [value.reshape(n_dp, rows_in, -1) for value in (hidden_0, hidden_1)]
    activations = put(after(places, *blocks), tokens, put_values)
    plane_sums = planes(after(place, activations), hidden, later)
    summed = lax.psum_scatter(
        plane_sums.reshape(n_dp * rows_in, -1), "dp", scatter_dimension=0, tiled=True
    )
    results = first_back(
        after(vec, plane_sums), picked, grad_rows, carry, [gm_0, gm_1], w_in
    )
    grad_values, first_sums, *last = together(*results, *last)
    blocks = add_blocks(place, [last], n_dp, rows_in)
    last = moves.over_z(blocks)
    input_grad = put(after(places, *blocks), cotangent, grad_values)
    input_grad, *last = together(input_grad, *last)
    table, mine, send = make_table(
        total,
        place,
        first_sums,
        sums_a,
        sums_b,
        turn_sums,
        sums_0,
        sums_1,
        summed,
        last,
    )
    parts = moves.over_z([table] * n_dp)
    theirs = moves.over_core(send)
    theirs, *parts = together(theirs, *parts)
    table = add_parts(moves.over_yx([add_parts(parts)] * moves.squares))
    table = table + moves.over_core(table)

    summed_expand, summed_contract = from_quarters(total, summed)
    own = lax.dynamic_slice_in_dim(table[:13], owner * columns, columns, axis=1)
    masters = (project_in, project_out, expand, contract, vectors)
    firsts = (first_in, first_out, first_expand, first_contract, first_vectors)
    seconds = (second_in, second_out, second_expand, second_contract, second_vectors)
    grad_norm, *updates = adam(
        place,
        table,
        mine,
        theirs,
        summed_expand,
        summed_contract,
        own,
        masters,
        firsts,
        seconds,
    )
    return (activations, input_grad, grad_norm.reshape(1), *updates)


def solution(mesh):
    split = P(AXES, None)
    columns = P(None, AXES)
    weights = (split, split, split, split, columns)
    return jax.shard_map(
        functools.partial(on_device, mesh.shape["dp"], mesh.shape["fsdp"]),
        mesh=mesh,
        in_specs=(split, split, split) + weights * 3,
        out_specs=(split, split, P()) + weights * 4,
        check_vma=False,
    )
```

```python
import functools
import math

import jax
import jax.numpy as jnp
from jax import lax
from jax.experimental import pallas as pl
from jax.experimental.pallas import tpu as pltpu
from jax.sharding import PartitionSpec as P

D = 768
HEADS = 12
HEAD_DIM = 64
KEEP_GLOBAL = 98
KEEP_LOCAL = 18
KEEP = 268
PARAMS = 7087872
STEP = 5

norm_eps = 1e-06
clip_share = 0.05
matrix_rate = 0.04
vector_rate = 0.3
matrix_decay = 0.05
first_beta = 0.5
second_beta = 0.5
adam_eps = 1e-08

AXES = ("dp", "fsdp")
BF = jnp.bfloat16
F32 = jnp.float32
NT = (((1,), (1,)), ((), ()))
TN = (((0,), (0,)), ((), ()))
PAD = -(-KEEP // 16) * 16
PAIRS = HEADS // 2
PW = 2 * HEAD_DIM
SETS = ((0,), (1, 2))
CHUNKS = 2
QUARTERS = 2 * CHUNKS
HIDDEN = 4 * D
IMAGES = 2
NEG = -1e30
SEGMENTS = (
    (0, 112, 0, KEEP_GLOBAL),
    (96, 112, KEEP_GLOBAL, 2 * KEEP_GLOBAL),
    (192, 80, 2 * KEEP_GLOBAL, KEEP),
)


def nn(left, right):
    return jnp.dot(left, right, preferred_element_type=F32)


def nt(left, right):
    return lax.dot_general(left, right, NT, preferred_element_type=F32)


def tn(left, right):
    return lax.dot_general(left, right, TN, preferred_element_type=F32)


def params(limit=60):
    return pltpu.CompilerParams(vmem_limit_bytes=limit * 2**20)


def cost(flops, moved, exps=0):
    return pl.CostEstimate(flops=int(flops), bytes_accessed=int(moved), transcendentals=int(exps))


def whole(shape):
    return pl.BlockSpec(shape, lambda *_: (0,) * len(shape))


ANY = pl.BlockSpec(memory_space=pl.ANY)
SMEM = pl.BlockSpec(memory_space=pltpu.SMEM)


def normalize(values):
    centred = values - jnp.mean(values, axis=-1, keepdims=True)
    spread = jnp.mean(centred * centred, axis=-1, keepdims=True)
    inverse = lax.rsqrt(spread + norm_eps)
    return centred * inverse, inverse


def norm_back(grad, normed, inverse, gain):
    pulled = grad * gain
    return inverse * (
        pulled
        - jnp.mean(pulled, axis=-1, keepdims=True)
        - normed * jnp.mean(pulled * normed, axis=-1, keepdims=True)
    )


def column_sum(values):
    return jnp.sum(values, axis=0, keepdims=True)


def window_start(step, image_tokens, rows, window):
    return jnp.minimum((IMAGES * image_tokens * step) // 16, (rows - window) // 16) * 16


def pick_kernel(image_tokens, rows, window, part, place, slots, source, picked):
    step = pl.program_id(0)
    shift = IMAGES * image_tokens * step - window_start(step, image_tokens, rows, window)
    for image in range(IMAGES):
        first = (image * image_tokens) // 16 * 16
        span = min(part, window - first)
        target = slots[image] + shift + image * image_tokens - first
        hot = lax.broadcasted_iota(jnp.int32, (PAD, span), 1) == target
        values = nn(hot.astype(F32).astype(BF), source[first : first + span, :])
        picked[image * PAD : (image + 1) * PAD, :] = values.astype(BF)


def pick(place, source, slots):
    rows = source.shape[0]
    count = slots.shape[0]
    image_tokens = rows // count
    window = -(-(IMAGES * image_tokens + 15) // 16) * 16
    part = -(-(image_tokens + 32) // 16) * 16
    start = functools.partial(
        window_start, image_tokens=image_tokens, rows=rows, window=window
    )
    return pl.pallas_call(
        functools.partial(pick_kernel, image_tokens, rows, window, part),
        grid=(count // IMAGES,),
        in_specs=[
            SMEM,
            pl.BlockSpec((IMAGES, PAD, 1), lambda i: (i, 0, 0)),
            pl.BlockSpec((pl.Element(window), pl.Element(D)), lambda i: (start(i), 0)),
        ],
        out_specs=pl.BlockSpec((IMAGES * PAD, D), lambda i: (i, 0)),
        out_shape=jax.ShapeDtypeStruct((count * PAD, D), BF),
        compiler_params=params(20),
        cost_estimate=cost(2 * count * PAD * window * D, 2 * rows * D + 2 * count * PAD * D),
        name="pick_rows",
    )(place, slots, source)


def local_mask():
    first, rows, low, high = SEGMENTS[2]
    slot = jnp.arange(rows) + first
    crop = jnp.where((slot >= low) & (slot < high), (slot - low) // KEEP_LOCAL, -1)
    same = (crop[:, None] == crop[None, :]) & (crop[:, None] >= 0)
    bias = jnp.where(same, 0.0, NEG).astype(F32)
    return jnp.concatenate([bias, bias], axis=1)


def lanes_of(rows):
    return lax.broadcasted_iota(jnp.int32, (rows, PW), 1) < HEAD_DIM


def split_heads(values):
    first = lanes_of(values.shape[0])
    zero = jnp.zeros_like(values)
    return jnp.concatenate(
        [jnp.where(first, values, zero), jnp.where(first, zero, values)], axis=0
    )


def join_heads(values):
    rows = values.shape[0] // 2
    return jnp.where(lanes_of(rows), values[:rows], values[rows:])


def rows_of(segment):
    return slice(segment[0], segment[0] + segment[1])


def attention(jobs, mask):
    chains = [(job, segment) for job in jobs for segment in SEGMENTS]
    scores = []
    for (query, key_rows, _), segment in chains:
        rows = rows_of(segment)
        scores.append(nt(split_heads(query[rows] * HEAD_DIM**-0.5), key_rows[rows]))
    mask = jnp.concatenate([mask[:, : mask.shape[0]]] * 2, axis=0)
    probs = []
    for (_, segment), score in zip(chains, scores):
        first, count, low, high = segment
        if low == 2 * KEEP_GLOBAL:
            score = score + mask
        else:
            slot = lax.broadcasted_iota(jnp.int32, (1, count), 1) + first
            score = jnp.where((slot >= low) & (slot < high), score, NEG)
        grown = jnp.exp(score - jnp.max(score, axis=-1, keepdims=True))
        probs.append((grown * (1.0 / jnp.sum(grown, axis=-1, keepdims=True))).astype(BF))
    parts = []
    for ((_, _, value), segment), prob in zip(chains, probs):
        parts.append(join_heads(nn(prob, value[rows_of(segment)])))
    slot = lax.broadcasted_iota(jnp.int32, (16, 1), 0)
    results = []
    for index in range(len(jobs)):
        one, two, three = parts[3 * index : 3 * index + 3]
        results.append(
            jnp.concatenate(
                [
                    one[:96],
                    jnp.where(slot + 96 < KEEP_GLOBAL, one[96:], two[:16]),
                    two[16:96],
                    jnp.where(slot + 192 < 2 * KEEP_GLOBAL, two[96:], three[:16]),
                    three[16:],
                ],
                axis=0,
            ).astype(BF)
        )
    return results


def attention_back(jobs, mask):
    chains = [(job, segment) for job in jobs for segment in SEGMENTS]
    halves, grads = [], []
    for (query, _, _, grad), segment in chains:
        first, count, low, high = segment
        rows = rows_of(segment)
        halves.append(split_heads(query[rows] * HEAD_DIM**-0.5))
        slot = lax.broadcasted_iota(jnp.int32, (count, 1), 0) + first
        kept = jnp.where((slot >= low) & (slot < high), grad[rows], jnp.zeros((), BF))
        grads.append(split_heads(kept))
    scores, grad_probs = [], []
    for ((_, key_rows, value, _), segment), half, grad in zip(chains, halves, grads):
        rows = rows_of(segment)
        scores.append(nt(key_rows[rows], half))
        grad_probs.append(nt(value[rows], grad))
    probs, grad_scores = [], []
    for (_, segment), score, pulled in zip(chains, scores, grad_probs):
        first, count, low, high = segment
        if low == 2 * KEEP_GLOBAL:
            score = score + mask
        else:
            slot = lax.broadcasted_iota(jnp.int32, (count, 1), 0) + first
            score = jnp.where((slot >= low) & (slot < high), score, NEG)
        grown = jnp.exp(score - jnp.max(score, axis=0, keepdims=True))
        prob = grown * (1.0 / jnp.sum(grown, axis=0, keepdims=True))
        weighted = jnp.sum(prob * pulled, axis=0, keepdims=True)
        probs.append(prob.astype(BF))
        grad_scores.append((prob * (pulled - weighted)).astype(BF))
    parts = [[], [], []]
    for prob, grad in zip(probs, grads):
        parts[2].append(nn(prob, grad))
    for score, half in zip(grad_scores, halves):
        parts[1].append(nn(score, half))
    for ((_, key_rows, _, _), segment), score in zip(chains, grad_scores):
        parts[0].append(join_heads(tn(score, key_rows[rows_of(segment)])) * HEAD_DIM**-0.5)
    results = []
    for index in range(len(jobs)):
        joined = []
        for part in parts:
            one, two, three = part[3 * index : 3 * index + 3]
            joined.append(
                jnp.concatenate(
                    [
                        one[:96],
                        one[96:] + two[:16],
                        two[16:96],
                        two[96:] + three[:16],
                        three[16:],
                    ],
                    axis=0,
                ).astype(BF)
            )
        results.append(joined)
    return results


def pairs_of(place, groups):
    core = place[2]
    return [2 * group + core for group in groups] + [2 * group + 1 - core for group in groups]


def lane_block(index):
    return pl.ds(pl.multiple_of(index * PW, PW), PW)


def heads_kernel(groups, place, mask, vec, source, own_w, other_w, *refs):
    if groups[0] == 0:
        mixed, heads, normed, weight = refs
        unit, _ = normalize(source[...].astype(F32))
        rows = (unit * vec[0:1, :].astype(F32) + vec[1:2, :].astype(F32)).astype(BF)
        normed[...] = rows
    else:
        mixed, heads, weight = refs
        rows = source[...]
    width = 3 * PW
    half = len(groups) * width

    @pl.when(pl.program_id(0) == 0)
    def _():
        weight[:, :half] = own_w[:, :half]
        weight[:, half:] = other_w[:, :half]

    product = nn(rows, weight[...])
    jobs, lanes = [], []
    for index, pair in enumerate(pairs_of(place, groups)):
        at = index * width
        block = lane_block(pair)
        query = (product[:, at : at + PW] + vec[2:3, block].astype(F32)).astype(BF)
        key_rows = product[:, at + PW : at + 2 * PW].astype(BF)
        value = (product[:, at + 2 * PW : at + width] + vec[3:4, block].astype(F32)).astype(BF)
        mixed[:, at : at + PW] = query
        mixed[:, at + PW : at + 2 * PW] = key_rows
        mixed[:, at + 2 * PW : at + width] = value
        for image in range(IMAGES):
            span = slice(image * PAD, (image + 1) * PAD)
            jobs.append((query[span], key_rows[span], value[span]))
            lanes.append((span, lane_block(pair - 2 * groups[0])))
    for (span, block), result in zip(lanes, attention(jobs, mask[...])):
        heads[span, block] = result


def heads_forward(groups, place, mask, vec, source, own_w, other_w):
    rows = source.shape[0]
    size = IMAGES * PAD
    width = 6 * PW * len(groups)
    wide = pl.BlockSpec((size, D), lambda i: (i, 0))
    weight = whole(own_w.shape)
    outs = [
        (pl.BlockSpec((size, width), lambda i: (i, 0)), jax.ShapeDtypeStruct((rows, width), BF)),
        (
            pl.BlockSpec((size, width // 3), lambda i: (i, 0)),
            jax.ShapeDtypeStruct((rows, width // 3), BF),
        ),
    ]
    if groups[0] == 0:
        outs.append((wide, jax.ShapeDtypeStruct((rows, D), BF)))
    return pl.pallas_call(
        functools.partial(heads_kernel, groups),
        grid=(rows // size,),
        in_specs=[SMEM, whole(mask.shape), whole((16, D)), wide, weight, weight],
        out_specs=tuple(out[0] for out in outs),
        out_shape=tuple(out[1] for out in outs),
        scratch_shapes=[pltpu.VMEM((D, width), BF)],
        compiler_params=params(32),
        cost_estimate=cost(2 * rows * D * width + rows * 1e5 * len(groups), 8 * rows * D),
        name=f"attention_{groups[0]}",
    )(place, mask, vec, source, own_w, other_w)


def heads_back_kernel(groups, steps, place, mask, grad_attended, normed, w_out, mixed, *refs):
    heads = refs[:-6] if len(refs) == 6 else refs[: -8]
    (grad_mixed, gw_own, gw_other, sums, kept_normed, kept_mixed) = refs[len(heads) :][:6]
    kept_heads, kept_grad = refs[len(heads) + 6 :] if heads else (None, None)
    step = pl.program_id(0)
    size = IMAGES * PAD
    width = 3 * PW
    half = len(groups) * width

    @pl.when(step == 0)
    def _():
        sums[...] = jnp.zeros_like(sums)

    @pl.when(step < steps)
    def _():
        rows = pl.ds(pl.multiple_of(step * size, 16), size)
        kept_normed[rows, :] = normed[...]
        incoming = grad_attended[...]
        if heads:
            kept_grad[rows, :] = incoming
            at = 0
            for part in heads:
                kept_heads[rows, at : at + part.shape[1]] = part[...]
                at += part.shape[1]
        jobs, places = [], []
        for index, pair in enumerate(pairs_of(place, groups)):
            at = index * width
            grad_heads = nt(incoming, w_out[lane_block(pair), :]).astype(BF)
            for image in range(IMAGES):
                span = slice(image * PAD, (image + 1) * PAD)
                jobs.append(
                    (
                        mixed[span, at : at + PW],
                        mixed[span, at + PW : at + 2 * PW],
                        mixed[span, at + 2 * PW : at + width],
                        grad_heads[span],
                    )
                )
                places.append((image, at))
        for (image, at), parts in zip(places, attention_back(jobs, mask[...])):
            for index, low in enumerate(parts):
                columns = slice(at + index * PW, at + (index + 1) * PW)
                grad_mixed[image * PAD : (image + 1) * PAD, columns] = low
                here = pl.ds(pl.multiple_of(step * size + image * PAD, 16), PAD)
                kept_mixed[here, columns] = low
                if index != 1:
                    sums[0:1, columns] += column_sum(low.astype(F32))

    @pl.when(step == steps)
    def _():
        first = 0
        if heads:
            first = D // 2
            core = place[2]
            own = pl.ds(pl.multiple_of(core * first, 128), first)
            other = pl.ds(pl.multiple_of((1 - core) * first, 128), first)
            gw_own[:, :first] = tn(kept_heads[...], kept_grad[:, own]).astype(BF)
            gw_other[:, :first] = tn(kept_heads[...], kept_grad[:, other]).astype(BF)
        gw_other[:, first:] = tn(kept_normed[...], kept_mixed[:, half:]).astype(BF)
        gw_own[:, first:] = tn(kept_normed[...], kept_mixed[:, :half]).astype(BF)


def heads_backward(groups, place, mask, grad_attended, normed, w_out, mixed, heads=()):
    rows, width = mixed.shape
    size = IMAGES * PAD
    steps = rows // size
    last = steps - 1

    def block(width):
        return pl.BlockSpec((size, width), lambda i: (jnp.minimum(i, last), 0))

    weight = (D, width // 2 + (D // 2 if heads else 0))
    kept = [D, width] + [D, D] * bool(heads)
    return pl.pallas_call(
        functools.partial(heads_back_kernel, groups, steps),
        grid=(steps + 1,),
        in_specs=[SMEM, whole(mask.shape), block(D), block(D)]
        + [pl.BlockSpec((D, D), lambda i: (0, w_out.shape[1] // D - 1)), block(width)]
        + [block(part.shape[1]) for part in heads],
        out_specs=(block(width), whole(weight), whole(weight), whole((8, width))),
        out_shape=(
            jax.ShapeDtypeStruct((rows, width), BF),
            jax.ShapeDtypeStruct(weight, BF),
            jax.ShapeDtypeStruct(weight, BF),
            jax.ShapeDtypeStruct((8, width), F32),
        ),
        scratch_shapes=[pltpu.VMEM((rows, lanes), BF) for lanes in kept],
        compiler_params=params(60 if heads else 40),
        cost_estimate=cost(
            2 * rows * D * (width // 3 + width) + rows * 3e5 * len(groups), 12 * rows * D
        ),
        name=f"attention_back_{groups[0]}",
    )(place, mask, grad_attended, normed, w_out, mixed, *heads)


TILE = 256


def gelu_and_slope(values):
    below = 0.5 + 0.5 * lax.erf(values * math.sqrt(0.5))
    bell = jnp.exp(-0.5 * values * values) * (1.0 / math.sqrt(2.0 * math.pi))
    return values * below, below + values * bell


def alternating(bias, weights, make_left, right, rows, kept_active, kept_before, sums):
    result = pulled = 0.0
    grad = nt(right, weights[1][...])
    left = make_left()
    before = nn(left, weights[0][...])
    for half in range(2):
        kept = slice(half * D, (half + 1) * D)
        active, slope = gelu_and_slope(before + bias[half])
        low = (grad * slope).astype(BF)
        active = active.astype(BF)
        kept_active[rows, kept] = active
        kept_before[rows, kept] = low
        if half == 0:
            before, grad = nn(left, weights[2][...]), nt(right, weights[3][...])
        sums[half] += column_sum(low.astype(F32))
        result = result + nn(active, weights[2 * half + 1][...])
        pulled = pulled + nt(low, weights[2 * half][...])
    return result, pulled


def both_ways(chunk, bias, weights, left, right, rows, kept_active, kept_before, sums):
    tiles = D // TILE
    for half in range(2):
        up, down = weights[2 * half], weights[2 * half + 1]
        for tile in range(tiles):
            columns = slice(tile * TILE, (tile + 1) * TILE)
            kept = slice(half * D + tile * TILE, half * D + (tile + 1) * TILE)
            before = nn(left, up[:, columns]) + bias[2 * chunk + half, :, columns]
            active, slope = gelu_and_slope(before)
            kept_active[rows, kept] = active.astype(BF)
            low = (nt(right, down[columns, :]) * slope).astype(BF)
            kept_before[rows, kept] = low
            sums[half, :, columns] += column_sum(low.astype(F32))
    result = nn(kept_active[rows, :D], weights[1][...])
    result += nn(kept_active[rows, D:], weights[3][...])
    pulled = nt(kept_before[rows, :D], weights[0][...])
    pulled += nt(kept_before[rows, D:], weights[2][...])
    return result, pulled


def hidden_grads(tile, blocks, kept, gw):
    kept_normed, kept_grad, kept_active, kept_before = kept

    def ordered(value):
        if blocks:
            value = jnp.concatenate([value[at : at + size] for at, size in blocks], axis=0)
        return value.astype(BF)

    for half in range(2):
        columns = slice(half * D, (half + 1) * D)

        @pl.when(tile == 2 * half)
        def _():
            gw[...] = ordered(tn(kept_normed[...], kept_before[:, columns]))

        @pl.when(tile == 2 * half + 1)
        def _():
            gw[...] = ordered(tn(kept_active[:, columns], kept_grad[...]))


def routed_rows(picked, grads, vec):
    inputs = picked[...].astype(F32)
    grad_rows = grads[...].astype(F32)
    routed = jnp.sum(inputs * vec[8:9, :].astype(F32), axis=-1, keepdims=True)
    return inputs, grad_rows, routed, routed * grad_rows


def first_mlp_kernel(steps, size, blocks, bias, vec, w_out, picked, grads, *refs):
    heads = refs[: len(SETS)]
    refs = refs[len(SETS) :]
    weights = refs[:4]
    attended, normed, out, back, gw, sums = refs[4:10]
    kept = refs[10:]
    kept_normed, kept_grad, kept_active, kept_before = kept
    step = pl.program_id(0)

    @pl.when(step == 0)
    def _():
        sums[...] = jnp.zeros_like(sums)

    @pl.when(step < steps)
    def _():
        rows = pl.ds(pl.multiple_of(step * size, 16), size)
        inputs, _, _, grad_branch = routed_rows(picked, grads, vec)
        right = grad_branch.astype(BF)
        joined = jnp.concatenate([part[...] for part in heads], axis=1)
        mixed = nn(joined, w_out[...]) + vec[4:5, :].astype(F32)
        attended[...] = mixed
        kept_grad[rows, :] = right

        def make_left():
            unit, _ = normalize(inputs + mixed)
            left = (unit * vec[5:6, :].astype(F32) + vec[6:7, :].astype(F32)).astype(BF)
            normed[...] = left
            kept_normed[rows, :] = left
            return left

        out[...], back[...] = alternating(
            bias, weights, make_left, right, rows, kept_active, kept_before, sums
        )

    @pl.when(step >= steps)
    def _():
        hidden_grads(step - steps, blocks, kept, gw)


def second_mlp_kernel(
    steps, size, blocks, place, bias, vec, picked, grads, normed, attended, out, back, *refs
):
    weights = refs[:4]
    (grad_attended, carry, values, turn_sums, sums, gw) = refs[4:10]
    kept = refs[10:]
    kept_normed, kept_grad, kept_active, kept_before = kept
    step = pl.program_id(0)

    @pl.when(step == 0)
    def _():
        sums[...] = jnp.zeros_like(sums)
        turn_sums[...] = jnp.zeros_like(turn_sums)

    @pl.when(step < steps)
    def _():
        rows = pl.ds(pl.multiple_of(step * size, 16), size)
        inputs, grad_rows, routed, grad_branch = routed_rows(picked, grads, vec)
        left = normed[...]
        right = grad_branch.astype(BF)
        kept_normed[rows, :] = left
        kept_grad[rows, :] = right
        result, pulled = both_ways(
            1, bias, weights, left, right, rows, kept_active, kept_before, sums
        )
        pulled += back[...]
        router = vec[8:9, :].astype(F32)
        mixed = attended[...]
        branch = mixed + (result + out[...]) + vec[7:8, :].astype(F32)
        values[...] = (inputs + routed * branch).astype(BF)
        grad_routed = jnp.sum(grad_rows * branch, axis=-1, keepdims=True)
        unit, inverse = normalize(inputs + mixed)
        residual = norm_back(pulled, unit, inverse, vec[5:6, :].astype(F32))
        low = (grad_branch + residual).astype(BF)
        grad_attended[...] = low
        carry[...] = residual + grad_routed * router
        turn_sums[0:1, :] += column_sum(low.astype(F32))
        turn_sums[1:2, :] += column_sum(pulled * unit)
        turn_sums[2:3, :] += column_sum(pulled)
        turn_sums[3:4, :] += column_sum(right.astype(F32))
        turn_sums[4:5, :] += column_sum(inputs * grad_routed)

    @pl.when(step >= steps)
    def _():
        hidden_grads(step - steps, blocks, kept, gw)


def mlp_specs(chunk, rows):
    size = PAD
    steps = rows // size
    last = steps - 1

    def wide(width=D):
        return pl.BlockSpec((size, width), lambda i: (jnp.minimum(i, last), 0))

    weights = [
        pl.BlockSpec((D, D), lambda i, at=at: (0, at), pipeline_mode=pl.Buffered(1))
        for at in (0, 2, 1, 3)
    ]

    def gw_block(i):
        tile = jnp.clip(i - steps, 0, 3)
        return (0, tile // 2 + 2 * (tile % 2))

    scratch = [
        pltpu.VMEM((rows, D), BF),
        pltpu.VMEM((rows, D), BF),
        pltpu.VMEM((rows, 2 * D), BF),
        pltpu.VMEM((rows, 2 * D), BF),
    ]
    return size, steps, 4, wide, weights, pl.BlockSpec((D, D), gw_block), scratch


def first_mlp(blocks, bias, vec, picked, grads, heads, weights):
    rows = picked.shape[0]
    size, steps, tiles, wide, weight_specs, gw, scratch = mlp_specs(0, rows)
    total = jax.ShapeDtypeStruct((rows, D), F32)
    return pl.pallas_call(
        functools.partial(first_mlp_kernel, steps, size, blocks),
        grid=(steps + tiles,),
        in_specs=[whole(bias.shape), whole((16, D))]
        + [pl.BlockSpec((D, D), lambda i: (0, 4), pipeline_mode=pl.Buffered(1))]
        + [wide()] * 2
        + [wide(part.shape[1]) for part in heads]
        + weight_specs,
        out_specs=(wide(),) * 4 + (gw, whole((2, 1, D))),
        out_shape=(
            total,
            jax.ShapeDtypeStruct((rows, D), BF),
            total,
            total,
            jax.ShapeDtypeStruct((D, 4 * D), BF),
            jax.ShapeDtypeStruct((2, 1, D), F32),
        ),
        scratch_shapes=scratch,
        compiler_params=params(),
        cost_estimate=cost(26 * rows * D * D, 30 * rows * D, 4 * rows * D),
        name="feed_forward_0",
    )(bias, vec, weights, picked, grads, *heads, *[weights] * 4)


def second_mlp(blocks, place, bias, vec, picked, grads, normed, attended, out, back, weights):
    rows = picked.shape[0]
    size, steps, tiles, wide, weight_specs, gw, scratch = mlp_specs(1, rows)
    low = jax.ShapeDtypeStruct((rows, D), BF)
    return pl.pallas_call(
        functools.partial(second_mlp_kernel, steps, size, blocks),
        grid=(steps + tiles,),
        in_specs=[SMEM, whole(bias.shape), whole((16, D))]
        + [wide()] * 6
        + weight_specs,
        out_specs=(wide(), wide(), wide(), whole((8, D)), whole((2, 1, D)), gw),
        out_shape=(
            low,
            jax.ShapeDtypeStruct((rows, D), F32),
            low,
            jax.ShapeDtypeStruct((8, D), F32),
            jax.ShapeDtypeStruct((2, 1, D), F32),
            jax.ShapeDtypeStruct((D, 4 * D), BF),
        ),
        scratch_shapes=scratch,
        compiler_params=params(),
        cost_estimate=cost(26 * rows * D * D, 40 * rows * D, 4 * rows * D),
        name="feed_forward_1",
    )(place, bias, vec, picked, grads, normed, attended, out, back, *[weights] * 4)


def first_back_kernel(count, vec, picked, grads, carry, *refs):
    mixed = refs[:count]
    weights = refs[count : 3 * count]
    values, sums = refs[3 * count : 3 * count + 2]
    kept = refs[3 * count + 2 :]

    @pl.when(pl.program_id(0) == 0)
    def _():
        sums[...] = jnp.zeros_like(sums)
        for index in range(count):
            half = mixed[index].shape[1] // 2
            kept[index][:, :half] = weights[2 * index][:, :half]
            kept[index][:, half:] = weights[2 * index + 1][:, :half]

    pulled = nt(mixed[0][...], kept[0][...])
    for index in range(1, count):
        pulled += nt(mixed[index][...], kept[index][...])
    unit, inverse = normalize(picked[...].astype(F32))
    grad = norm_back(pulled, unit, inverse, vec[0:1, :].astype(F32))
    values[...] = (grads[...].astype(F32) + grad + carry[...]).astype(BF)
    sums[0:1, :] += column_sum(pulled * unit)
    sums[1:2, :] += column_sum(pulled)


def first_back(vec, picked, grads, carry, mixed, weights):
    rows = picked.shape[0]
    size = 2 * PAD
    wide = pl.BlockSpec((size, D), lambda i: (i, 0))
    flat = [weight for pair in weights for weight in pair]
    return pl.pallas_call(
        functools.partial(first_back_kernel, len(mixed)),
        grid=(rows // size,),
        in_specs=[whole((16, D)), wide, wide, wide]
        + [pl.BlockSpec((size, part.shape[1]), lambda i: (i, 0)) for part in mixed]
        + [whole(weight.shape) for weight in flat],
        out_specs=(wide, whole((8, D))),
        out_shape=(jax.ShapeDtypeStruct((rows, D), BF), jax.ShapeDtypeStruct((8, D), F32)),
        scratch_shapes=[pltpu.VMEM((D, part.shape[1]), BF) for part in mixed],
        compiler_params=params(44),
        cost_estimate=cost(6 * rows * D * D, 16 * rows * D),
        name="first_norm_back",
    )(vec, picked, grads, carry, *mixed, *flat)


def put_kernel(span, places, source, value, after, out, both):
    width = places.shape[2]
    for image in range(IMAGES):
        rows = slice(image * span, (image + 1) * span)
        both[:PAD, :] = value[image * PAD : (image + 1) * PAD, :]
        if image + 1 < IMAGES:
            both[PAD:, :] = value[(image + 1) * PAD : (image + 1) * PAD + 16, :]
        else:
            both[PAD:, :] = after[...]
        same = lax.broadcasted_iota(jnp.int32, (span, width), 0) == places[image]
        hot = same.astype(F32)
        kept = jnp.max(hot, axis=-1, keepdims=True) > 0.5
        moved = nn(hot.astype(BF), both[...])
        out[rows, :] = jnp.where(kept, moved, source[rows, :].astype(F32)).astype(BF)


def put(places, source, values):
    rows = source.shape[0]
    count = places.shape[0]
    span = -(-(rows // count) // 16) * 16
    steps = count // IMAGES
    block = pl.BlockSpec((IMAGES * span, D), lambda i: (i, 0))
    return pl.pallas_call(
        functools.partial(put_kernel, span),
        grid=(steps,),
        in_specs=[
            pl.BlockSpec((IMAGES, 1, places.shape[2]), lambda i: (i, 0, 0)),
            block,
            pl.BlockSpec((IMAGES * PAD, D), lambda i: (i, 0)),
            pl.BlockSpec(
                (16, D), lambda i: (jnp.minimum(i + 1, steps - 1) * (IMAGES * PAD // 16), 0)
            ),
        ],
        out_specs=block,
        out_shape=jax.ShapeDtypeStruct((rows, D), BF),
        scratch_shapes=[pltpu.VMEM((PAD + 16, D), BF)],
        compiler_params=params(24),
        cost_estimate=cost(2 * rows * D * (PAD + 16), 6 * rows * D),
        name="put_rows",
    )(places, source, values, values)


def put_places(keep_slots, image_tokens):
    count = keep_slots.shape[0]
    span = -(-image_tokens // 16) * 16
    image = jnp.arange(count, dtype=jnp.int32)[:, None]
    own = keep_slots + image * (image_tokens - span)
    following = jnp.concatenate([keep_slots[1:, :16], jnp.full((1, 16), -span, jnp.int32)], axis=0)
    following = following + (image + 1) * image_tokens - image * span
    following = jnp.where(image < count - 1, following, -1)
    gap = jnp.full((count, PAD - KEEP), -1, jnp.int32)
    return jnp.concatenate([own, gap, following], axis=1)[:, None, :]


class Moves:
    def __init__(self, n_dp, n_fsdp):
        self.n_dp = n_dp
        self.n_fsdp = n_fsdp
        self.squares = n_fsdp // 2
        outer = lax.axis_index("dp")
        inner = lax.axis_index("fsdp")
        self.z = outer
        self.yx = inner // 2
        self.core = inner % 2
        self.place = jnp.stack([self.z, self.yx, self.core]).astype(jnp.int32)

    def swap(self, value, mask):
        total = self.n_dp * self.n_fsdp
        return lax.ppermute(value, AXES, [(i, i ^ mask) for i in range(total)])

    def over_z(self, values):
        return [values[0]] + [self.swap(values[k], k * self.n_fsdp) for k in range(1, self.n_dp)]

    def over_yx(self, values):
        return [values[0]] + [self.swap(values[k], 2 * k) for k in range(1, self.squares)]

    def over_core(self, value):
        return self.swap(value, 1)

    def square_blocks(self, size):
        return [
            ((z * self.n_fsdp + inner) * size, size)
            for inner in range(self.n_fsdp)
            for z in range(self.n_dp)
        ]

    def over_square(self, value, ordered):
        rows, n = value.shape
        if not ordered:
            value = value.reshape(self.n_dp, self.n_fsdp, -1, n).transpose(1, 0, 2, 3)
        value = value.reshape(rows, n)
        return lax.psum_scatter(value, "fsdp", scatter_dimension=0, tiled=True)

    def by_chip(self, value):
        chips = self.n_dp * self.squares
        return value.reshape(self.n_dp, self.squares, value.shape[0] // chips, value.shape[1])

    def add_cores(self, place, keeps, arrived):
        keeps = [self.by_chip(value) for value in keeps]
        arrived = [self.by_chip(value) for value in arrived]
        return add_pairs(place, keeps, arrived, self.squares)


def add_parts(parts):
    total = parts[0].astype(F32)
    for part in parts[1:]:
        total = total + part.astype(F32)
    return total


def together(*values):
    return lax.optimization_barrier(values)


def after(value, *others):
    return lax.optimization_barrier((value, *others))[0]


def place_kernel(axis, count, cuts, place, *refs):
    outs = refs[count:]
    me = place[axis]
    for k in range(count):
        for (first, width), out in zip(cuts, outs):
            if axis == 0:
                out[me ^ k] = refs[k][:, first : first + width]
            else:
                out[:, me ^ k] = refs[k][...]


def place_blocks(place, axis, blocks, widths):
    count = len(blocks)
    cuts, at = [], 0
    for width in widths:
        cuts.append((at, width))
        at += width
    shape = blocks[0].shape[:-1]
    shape = shape[:axis] + (count,) + shape[axis:]
    vmem = pl.BlockSpec(memory_space=pltpu.VMEM)
    return pl.pallas_call(
        functools.partial(place_kernel, axis, count, cuts),
        in_specs=[SMEM] + [vmem] * count,
        out_specs=[vmem] * len(widths),
        out_shape=[jax.ShapeDtypeStruct(shape + (width,), BF) for width in widths],
        compiler_params=params(24),
        cost_estimate=cost(0, 4 * math.prod(shape) * at),
        name="place_blocks",
    )(place, *blocks)


def add_pairs_kernel(parts, squares, place, *refs):
    outs = refs[2 * parts * squares :]
    at = 0
    for part in range(parts):
        for k in range(squares):
            index = part * squares + k
            left, right = refs[index], refs[parts * squares + index]
            width = left.shape[3]
            total = left[...].astype(F32) + right[...].astype(F32)
            outs[k][:, :, at : at + width] = total[:, 0].astype(BF)
        at += width


def add_pairs(place, keeps, arrived, squares):
    specs, left, right = [], [], []
    n_dp, _, m, _ = keeps[0].shape
    for keep, other in zip(keeps, arrived):
        for k in range(squares):
            specs.append(
                pl.BlockSpec(
                    (n_dp, 1, m, keep.shape[3]), lambda i, place, k=k: (0, place[1] ^ k, 0, 0)
                )
            )
            left.append(keep)
            right.append(other)
    shape = (n_dp, m, sum(keep.shape[3] for keep in keeps))
    return pl.pallas_call(
        functools.partial(add_pairs_kernel, len(keeps), squares),
        grid_spec=pltpu.PrefetchScalarGridSpec(
            num_scalar_prefetch=1,
            grid=(1,),
            in_specs=specs + specs,
            out_specs=[pl.BlockSpec(shape, lambda i, place: (0, 0, 0))] * squares,
        ),
        out_shape=[jax.ShapeDtypeStruct(shape, BF)] * squares,
        compiler_params=params(24),
        cost_estimate=cost(0, 6 * squares * math.prod(shape)),
        name="add_cores",
    )(place, *left, *right)


def add_blocks_kernel(count, rows, sizes, place, *refs):
    outs = refs[count * sum(sizes) :]
    at = 0
    for index in range(count):
        lane = 0
        for terms in sizes:
            total = refs[at][0].astype(F32)
            for term in range(1, terms):
                total = total + refs[at + term][0].astype(F32)
            at += terms
            for first in range(0, total.shape[0], rows):
                width = total.shape[1]
                outs[index][:, lane : lane + width] = total[first : first + rows].astype(BF)
                lane += width


def add_blocks(place, groups, n_dp, rows):
    specs, operands, lanes = [], [], 0
    for arrays in groups:
        _, m, n = arrays[0].shape
        lanes += n * (m // rows)
    for k in range(n_dp):
        for arrays in groups:
            _, m, n = arrays[0].shape
            spec = pl.BlockSpec((1, m, n), lambda i, place, k=k: (place[0] ^ k, 0, 0))
            specs += [spec] * len(arrays)
            operands += arrays
    sizes = [len(arrays) for arrays in groups]
    return pl.pallas_call(
        functools.partial(add_blocks_kernel, n_dp, rows, sizes),
        grid_spec=pltpu.PrefetchScalarGridSpec(
            num_scalar_prefetch=1,
            grid=(1,),
            in_specs=specs,
            out_specs=[pl.BlockSpec((rows, lanes), lambda i, place: (0, 0))] * n_dp,
        ),
        out_shape=[jax.ShapeDtypeStruct((rows, lanes), BF)] * n_dp,
        compiler_params=params(24),
        cost_estimate=cost(0, 4 * n_dp * rows * lanes * max(sizes)),
        name="add_squares",
    )(place, *operands)


def planes_kernel(count, place, *refs):
    rows = refs[0].shape[1]
    out = refs[-1]
    lane = 0
    for ref in refs[:count]:
        out[:, :, lane : lane + ref.shape[2]] = ref[...]
        lane += ref.shape[2]
    total = refs[count][...].astype(F32)
    for ref in refs[count + 1 : -1]:
        total = total + ref[...].astype(F32)
    width = total.shape[2]
    for first in range(0, total.shape[1], rows):
        out[:, :, lane : lane + width] = total[:, first : first + rows].astype(BF)
        lane += width


def planes(place, ready, parts):
    n_dp, rows, _ = ready[0].shape
    arrays = ready + parts
    lanes = sum(value.shape[2] for value in ready) + parts[0].shape[1] // rows * parts[0].shape[2]
    return pl.pallas_call(
        functools.partial(planes_kernel, len(ready)),
        in_specs=[SMEM] + [pl.BlockSpec(memory_space=pltpu.VMEM)] * len(arrays),
        out_specs=pl.BlockSpec(memory_space=pltpu.VMEM),
        out_shape=jax.ShapeDtypeStruct((n_dp, rows, lanes), BF),
        compiler_params=params(),
        cost_estimate=cost(0, 4 * n_dp * rows * lanes),
        name="planes",
    )(place, *arrays)


def quarters_kernel(total, part, up, down, project_out, *outs):
    outs[0][:, 4 * D :] = project_out[...].astype(BF)
    for chunk, out in enumerate(outs):
        for half in range(2):
            quarter = 2 * chunk + half
            pieces = [
                up[:, (owner * QUARTERS + quarter) * part : (owner * QUARTERS + quarter + 1) * part]
                for owner in range(total)
            ]
            out[:, half * D : (half + 1) * D] = jnp.concatenate(pieces, axis=1).astype(BF)
            rows = slice(quarter * part, (quarter + 1) * part)
            out[:, (2 + half) * D : (3 + half) * D] = down[rows, :].astype(BF)


def to_quarters(total, up, down, project_out):
    rows = up.shape[0]
    part = down.shape[0] // QUARTERS
    shape = jax.ShapeDtypeStruct((rows, 4 * D), BF)
    if part % 8:
        ups = up.astype(BF).reshape(rows, total, QUARTERS, part).transpose(2, 0, 1, 3)
        ups = ups.reshape(QUARTERS, rows, D)
        downs = down.astype(BF).reshape(QUARTERS, part, D)
        first = [ups[0], ups[1], downs[0], downs[1], project_out.astype(BF)]
        second = [ups[2], ups[3], downs[2], downs[3]]
        return [jnp.concatenate(first, axis=1), jnp.concatenate(second, axis=1)]
    vmem = pl.BlockSpec(memory_space=pltpu.VMEM)
    return pl.pallas_call(
        functools.partial(quarters_kernel, total, part),
        in_specs=[vmem] * 3,
        out_specs=[vmem] * 2,
        out_shape=[jax.ShapeDtypeStruct((rows, 5 * D), BF), shape],
        compiler_params=params(),
        cost_estimate=cost(0, 12 * rows * 4 * D),
        name="to_quarters",
    )(up, down, project_out)


def hidden_kernel(total, part, value, up, down):
    pieces = []
    for owner in range(total):
        for quarter in range(QUARTERS):
            at = (4 * (quarter // 2) + quarter % 2) * D + owner * part
            pieces.append(value[:, at : at + part].astype(F32))
    up[...] = jnp.concatenate(pieces, axis=1)
    for quarter in range(QUARTERS):
        at = (4 * (quarter // 2) + 2 + quarter % 2) * D
        down[quarter * part : (quarter + 1) * part, :] = value[:, at : at + D].astype(F32)


def from_quarters(total, value):
    rows = value.shape[0]
    part = D // total
    if part % 8:
        quarters = value[:, : 8 * D].astype(F32).reshape(rows, CHUNKS, 2, 2, D)
        ups = quarters[:, :, 0].reshape(rows, QUARTERS, total, part).transpose(0, 2, 1, 3)
        downs = quarters[:, :, 1].reshape(rows, QUARTERS, D).transpose(1, 0, 2)
        return ups.reshape(rows, HIDDEN), downs.reshape(QUARTERS * part, D)
    vmem = pl.BlockSpec(memory_space=pltpu.VMEM)
    return pl.pallas_call(
        functools.partial(hidden_kernel, total, part),
        in_specs=[vmem],
        out_specs=[vmem] * 2,
        out_shape=[
            jax.ShapeDtypeStruct((rows, HIDDEN), F32),
            jax.ShapeDtypeStruct((QUARTERS * part, D), F32),
        ],
        compiler_params=params(),
        cost_estimate=cost(0, 6 * rows * 8 * D),
        name="from_quarters",
    )(value)


def unit_pieces(total):
    part = D // total
    for quarter in range(QUARTERS):
        for owner in range(total):
            first = (owner * QUARTERS + quarter) * part
            yield quarter, owner * part, first // D, first % D


def vectors_kernel(total, source, vec, bias):
    rows = source[...].astype(F32).T[:16, :]
    vec[...] = rows.astype(BF)
    part = D // total
    pieces = [[] for _ in range(QUARTERS)]
    for quarter, _, row, lane in unit_pieces(total):
        pieces[quarter].append(rows[9 + row : 10 + row, lane : lane + part])
    for quarter in range(QUARTERS):
        bias[quarter] = jnp.concatenate(pieces[quarter], axis=1)


def vectors_of(total, gathered):
    if D // total % 8:
        vec = gathered[:, -128:-112].T
        bias = vec[9:13].astype(F32).reshape(total, QUARTERS, -1).transpose(1, 0, 2)
        return vec, bias.reshape(QUARTERS, 1, D)
    return pl.pallas_call(
        functools.partial(vectors_kernel, total),
        grid=(1,),
        in_specs=[pl.BlockSpec((D, 128), lambda i: (0, gathered.shape[1] // 128 - 1))],
        out_specs=[whole((16, D)), whole((QUARTERS, 1, D))],
        out_shape=[
            jax.ShapeDtypeStruct((16, D), BF),
            jax.ShapeDtypeStruct((QUARTERS, 1, D), F32),
        ],
        compiler_params=params(16),
        cost_estimate=cost(0, 4 * D * 128),
        name="vectors",
    )(gathered)


def pair_sums(core, sums, groups, part):
    width = 3 * PW
    half = len(groups) * width
    pieces = []
    for index in range(len(groups)):
        at = index * width + part * PW
        own = sums[0:1, at : at + PW]
        other = sums[0:1, half + at : half + at + PW]
        pieces += [jnp.where(core == 0, own, other), jnp.where(core == 0, other, own)]
    return pieces


def table_kernel(total, place, *refs):
    (first, sums_a, sums_b, turn, sums_0, sums_1, summed) = refs[:7]
    parts, (table, mine, send) = refs[7:-3], refs[-3:]
    core = place[2]
    table[...] = jnp.zeros_like(table)
    table[0:2, :] = first[0:2, :]
    for row, part in ((2, 0), (3, 2)):
        pieces = pair_sums(core, sums_a, SETS[0], part) + pair_sums(core, sums_b, SETS[1], part)
        table[row : row + 1, :] = jnp.concatenate(pieces, axis=1)
    table[4:9, :] = turn[0:5, :]
    size = D // total
    pieces = sorted((row, lane, quarter, at) for quarter, at, row, lane in unit_pieces(total))
    for row in range(4):
        values = []
        for _, _, quarter, at in pieces[row * len(pieces) // 4 : (row + 1) * len(pieces) // 4]:
            source = sums_1 if quarter // 2 else sums_0
            values.append(source[quarter % 2][:, at : at + size])
        table[9 + row : 10 + row, :] = jnp.concatenate(values, axis=1)
    last = parts[0][...].astype(F32)
    for part in parts[1:]:
        last = last + part[...].astype(F32)
    hidden = 8 * D
    half = (summed.shape[1] - hidden) // 2
    squares = jnp.sum(last * last, keepdims=True)
    for at in range(0, summed.shape[1], 2 * D):
        piece = summed[:, at : min(at + 2 * D, summed.shape[1])].astype(F32)
        squares = squares + jnp.sum(piece * piece, keepdims=True)
    table[13:14, :] = jnp.broadcast_to(squares, (1, D))
    later = summed[:, hidden:].astype(F32)
    for at, value in ((0, later), (half, last)):
        width = value.shape[1] // 2
        one, two = value[:, :width], value[:, width:]
        mine[:, at : at + width] = jnp.where(core == 0, one, two)
        send[:, at : at + width] = jnp.where(core == 0, two, one)


def make_table(total, place, first, sums_a, sums_b, turn, sums_0, sums_1, summed, parts):
    rows = summed.shape[0]
    lanes = (summed.shape[1] - 8 * D + parts[0].shape[1]) // 2
    vmem = pl.BlockSpec(memory_space=pltpu.VMEM)
    half = jax.ShapeDtypeStruct((rows, lanes), F32)
    return pl.pallas_call(
        functools.partial(table_kernel, total),
        in_specs=[SMEM] + [vmem] * (7 + len(parts)),
        out_specs=[vmem] * 3,
        out_shape=[jax.ShapeDtypeStruct((16, D), F32), half, half],
        compiler_params=params(),
        cost_estimate=cost(0, 20 * rows * lanes),
        name="table",
    )(place, first, sums_a, sums_b, turn, sums_0, sums_1, summed, *parts)


def whole_rows(core, mine, theirs):
    ordered = (
        jnp.where(core == 0, mine[...], theirs[...]),
        jnp.where(core == 0, theirs[...], mine[...]),
    )
    half = D // 2
    outs = jnp.concatenate([value[:, :half] for value in ordered], axis=1)
    pieces = []
    for part in range(3):
        at = half
        for groups in SETS:
            for index in range(len(groups)):
                lane = at + (3 * index + part) * PW
                pieces += [value[:, lane : lane + PW] for value in ordered]
            at += 3 * PW * len(groups)
    return jnp.concatenate(pieces, axis=1), outs


def adam_kernel(place, table, mine, theirs, up, down, own, *refs):
    kinds = 5
    masters, firsts, seconds = (refs[i * kinds : (i + 1) * kinds] for i in range(3))
    outs = refs[3 * kinds :]
    grads = whole_rows(place[2], mine, theirs) + (up[...], down[...], own[...])
    vector_rows = masters[4].shape[0]
    vectors = table[:vector_rows, :]
    squares = jnp.sum(vectors * vectors, keepdims=True) + table[vector_rows : vector_rows + 1, :1]
    grad_norm = jnp.sqrt(squares)
    factor = jnp.minimum(1.0, clip_share * math.sqrt(PARAMS) / (grad_norm + 1e-06))
    outs[0][...] = grad_norm
    for kind in range(kinds):
        rate = vector_rate if kind == 4 else matrix_rate
        decay = 0.0 if kind == 4 else matrix_decay
        master = masters[kind][...]
        grad = grads[kind] * factor
        first_new = first_beta * firsts[kind][...] + (1.0 - first_beta) * grad
        second_new = second_beta * seconds[kind][...] + (1.0 - second_beta) * grad * grad
        first_hat = first_new * (1.0 / (1.0 - first_beta**STEP))
        second_hat = second_new * (1.0 / (1.0 - second_beta**STEP))
        step = first_hat / (jnp.sqrt(second_hat) + adam_eps)
        updated = master - rate * (step + decay * master)
        outs[1 + kind][...] = first_new
        outs[1 + kinds + kind][...] = second_new
        outs[1 + 2 * kinds + kind][...] = updated
        outs[1 + 3 * kinds + kind][...] = updated.astype(BF)


def adam(place, table, mine, theirs, up, down, own, masters, firsts, seconds):
    vmem = pl.BlockSpec(memory_space=pltpu.VMEM)
    shapes = [master.shape for master in masters]
    states = [jax.ShapeDtypeStruct(shape, F32) for shape in shapes]
    outs = [jax.ShapeDtypeStruct((1, 1), F32)] + states * 3
    outs += [jax.ShapeDtypeStruct(shape, BF) for shape in shapes]
    elements = sum(math.prod(shape) for shape in shapes)
    return pl.pallas_call(
        adam_kernel,
        in_specs=[SMEM] + [vmem] * 21,
        out_specs=[vmem] * len(outs),
        out_shape=outs,
        compiler_params=params(),
        cost_estimate=cost(20 * elements, 30 * elements),
        name="adam",
    )(place, table, mine, theirs, up, down, own, *masters, *firsts, *seconds)


def on_device(
    n_dp,
    n_fsdp,
    tokens,
    keep_slots,
    cotangent,
    project_in,
    project_out,
    expand,
    contract,
    vectors,
    first_in,
    first_out,
    first_expand,
    first_contract,
    first_vectors,
    second_in,
    second_out,
    second_expand,
    second_contract,
    second_vectors,
):
    moves = Moves(n_dp, n_fsdp)
    place, core = moves.place, moves.core
    total = n_dp * n_fsdp
    rows_in = project_in.shape[0]
    part = contract.shape[0] // QUARTERS
    owner = moves.z * n_fsdp + lax.axis_index("fsdp")
    columns = vectors.shape[1]

    shards = to_quarters(total, expand, contract, project_out)
    w_hidden = [lax.all_gather(shards[0], AXES, axis=0, tiled=True)]

    def pair_columns(value, pair):
        return [value[:, at * D + pair * PW : at * D + (pair + 1) * PW] for at in range(3)]

    low_in = project_in.astype(BF)
    low_vec = jnp.pad(vectors.astype(BF).T, ((0, 0), (0, 128 - vectors.shape[0])))
    halves = []
    for parity in range(2):
        parts = []
        for index, groups in enumerate(SETS):
            for group in groups:
                parts += pair_columns(low_in, 2 * group + parity)
            if index == 0:
                parts.append(low_vec)
        halves.append(jnp.concatenate(parts, axis=1))
    mine = jnp.where(core == 0, halves[0], halves[1])
    theirs = jnp.where(core == 0, halves[1], halves[0])
    arrived = moves.over_core(theirs)
    rows = jnp.where(
        core == 0,
        jnp.concatenate([mine, arrived], axis=0),
        jnp.concatenate([arrived, mine], axis=0),
    )
    step = 3 * PW
    cut = len(SETS[0]) * step + 128
    widths = (cut, rows.shape[1] - cut)

    count = keep_slots.shape[0]
    image_tokens = tokens.shape[0] // count
    slots = jnp.pad(keep_slots, ((0, 0), (0, PAD - KEEP)), constant_values=-4 * image_tokens)
    slots = slots[:, :, None]
    parts = moves.over_z([rows] * n_dp)
    picked = pick(place, tokens, slots)
    picked, *parts = together(picked, *parts)
    first_stack, second_stack = place_blocks(place, 0, parts, widths)
    parts = moves.over_yx([first_stack] * moves.squares)
    (first_own,) = place_blocks(place, 1, parts, widths[:1])
    first_own = first_own.reshape(D, widths[0])
    first_other = moves.over_core(first_own)
    vec, bias = vectors_of(total, first_own)

    mask = local_mask()
    first_own, first_other, second_stack = together(first_own, first_other, second_stack)
    parts = moves.over_yx([second_stack] * moves.squares)
    mixed_0, heads_0, normed_one = heads_forward(
        SETS[0], place, mask, vec, picked, first_own, first_other
    )
    grad_rows = pick(after(place, heads_0), cotangent, slots)
    mixed_0, heads_0, normed_one, grad_rows, *parts = together(
        mixed_0, heads_0, normed_one, grad_rows, *parts
    )
    (second_own,) = place_blocks(place, 1, parts, widths[1:])
    second_own = second_own.reshape(D, widths[1])
    second_other = moves.over_core(second_own)
    w_in = [(first_own, first_other), (second_own, second_other)]
    shard = after(shards[1], second_own)
    parts = moves.over_z([shard] * n_dp)
    mixed_1, heads_1 = heads_forward(SETS[1], place, mask, vec, normed_one, *w_in[1])
    mixed_1, heads_1, *parts = together(mixed_1, heads_1, *parts)
    (stack,) = place_blocks(place, 0, parts, [shard.shape[1]])
    gathered = lax.all_gather(stack, "fsdp", axis=1, tiled=True)
    w_hidden.append(gathered.reshape(D, shard.shape[1]))
    heads = [heads_0, heads_1]

    blocks = moves.square_blocks(rows_in) if rows_in % 8 == 0 else []
    attended, normed_two, out, back, gw_0, sums_0 = first_mlp(
        blocks, bias, vec, picked, grad_rows, heads, w_hidden[0]
    )
    hidden_0 = moves.over_square(gw_0, blocks)
    (
        grad_attended,
        carry,
        put_values,
        turn_sums,
        sums_1,
        gw_1,
    ) = second_mlp(
        blocks,
        place,
        bias,
        vec,
        picked,
        grad_rows,
        normed_two,
        attended,
        out,
        back,
        w_hidden[1],
    )
    hidden_1 = moves.over_square(gw_1, blocks)
    places = put_places(keep_slots, image_tokens)

    results = heads_backward(
        SETS[0], place, mask, grad_attended, normed_one, w_hidden[0], mixed_0, heads
    )
    gm_0, gw_own, gw_other, sums_a, hidden_0 = together(*results, hidden_0)
    blocks = moves.add_cores(place, [gw_own], [moves.over_core(gw_other)])
    later = moves.over_yx(blocks)
    results = heads_backward(
        SETS[1], after(place, *blocks), mask, grad_attended, normed_one, w_hidden[0], mixed_1
    )
    gm_1, gw_own, gw_other, sums_b, *later = together(*results, *later)
    blocks = moves.add_cores(place, [gw_own], [moves.over_core(gw_other)])
    last = moves.over_yx(blocks)
    hidden = [value.reshape(n_dp, rows_in, -1) for value in (hidden_0, hidden_1)]
    activations = put(after(places, *blocks), tokens, put_values)
    plane_sums = planes(after(place, activations), hidden, later)
    summed = lax.psum_scatter(
        plane_sums.reshape(n_dp * rows_in, -1), "dp", scatter_dimension=0, tiled=True
    )
    results = first_back(
        after(vec, plane_sums), picked, grad_rows, carry, [gm_0, gm_1], w_in
    )
    grad_values, first_sums, *last = together(*results, *last)
    blocks = add_blocks(place, [last], n_dp, rows_in)
    last = moves.over_z(blocks)
    input_grad = put(after(places, *blocks), cotangent, grad_values)
    input_grad, *last = together(input_grad, *last)
    table, mine, send = make_table(
        total,
        place,
        first_sums,
        sums_a,
        sums_b,
        turn_sums,
        sums_0,
        sums_1,
        summed,
        last,
    )
    parts = moves.over_z([table] * n_dp)
    theirs = moves.over_core(send)
    summed_expand, summed_contract = from_quarters(total, summed)
    theirs, summed_expand, summed_contract, *parts = together(
        theirs, summed_expand, summed_contract, *parts
    )
    table = add_parts(moves.over_yx([add_parts(parts)] * moves.squares))
    table = table + moves.over_core(table)

    own = lax.dynamic_slice_in_dim(table[:13], owner * columns, columns, axis=1)
    masters = (project_in, project_out, expand, contract, vectors)
    firsts = (first_in, first_out, first_expand, first_contract, first_vectors)
    seconds = (second_in, second_out, second_expand, second_contract, second_vectors)
    grad_norm, *updates = adam(
        place,
        table,
        mine,
        theirs,
        summed_expand,
        summed_contract,
        own,
        masters,
        firsts,
        seconds,
    )
    return (activations, input_grad, grad_norm.reshape(1), *updates)


def solution(mesh):
    split = P(AXES, None)
    columns = P(None, AXES)
    weights = (split, split, split, split, columns)
    return jax.shard_map(
        functools.partial(on_device, mesh.shape["dp"], mesh.shape["fsdp"]),
        mesh=mesh,
        in_specs=(split, split, split) + weights * 3,
        out_specs=(split, split, P()) + weights * 4,
        check_vma=False,
    )
```

```python
import functools
import math

import jax
import jax.numpy as jnp
from jax import lax
from jax.experimental import pallas as pl
from jax.experimental.pallas import tpu as pltpu
from jax.sharding import PartitionSpec as P

D = 768
HEADS = 12
HEAD_DIM = 64
KEEP_GLOBAL = 98
KEEP_LOCAL = 18
KEEP = 268
PARAMS = 7087872
STEP = 5

norm_eps = 1e-06
clip_share = 0.05
matrix_rate = 0.04
vector_rate = 0.3
matrix_decay = 0.05
first_beta = 0.5
second_beta = 0.5
adam_eps = 1e-08

AXES = ("dp", "fsdp")
BF = jnp.bfloat16
F32 = jnp.float32
NT = (((1,), (1,)), ((), ()))
TN = (((0,), (0,)), ((), ()))
PAD = -(-KEEP // 16) * 16
PAIRS = HEADS // 2
PW = 2 * HEAD_DIM
SETS = ((0,), (1, 2))
CHUNKS = 2
QUARTERS = 2 * CHUNKS
HIDDEN = 4 * D
IMAGES = 2
NEG = -1e30
SEGMENTS = (
    (0, 112, 0, KEEP_GLOBAL),
    (96, 112, KEEP_GLOBAL, 2 * KEEP_GLOBAL),
    (192, 80, 2 * KEEP_GLOBAL, KEEP),
)


def nn(left, right):
    return jnp.dot(left, right, preferred_element_type=F32)


def nt(left, right):
    return lax.dot_general(left, right, NT, preferred_element_type=F32)


def tn(left, right):
    return lax.dot_general(left, right, TN, preferred_element_type=F32)


def params(limit=60):
    return pltpu.CompilerParams(vmem_limit_bytes=limit * 2**20)


def cost(flops, moved, exps=0):
    return pl.CostEstimate(flops=int(flops), bytes_accessed=int(moved), transcendentals=int(exps))


def whole(shape):
    return pl.BlockSpec(shape, lambda *_: (0,) * len(shape))


ANY = pl.BlockSpec(memory_space=pl.ANY)
SMEM = pl.BlockSpec(memory_space=pltpu.SMEM)


def normalize(values):
    centred = values - jnp.mean(values, axis=-1, keepdims=True)
    spread = jnp.mean(centred * centred, axis=-1, keepdims=True)
    inverse = lax.rsqrt(spread + norm_eps)
    return centred * inverse, inverse


def norm_back(grad, normed, inverse, gain):
    pulled = grad * gain
    return inverse * (
        pulled
        - jnp.mean(pulled, axis=-1, keepdims=True)
        - normed * jnp.mean(pulled * normed, axis=-1, keepdims=True)
    )


def column_sum(values):
    return jnp.sum(values, axis=0, keepdims=True)


def window_start(step, image_tokens, rows, window):
    return jnp.minimum((IMAGES * image_tokens * step) // 16, (rows - window) // 16) * 16


def pick_kernel(image_tokens, rows, window, part, place, slots, source, picked):
    step = pl.program_id(0)
    shift = IMAGES * image_tokens * step - window_start(step, image_tokens, rows, window)
    for image in range(IMAGES):
        first = (image * image_tokens) // 16 * 16
        span = min(part, window - first)
        target = slots[image] + shift + image * image_tokens - first
        hot = lax.broadcasted_iota(jnp.int32, (PAD, span), 1) == target
        values = nn(hot.astype(F32).astype(BF), source[first : first + span, :])
        picked[image * PAD : (image + 1) * PAD, :] = values.astype(BF)


def pick(place, source, slots):
    rows = source.shape[0]
    count = slots.shape[0]
    image_tokens = rows // count
    window = -(-(IMAGES * image_tokens + 15) // 16) * 16
    part = -(-(image_tokens + 32) // 16) * 16
    start = functools.partial(
        window_start, image_tokens=image_tokens, rows=rows, window=window
    )
    return pl.pallas_call(
        functools.partial(pick_kernel, image_tokens, rows, window, part),
        grid=(count // IMAGES,),
        in_specs=[
            SMEM,
            pl.BlockSpec((IMAGES, PAD, 1), lambda i: (i, 0, 0)),
            pl.BlockSpec((pl.Element(window), pl.Element(D)), lambda i: (start(i), 0)),
        ],
        out_specs=pl.BlockSpec((IMAGES * PAD, D), lambda i: (i, 0)),
        out_shape=jax.ShapeDtypeStruct((count * PAD, D), BF),
        compiler_params=params(20),
        cost_estimate=cost(2 * count * PAD * window * D, 2 * rows * D + 2 * count * PAD * D),
        name="pick_rows",
    )(place, slots, source)


def local_mask():
    first, rows, low, high = SEGMENTS[2]
    slot = jnp.arange(rows) + first
    crop = jnp.where((slot >= low) & (slot < high), (slot - low) // KEEP_LOCAL, -1)
    same = (crop[:, None] == crop[None, :]) & (crop[:, None] >= 0)
    bias = jnp.where(same, 0.0, NEG).astype(F32)
    return jnp.concatenate([bias, bias], axis=1)


def lanes_of(rows):
    return lax.broadcasted_iota(jnp.int32, (rows, PW), 1) < HEAD_DIM


def split_heads(values):
    first = lanes_of(values.shape[0])
    zero = jnp.zeros_like(values)
    return jnp.concatenate(
        [jnp.where(first, values, zero), jnp.where(first, zero, values)], axis=0
    )


def join_heads(values):
    rows = values.shape[0] // 2
    return jnp.where(lanes_of(rows), values[:rows], values[rows:])


def rows_of(segment):
    return slice(segment[0], segment[0] + segment[1])


def attention(jobs, mask):
    chains = [(job, segment) for job in jobs for segment in SEGMENTS]
    scores = []
    for (query, key_rows, _), segment in chains:
        rows = rows_of(segment)
        scores.append(nt(split_heads(query[rows] * HEAD_DIM**-0.5), key_rows[rows]))
    mask = jnp.concatenate([mask[:, : mask.shape[0]]] * 2, axis=0)
    probs = []
    for (_, segment), score in zip(chains, scores):
        first, count, low, high = segment
        if low == 2 * KEEP_GLOBAL:
            score = score + mask
        else:
            slot = lax.broadcasted_iota(jnp.int32, (1, count), 1) + first
            score = jnp.where((slot >= low) & (slot < high), score, NEG)
        grown = jnp.exp(score - jnp.max(score, axis=-1, keepdims=True))
        probs.append((grown * (1.0 / jnp.sum(grown, axis=-1, keepdims=True))).astype(BF))
    parts = []
    for ((_, _, value), segment), prob in zip(chains, probs):
        parts.append(join_heads(nn(prob, value[rows_of(segment)])))
    slot = lax.broadcasted_iota(jnp.int32, (16, 1), 0)
    results = []
    for index in range(len(jobs)):
        one, two, three = parts[3 * index : 3 * index + 3]
        results.append(
            jnp.concatenate(
                [
                    one[:96],
                    jnp.where(slot + 96 < KEEP_GLOBAL, one[96:], two[:16]),
                    two[16:96],
                    jnp.where(slot + 192 < 2 * KEEP_GLOBAL, two[96:], three[:16]),
                    three[16:],
                ],
                axis=0,
            ).astype(BF)
        )
    return results


def attention_back(jobs, mask):
    chains = [(job, segment) for job in jobs for segment in SEGMENTS]
    halves, grads = [], []
    for (query, _, _, grad), segment in chains:
        first, count, low, high = segment
        rows = rows_of(segment)
        halves.append(split_heads(query[rows] * HEAD_DIM**-0.5))
        slot = lax.broadcasted_iota(jnp.int32, (count, 1), 0) + first
        kept = jnp.where((slot >= low) & (slot < high), grad[rows], jnp.zeros((), BF))
        grads.append(split_heads(kept))
    scores, grad_probs = [], []
    for ((_, key_rows, value, _), segment), half, grad in zip(chains, halves, grads):
        rows = rows_of(segment)
        scores.append(nt(key_rows[rows], half))
        grad_probs.append(nt(value[rows], grad))
    probs, grad_scores = [], []
    for (_, segment), score, pulled in zip(chains, scores, grad_probs):
        first, count, low, high = segment
        if low == 2 * KEEP_GLOBAL:
            score = score + mask
        else:
            slot = lax.broadcasted_iota(jnp.int32, (count, 1), 0) + first
            score = jnp.where((slot >= low) & (slot < high), score, NEG)
        grown = jnp.exp(score - jnp.max(score, axis=0, keepdims=True))
        prob = grown * (1.0 / jnp.sum(grown, axis=0, keepdims=True))
        weighted = jnp.sum(prob * pulled, axis=0, keepdims=True)
        probs.append(prob.astype(BF))
        grad_scores.append((prob * (pulled - weighted)).astype(BF))
    parts = [[], [], []]
    for prob, grad in zip(probs, grads):
        parts[2].append(nn(prob, grad))
    for score, half in zip(grad_scores, halves):
        parts[1].append(nn(score, half))
    for ((_, key_rows, _, _), segment), score in zip(chains, grad_scores):
        parts[0].append(join_heads(tn(score, key_rows[rows_of(segment)])) * HEAD_DIM**-0.5)
    results = []
    for index in range(len(jobs)):
        joined = []
        for part in parts:
            one, two, three = part[3 * index : 3 * index + 3]
            joined.append(
                jnp.concatenate(
                    [
                        one[:96],
                        one[96:] + two[:16],
                        two[16:96],
                        two[96:] + three[:16],
                        three[16:],
                    ],
                    axis=0,
                ).astype(BF)
            )
        results.append(joined)
    return results


def pairs_of(place, groups):
    core = place[2]
    return [2 * group + core for group in groups] + [2 * group + 1 - core for group in groups]


def lane_block(index):
    return pl.ds(pl.multiple_of(index * PW, PW), PW)


def heads_kernel(groups, place, mask, vec, source, own_w, other_w, *refs):
    if groups[0] == 0:
        mixed, heads, normed, weight = refs
        unit, _ = normalize(source[...].astype(F32))
        rows = (unit * vec[0:1, :].astype(F32) + vec[1:2, :].astype(F32)).astype(BF)
        normed[...] = rows
    else:
        mixed, heads, weight = refs
        rows = source[...]
    width = 3 * PW
    half = len(groups) * width

    @pl.when(pl.program_id(0) == 0)
    def _():
        weight[:, :half] = own_w[:, :half]
        weight[:, half:] = other_w[:, :half]

    product = nn(rows, weight[...])
    jobs, lanes = [], []
    for index, pair in enumerate(pairs_of(place, groups)):
        at = index * width
        block = lane_block(pair)
        query = (product[:, at : at + PW] + vec[2:3, block].astype(F32)).astype(BF)
        key_rows = product[:, at + PW : at + 2 * PW].astype(BF)
        value = (product[:, at + 2 * PW : at + width] + vec[3:4, block].astype(F32)).astype(BF)
        mixed[:, at : at + PW] = query
        mixed[:, at + PW : at + 2 * PW] = key_rows
        mixed[:, at + 2 * PW : at + width] = value
        for image in range(IMAGES):
            span = slice(image * PAD, (image + 1) * PAD)
            jobs.append((query[span], key_rows[span], value[span]))
            lanes.append((span, lane_block(pair - 2 * groups[0])))
    for (span, block), result in zip(lanes, attention(jobs, mask[...])):
        heads[span, block] = result


def heads_forward(groups, place, mask, vec, source, own_w, other_w):
    rows = source.shape[0]
    size = IMAGES * PAD
    width = 6 * PW * len(groups)
    wide = pl.BlockSpec((size, D), lambda i: (i, 0))
    weight = whole(own_w.shape)
    outs = [
        (pl.BlockSpec((size, width), lambda i: (i, 0)), jax.ShapeDtypeStruct((rows, width), BF)),
        (
            pl.BlockSpec((size, width // 3), lambda i: (i, 0)),
            jax.ShapeDtypeStruct((rows, width // 3), BF),
        ),
    ]
    if groups[0] == 0:
        outs.append((wide, jax.ShapeDtypeStruct((rows, D), BF)))
    return pl.pallas_call(
        functools.partial(heads_kernel, groups),
        grid=(rows // size,),
        in_specs=[SMEM, whole(mask.shape), whole((16, D)), wide, weight, weight],
        out_specs=tuple(out[0] for out in outs),
        out_shape=tuple(out[1] for out in outs),
        scratch_shapes=[pltpu.VMEM((D, width), BF)],
        compiler_params=params(32),
        cost_estimate=cost(2 * rows * D * width + rows * 1e5 * len(groups), 8 * rows * D),
        name=f"attention_{groups[0]}",
    )(place, mask, vec, source, own_w, other_w)


def heads_back_kernel(groups, steps, place, mask, grad_attended, normed, w_out, mixed, *refs):
    heads = refs[:-6] if len(refs) == 6 else refs[: -8]
    (grad_mixed, gw_own, gw_other, sums, kept_normed, kept_mixed) = refs[len(heads) :][:6]
    kept_heads, kept_grad = refs[len(heads) + 6 :] if heads else (None, None)
    step = pl.program_id(0)
    size = IMAGES * PAD
    width = 3 * PW
    half = len(groups) * width

    @pl.when(step == 0)
    def _():
        sums[...] = jnp.zeros_like(sums)

    @pl.when(step < steps)
    def _():
        rows = pl.ds(pl.multiple_of(step * size, 16), size)
        kept_normed[rows, :] = normed[...]
        incoming = grad_attended[...]
        if heads:
            kept_grad[rows, :] = incoming
            at = 0
            for part in heads:
                kept_heads[rows, at : at + part.shape[1]] = part[...]
                at += part.shape[1]
        jobs, places = [], []
        for index, pair in enumerate(pairs_of(place, groups)):
            at = index * width
            grad_heads = nt(incoming, w_out[lane_block(pair), :]).astype(BF)
            for image in range(IMAGES):
                span = slice(image * PAD, (image + 1) * PAD)
                jobs.append(
                    (
                        mixed[span, at : at + PW],
                        mixed[span, at + PW : at + 2 * PW],
                        mixed[span, at + 2 * PW : at + width],
                        grad_heads[span],
                    )
                )
                places.append((image, at))
        for (image, at), parts in zip(places, attention_back(jobs, mask[...])):
            for index, low in enumerate(parts):
                columns = slice(at + index * PW, at + (index + 1) * PW)
                grad_mixed[image * PAD : (image + 1) * PAD, columns] = low
                here = pl.ds(pl.multiple_of(step * size + image * PAD, 16), PAD)
                kept_mixed[here, columns] = low
                if index != 1:
                    sums[0:1, columns] += column_sum(low.astype(F32))

    @pl.when(step == steps)
    def _():
        first = 0
        if heads:
            first = D // 2
            core = place[2]
            own = pl.ds(pl.multiple_of(core * first, 128), first)
            other = pl.ds(pl.multiple_of((1 - core) * first, 128), first)
            gw_own[:, :first] = tn(kept_heads[...], kept_grad[:, own]).astype(BF)
            gw_other[:, :first] = tn(kept_heads[...], kept_grad[:, other]).astype(BF)
        gw_other[:, first:] = tn(kept_normed[...], kept_mixed[:, half:]).astype(BF)
        gw_own[:, first:] = tn(kept_normed[...], kept_mixed[:, :half]).astype(BF)


def heads_backward(groups, place, mask, grad_attended, normed, w_out, mixed, heads=()):
    rows, width = mixed.shape
    size = IMAGES * PAD
    steps = rows // size
    last = steps - 1

    def block(width):
        return pl.BlockSpec((size, width), lambda i: (jnp.minimum(i, last), 0))

    weight = (D, width // 2 + (D // 2 if heads else 0))
    kept = [D, width] + [D, D] * bool(heads)
    return pl.pallas_call(
        functools.partial(heads_back_kernel, groups, steps),
        grid=(steps + 1,),
        in_specs=[SMEM, whole(mask.shape), block(D), block(D)]
        + [pl.BlockSpec((D, D), lambda i: (0, w_out.shape[1] // D - 1)), block(width)]
        + [block(part.shape[1]) for part in heads],
        out_specs=(block(width), whole(weight), whole(weight), whole((8, width))),
        out_shape=(
            jax.ShapeDtypeStruct((rows, width), BF),
            jax.ShapeDtypeStruct(weight, BF),
            jax.ShapeDtypeStruct(weight, BF),
            jax.ShapeDtypeStruct((8, width), F32),
        ),
        scratch_shapes=[pltpu.VMEM((rows, lanes), BF) for lanes in kept],
        compiler_params=params(60 if heads else 40),
        cost_estimate=cost(
            2 * rows * D * (width // 3 + width) + rows * 3e5 * len(groups), 12 * rows * D
        ),
        name=f"attention_back_{groups[0]}",
    )(place, mask, grad_attended, normed, w_out, mixed, *heads)


TILE = 256


def gelu_and_slope(values):
    below = 0.5 + 0.5 * lax.erf(values * math.sqrt(0.5))
    bell = jnp.exp(-0.5 * values * values) * (1.0 / math.sqrt(2.0 * math.pi))
    return values * below, below + values * bell


def alternating(bias, weights, make_left, right, rows, kept_active, kept_before, sums):
    result = pulled = 0.0
    grad = nt(right, weights[1][...])
    left = make_left()
    before = nn(left, weights[0][...])
    for half in range(2):
        kept = slice(half * D, (half + 1) * D)
        active, slope = gelu_and_slope(before + bias[half])
        low = (grad * slope).astype(BF)
        active = active.astype(BF)
        kept_active[rows, kept] = active
        kept_before[rows, kept] = low
        if half == 0:
            before, grad = nn(left, weights[2][...]), nt(right, weights[3][...])
        sums[half] += column_sum(low.astype(F32))
        result = result + nn(active, weights[2 * half + 1][...])
        pulled = pulled + nt(low, weights[2 * half][...])
    return result, pulled


def both_ways(chunk, bias, weights, left, right, rows, kept_active, kept_before, sums):
    tiles = D // TILE
    for half in range(2):
        up, down = weights[2 * half], weights[2 * half + 1]
        for tile in range(tiles):
            columns = slice(tile * TILE, (tile + 1) * TILE)
            kept = slice(half * D + tile * TILE, half * D + (tile + 1) * TILE)
            before = nn(left, up[:, columns]) + bias[2 * chunk + half, :, columns]
            active, slope = gelu_and_slope(before)
            kept_active[rows, kept] = active.astype(BF)
            low = (nt(right, down[columns, :]) * slope).astype(BF)
            kept_before[rows, kept] = low
            sums[half, :, columns] += column_sum(low.astype(F32))
    result = nn(kept_active[rows, :D], weights[1][...])
    result += nn(kept_active[rows, D:], weights[3][...])
    pulled = nt(kept_before[rows, :D], weights[0][...])
    pulled += nt(kept_before[rows, D:], weights[2][...])
    return result, pulled


def hidden_grads(tile, blocks, kept, gw):
    kept_normed, kept_grad, kept_active, kept_before = kept

    def ordered(value):
        if blocks:
            value = jnp.concatenate([value[at : at + size] for at, size in blocks], axis=0)
        return value.astype(BF)

    for half in range(2):
        columns = slice(half * D, (half + 1) * D)

        @pl.when(tile == 2 * half)
        def _():
            gw[...] = ordered(tn(kept_normed[...], kept_before[:, columns]))

        @pl.when(tile == 2 * half + 1)
        def _():
            gw[...] = ordered(tn(kept_active[:, columns], kept_grad[...]))


def routed_rows(picked, grads, vec):
    inputs = picked[...].astype(F32)
    grad_rows = grads[...].astype(F32)
    routed = jnp.sum(inputs * vec[8:9, :].astype(F32), axis=-1, keepdims=True)
    return inputs, grad_rows, routed, routed * grad_rows


def first_mlp_kernel(steps, size, blocks, bias, vec, w_out, picked, grads, *refs):
    heads = refs[: len(SETS)]
    refs = refs[len(SETS) :]
    weights = refs[:4]
    attended, normed, out, back, gw, sums = refs[4:10]
    kept = refs[10:]
    kept_normed, kept_grad, kept_active, kept_before = kept
    step = pl.program_id(0)

    @pl.when(step == 0)
    def _():
        sums[...] = jnp.zeros_like(sums)

    @pl.when(step < steps)
    def _():
        rows = pl.ds(pl.multiple_of(step * size, 16), size)
        inputs, _, _, grad_branch = routed_rows(picked, grads, vec)
        right = grad_branch.astype(BF)
        joined = jnp.concatenate([part[...] for part in heads], axis=1)
        mixed = nn(joined, w_out[...]) + vec[4:5, :].astype(F32)
        attended[...] = mixed
        kept_grad[rows, :] = right

        def make_left():
            unit, _ = normalize(inputs + mixed)
            left = (unit * vec[5:6, :].astype(F32) + vec[6:7, :].astype(F32)).astype(BF)
            normed[...] = left
            kept_normed[rows, :] = left
            return left

        out[...], back[...] = alternating(
            bias, weights, make_left, right, rows, kept_active, kept_before, sums
        )

    @pl.when(step >= steps)
    def _():
        hidden_grads(step - steps, blocks, kept, gw)


def second_mlp_kernel(
    steps, size, blocks, place, bias, vec, picked, grads, normed, attended, out, back, *refs
):
    weights = refs[:4]
    (grad_attended, carry, values, turn_sums, sums, gw) = refs[4:10]
    kept = refs[10:]
    kept_normed, kept_grad, kept_active, kept_before = kept
    step = pl.program_id(0)

    @pl.when(step == 0)
    def _():
        sums[...] = jnp.zeros_like(sums)
        turn_sums[...] = jnp.zeros_like(turn_sums)

    @pl.when(step < steps)
    def _():
        rows = pl.ds(pl.multiple_of(step * size, 16), size)
        inputs, grad_rows, routed, grad_branch = routed_rows(picked, grads, vec)
        left = normed[...]
        right = grad_branch.astype(BF)
        kept_normed[rows, :] = left
        kept_grad[rows, :] = right
        result, pulled = both_ways(
            1, bias, weights, left, right, rows, kept_active, kept_before, sums
        )
        pulled += back[...]
        router = vec[8:9, :].astype(F32)
        mixed = attended[...]
        branch = mixed + (result + out[...]) + vec[7:8, :].astype(F32)
        values[...] = (inputs + routed * branch).astype(BF)
        grad_routed = jnp.sum(grad_rows * branch, axis=-1, keepdims=True)
        unit, inverse = normalize(inputs + mixed)
        residual = norm_back(pulled, unit, inverse, vec[5:6, :].astype(F32))
        low = (grad_branch + residual).astype(BF)
        grad_attended[...] = low
        carry[...] = residual + grad_routed * router
        turn_sums[0:1, :] += column_sum(low.astype(F32))
        turn_sums[1:2, :] += column_sum(pulled * unit)
        turn_sums[2:3, :] += column_sum(pulled)
        turn_sums[3:4, :] += column_sum(right.astype(F32))
        turn_sums[4:5, :] += column_sum(inputs * grad_routed)

    @pl.when(step >= steps)
    def _():
        hidden_grads(step - steps, blocks, kept, gw)


def mlp_specs(chunk, rows):
    size = PAD
    steps = rows // size
    last = steps - 1

    def wide(width=D):
        return pl.BlockSpec((size, width), lambda i: (jnp.minimum(i, last), 0))

    weights = [
        pl.BlockSpec((D, D), lambda i, at=at: (0, at), pipeline_mode=pl.Buffered(1))
        for at in (0, 2, 1, 3)
    ]

    def gw_block(i):
        tile = jnp.clip(i - steps, 0, 3)
        return (0, tile // 2 + 2 * (tile % 2))

    scratch = [
        pltpu.VMEM((rows, D), BF),
        pltpu.VMEM((rows, D), BF),
        pltpu.VMEM((rows, 2 * D), BF),
        pltpu.VMEM((rows, 2 * D), BF),
    ]
    return size, steps, 4, wide, weights, pl.BlockSpec((D, D), gw_block), scratch


def first_mlp(blocks, bias, vec, picked, grads, heads, weights):
    rows = picked.shape[0]
    size, steps, tiles, wide, weight_specs, gw, scratch = mlp_specs(0, rows)
    total = jax.ShapeDtypeStruct((rows, D), F32)
    return pl.pallas_call(
        functools.partial(first_mlp_kernel, steps, size, blocks),
        grid=(steps + tiles,),
        in_specs=[whole(bias.shape), whole((16, D))]
        + [pl.BlockSpec((D, D), lambda i: (0, 4), pipeline_mode=pl.Buffered(1))]
        + [wide()] * 2
        + [wide(part.shape[1]) for part in heads]
        + weight_specs,
        out_specs=(wide(),) * 4 + (gw, whole((2, 1, D))),
        out_shape=(
            total,
            jax.ShapeDtypeStruct((rows, D), BF),
            total,
            total,
            jax.ShapeDtypeStruct((D, 4 * D), BF),
            jax.ShapeDtypeStruct((2, 1, D), F32),
        ),
        scratch_shapes=scratch,
        compiler_params=params(),
        cost_estimate=cost(26 * rows * D * D, 30 * rows * D, 4 * rows * D),
        name="feed_forward_0",
    )(bias, vec, weights, picked, grads, *heads, *[weights] * 4)


def second_mlp(blocks, place, bias, vec, picked, grads, normed, attended, out, back, weights):
    rows = picked.shape[0]
    size, steps, tiles, wide, weight_specs, gw, scratch = mlp_specs(1, rows)
    low = jax.ShapeDtypeStruct((rows, D), BF)
    return pl.pallas_call(
        functools.partial(second_mlp_kernel, steps, size, blocks),
        grid=(steps + tiles,),
        in_specs=[SMEM, whole(bias.shape), whole((16, D))]
        + [wide()] * 6
        + weight_specs,
        out_specs=(wide(), wide(), wide(), whole((8, D)), whole((2, 1, D)), gw),
        out_shape=(
            low,
            jax.ShapeDtypeStruct((rows, D), F32),
            low,
            jax.ShapeDtypeStruct((8, D), F32),
            jax.ShapeDtypeStruct((2, 1, D), F32),
            jax.ShapeDtypeStruct((D, 4 * D), BF),
        ),
        scratch_shapes=scratch,
        compiler_params=params(),
        cost_estimate=cost(26 * rows * D * D, 40 * rows * D, 4 * rows * D),
        name="feed_forward_1",
    )(place, bias, vec, picked, grads, normed, attended, out, back, *[weights] * 4)


def first_back_kernel(count, vec, picked, grads, carry, *refs):
    mixed = refs[:count]
    weights = refs[count : 3 * count]
    values, sums = refs[3 * count : 3 * count + 2]
    kept = refs[3 * count + 2 :]

    @pl.when(pl.program_id(0) == 0)
    def _():
        sums[...] = jnp.zeros_like(sums)
        for index in range(count):
            half = mixed[index].shape[1] // 2
            kept[index][:, :half] = weights[2 * index][:, :half]
            kept[index][:, half:] = weights[2 * index + 1][:, :half]

    pulled = nt(mixed[0][...], kept[0][...])
    for index in range(1, count):
        pulled += nt(mixed[index][...], kept[index][...])
    unit, inverse = normalize(picked[...].astype(F32))
    grad = norm_back(pulled, unit, inverse, vec[0:1, :].astype(F32))
    values[...] = (grads[...].astype(F32) + grad + carry[...]).astype(BF)
    sums[0:1, :] += column_sum(pulled * unit)
    sums[1:2, :] += column_sum(pulled)


def first_back(vec, picked, grads, carry, mixed, weights):
    rows = picked.shape[0]
    size = 2 * PAD
    wide = pl.BlockSpec((size, D), lambda i: (i, 0))
    flat = [weight for pair in weights for weight in pair]
    return pl.pallas_call(
        functools.partial(first_back_kernel, len(mixed)),
        grid=(rows // size,),
        in_specs=[whole((16, D)), wide, wide, wide]
        + [pl.BlockSpec((size, part.shape[1]), lambda i: (i, 0)) for part in mixed]
        + [whole(weight.shape) for weight in flat],
        out_specs=(wide, whole((8, D))),
        out_shape=(jax.ShapeDtypeStruct((rows, D), BF), jax.ShapeDtypeStruct((8, D), F32)),
        scratch_shapes=[pltpu.VMEM((D, part.shape[1]), BF) for part in mixed],
        compiler_params=params(44),
        cost_estimate=cost(6 * rows * D * D, 16 * rows * D),
        name="first_norm_back",
    )(vec, picked, grads, carry, *mixed, *flat)


def put_kernel(span, places, source, value, after, out, both):
    width = places.shape[2]
    for image in range(IMAGES):
        rows = slice(image * span, (image + 1) * span)
        both[:PAD, :] = value[image * PAD : (image + 1) * PAD, :]
        if image + 1 < IMAGES:
            both[PAD:, :] = value[(image + 1) * PAD : (image + 1) * PAD + 16, :]
        else:
            both[PAD:, :] = after[...]
        same = lax.broadcasted_iota(jnp.int32, (span, width), 0) == places[image]
        hot = same.astype(F32)
        kept = jnp.max(hot, axis=-1, keepdims=True) > 0.5
        moved = nn(hot.astype(BF), both[...])
        out[rows, :] = jnp.where(kept, moved, source[rows, :].astype(F32)).astype(BF)


def put(places, source, values):
    rows = source.shape[0]
    count = places.shape[0]
    span = -(-(rows // count) // 16) * 16
    steps = count // IMAGES
    block = pl.BlockSpec((IMAGES * span, D), lambda i: (i, 0))
    return pl.pallas_call(
        functools.partial(put_kernel, span),
        grid=(steps,),
        in_specs=[
            pl.BlockSpec((IMAGES, 1, places.shape[2]), lambda i: (i, 0, 0)),
            block,
            pl.BlockSpec((IMAGES * PAD, D), lambda i: (i, 0)),
            pl.BlockSpec(
                (16, D), lambda i: (jnp.minimum(i + 1, steps - 1) * (IMAGES * PAD // 16), 0)
            ),
        ],
        out_specs=block,
        out_shape=jax.ShapeDtypeStruct((rows, D), BF),
        scratch_shapes=[pltpu.VMEM((PAD + 16, D), BF)],
        compiler_params=params(24),
        cost_estimate=cost(2 * rows * D * (PAD + 16), 6 * rows * D),
        name="put_rows",
    )(places, source, values, values)


def put_places(keep_slots, image_tokens):
    count = keep_slots.shape[0]
    span = -(-image_tokens // 16) * 16
    image = jnp.arange(count, dtype=jnp.int32)[:, None]
    own = keep_slots + image * (image_tokens - span)
    following = jnp.concatenate([keep_slots[1:, :16], jnp.full((1, 16), -span, jnp.int32)], axis=0)
    following = following + (image + 1) * image_tokens - image * span
    following = jnp.where(image < count - 1, following, -1)
    gap = jnp.full((count, PAD - KEEP), -1, jnp.int32)
    return jnp.concatenate([own, gap, following], axis=1)[:, None, :]


class Moves:
    def __init__(self, n_dp, n_fsdp):
        self.n_dp = n_dp
        self.n_fsdp = n_fsdp
        self.squares = n_fsdp // 2
        outer = lax.axis_index("dp")
        inner = lax.axis_index("fsdp")
        self.z = outer
        self.yx = inner // 2
        self.core = inner % 2
        self.place = jnp.stack([self.z, self.yx, self.core]).astype(jnp.int32)

    def swap(self, value, mask):
        total = self.n_dp * self.n_fsdp
        return lax.ppermute(value, AXES, [(i, i ^ mask) for i in range(total)])

    def over_z(self, values):
        return [values[0]] + [self.swap(values[k], k * self.n_fsdp) for k in range(1, self.n_dp)]

    def over_yx(self, values):
        return [values[0]] + [self.swap(values[k], 2 * k) for k in range(1, self.squares)]

    def over_core(self, value):
        return self.swap(value, 1)

    def square_blocks(self, size):
        return [
            ((z * self.n_fsdp + inner) * size, size)
            for inner in range(self.n_fsdp)
            for z in range(self.n_dp)
        ]

    def over_square(self, value, ordered):
        rows, n = value.shape
        if not ordered:
            value = value.reshape(self.n_dp, self.n_fsdp, -1, n).transpose(1, 0, 2, 3)
        value = value.reshape(rows, n)
        return lax.psum_scatter(value, "fsdp", scatter_dimension=0, tiled=True)

    def by_chip(self, value):
        chips = self.n_dp * self.squares
        return value.reshape(self.n_dp, self.squares, value.shape[0] // chips, value.shape[1])

    def add_cores(self, place, keeps, arrived):
        keeps = [self.by_chip(value) for value in keeps]
        arrived = [self.by_chip(value) for value in arrived]
        return add_pairs(place, keeps, arrived, self.squares)


def add_parts(parts):
    total = parts[0].astype(F32)
    for part in parts[1:]:
        total = total + part.astype(F32)
    return total


def together(*values):
    return lax.optimization_barrier(values)


def after(value, *others):
    return lax.optimization_barrier((value, *others))[0]


def place_kernel(axis, count, cuts, place, *refs):
    outs = refs[count:]
    me = place[axis]
    for k in range(count):
        for (first, width), out in zip(cuts, outs):
            if axis == 0:
                out[me ^ k] = refs[k][:, first : first + width]
            else:
                out[:, me ^ k] = refs[k][...]


def place_blocks(place, axis, blocks, widths):
    count = len(blocks)
    cuts, at = [], 0
    for width in widths:
        cuts.append((at, width))
        at += width
    shape = blocks[0].shape[:-1]
    shape = shape[:axis] + (count,) + shape[axis:]
    vmem = pl.BlockSpec(memory_space=pltpu.VMEM)
    return pl.pallas_call(
        functools.partial(place_kernel, axis, count, cuts),
        in_specs=[SMEM] + [vmem] * count,
        out_specs=[vmem] * len(widths),
        out_shape=[jax.ShapeDtypeStruct(shape + (width,), BF) for width in widths],
        compiler_params=params(24),
        cost_estimate=cost(0, 4 * math.prod(shape) * at),
        name="place_blocks",
    )(place, *blocks)


def add_pairs_kernel(parts, squares, place, *refs):
    outs = refs[2 * parts * squares :]
    at = 0
    for part in range(parts):
        for k in range(squares):
            index = part * squares + k
            left, right = refs[index], refs[parts * squares + index]
            width = left.shape[3]
            total = left[...].astype(F32) + right[...].astype(F32)
            outs[k][:, :, at : at + width] = total[:, 0].astype(BF)
        at += width


def add_pairs(place, keeps, arrived, squares):
    specs, left, right = [], [], []
    n_dp, _, m, _ = keeps[0].shape
    for keep, other in zip(keeps, arrived):
        for k in range(squares):
            specs.append(
                pl.BlockSpec(
                    (n_dp, 1, m, keep.shape[3]), lambda i, place, k=k: (0, place[1] ^ k, 0, 0)
                )
            )
            left.append(keep)
            right.append(other)
    shape = (n_dp, m, sum(keep.shape[3] for keep in keeps))
    return pl.pallas_call(
        functools.partial(add_pairs_kernel, len(keeps), squares),
        grid_spec=pltpu.PrefetchScalarGridSpec(
            num_scalar_prefetch=1,
            grid=(1,),
            in_specs=specs + specs,
            out_specs=[pl.BlockSpec(shape, lambda i, place: (0, 0, 0))] * squares,
        ),
        out_shape=[jax.ShapeDtypeStruct(shape, BF)] * squares,
        compiler_params=params(24),
        cost_estimate=cost(0, 6 * squares * math.prod(shape)),
        name="add_cores",
    )(place, *left, *right)


def add_blocks_kernel(count, rows, sizes, place, *refs):
    outs = refs[count * sum(sizes) :]
    at = 0
    for index in range(count):
        lane = 0
        for terms in sizes:
            total = refs[at][0].astype(F32)
            for term in range(1, terms):
                total = total + refs[at + term][0].astype(F32)
            at += terms
            for first in range(0, total.shape[0], rows):
                width = total.shape[1]
                outs[index][:, lane : lane + width] = total[first : first + rows].astype(BF)
                lane += width


def add_blocks(place, groups, n_dp, rows):
    specs, operands, lanes = [], [], 0
    for arrays in groups:
        _, m, n = arrays[0].shape
        lanes += n * (m // rows)
    for k in range(n_dp):
        for arrays in groups:
            _, m, n = arrays[0].shape
            spec = pl.BlockSpec((1, m, n), lambda i, place, k=k: (place[0] ^ k, 0, 0))
            specs += [spec] * len(arrays)
            operands += arrays
    sizes = [len(arrays) for arrays in groups]
    return pl.pallas_call(
        functools.partial(add_blocks_kernel, n_dp, rows, sizes),
        grid_spec=pltpu.PrefetchScalarGridSpec(
            num_scalar_prefetch=1,
            grid=(1,),
            in_specs=specs,
            out_specs=[pl.BlockSpec((rows, lanes), lambda i, place: (0, 0))] * n_dp,
        ),
        out_shape=[jax.ShapeDtypeStruct((rows, lanes), BF)] * n_dp,
        compiler_params=params(24),
        cost_estimate=cost(0, 4 * n_dp * rows * lanes * max(sizes)),
        name="add_squares",
    )(place, *operands)


def planes_kernel(place, *refs):
    out = refs[-1]
    lane = 0
    for ref in refs[:-1]:
        out[:, :, lane : lane + ref.shape[2]] = ref[...]
        lane += ref.shape[2]


def planes(place, arrays):
    n_dp, rows, _ = arrays[0].shape
    lanes = sum(value.shape[2] for value in arrays)
    vmem = pl.BlockSpec(memory_space=pltpu.VMEM)
    return pl.pallas_call(
        planes_kernel,
        in_specs=[SMEM] + [vmem] * len(arrays),
        out_specs=vmem,
        out_shape=jax.ShapeDtypeStruct((n_dp, rows, lanes), BF),
        compiler_params=params(),
        cost_estimate=cost(0, 4 * n_dp * rows * lanes),
        name="planes",
    )(place, *arrays)


def quarters_kernel(total, part, up, down, project_out, *outs):
    outs[0][:, 4 * D :] = project_out[...].astype(BF)
    for chunk, out in enumerate(outs):
        for half in range(2):
            quarter = 2 * chunk + half
            pieces = [
                up[:, (owner * QUARTERS + quarter) * part : (owner * QUARTERS + quarter + 1) * part]
                for owner in range(total)
            ]
            out[:, half * D : (half + 1) * D] = jnp.concatenate(pieces, axis=1).astype(BF)
            rows = slice(quarter * part, (quarter + 1) * part)
            out[:, (2 + half) * D : (3 + half) * D] = down[rows, :].astype(BF)


def to_quarters(total, up, down, project_out):
    rows = up.shape[0]
    part = down.shape[0] // QUARTERS
    shape = jax.ShapeDtypeStruct((rows, 4 * D), BF)
    if part % 8:
        ups = up.astype(BF).reshape(rows, total, QUARTERS, part).transpose(2, 0, 1, 3)
        ups = ups.reshape(QUARTERS, rows, D)
        downs = down.astype(BF).reshape(QUARTERS, part, D)
        first = [ups[0], ups[1], downs[0], downs[1], project_out.astype(BF)]
        second = [ups[2], ups[3], downs[2], downs[3]]
        return [jnp.concatenate(first, axis=1), jnp.concatenate(second, axis=1)]
    vmem = pl.BlockSpec(memory_space=pltpu.VMEM)
    return pl.pallas_call(
        functools.partial(quarters_kernel, total, part),
        in_specs=[vmem] * 3,
        out_specs=[vmem] * 2,
        out_shape=[jax.ShapeDtypeStruct((rows, 5 * D), BF), shape],
        compiler_params=params(),
        cost_estimate=cost(0, 12 * rows * 4 * D),
        name="to_quarters",
    )(up, down, project_out)


def hidden_kernel(total, part, value, up, down):
    pieces = []
    for owner in range(total):
        for quarter in range(QUARTERS):
            at = (4 * (quarter // 2) + quarter % 2) * D + owner * part
            pieces.append(value[:, at : at + part].astype(F32))
    up[...] = jnp.concatenate(pieces, axis=1)
    for quarter in range(QUARTERS):
        at = (4 * (quarter // 2) + 2 + quarter % 2) * D
        down[quarter * part : (quarter + 1) * part, :] = value[:, at : at + D].astype(F32)


def from_quarters(total, value):
    rows = value.shape[0]
    part = D // total
    if part % 8:
        quarters = value[:, : 8 * D].astype(F32).reshape(rows, CHUNKS, 2, 2, D)
        ups = quarters[:, :, 0].reshape(rows, QUARTERS, total, part).transpose(0, 2, 1, 3)
        downs = quarters[:, :, 1].reshape(rows, QUARTERS, D).transpose(1, 0, 2)
        return ups.reshape(rows, HIDDEN), downs.reshape(QUARTERS * part, D)
    vmem = pl.BlockSpec(memory_space=pltpu.VMEM)
    return pl.pallas_call(
        functools.partial(hidden_kernel, total, part),
        in_specs=[vmem],
        out_specs=[vmem] * 2,
        out_shape=[
            jax.ShapeDtypeStruct((rows, HIDDEN), F32),
            jax.ShapeDtypeStruct((QUARTERS * part, D), F32),
        ],
        compiler_params=params(),
        cost_estimate=cost(0, 6 * rows * 8 * D),
        name="from_quarters",
    )(value)


def unit_pieces(total):
    part = D // total
    for quarter in range(QUARTERS):
        for owner in range(total):
            first = (owner * QUARTERS + quarter) * part
            yield quarter, owner * part, first // D, first % D


def vectors_kernel(total, source, vec, bias):
    rows = source[...].astype(F32).T[:16, :]
    vec[...] = rows.astype(BF)
    part = D // total
    pieces = [[] for _ in range(QUARTERS)]
    for quarter, _, row, lane in unit_pieces(total):
        pieces[quarter].append(rows[9 + row : 10 + row, lane : lane + part])
    for quarter in range(QUARTERS):
        bias[quarter] = jnp.concatenate(pieces[quarter], axis=1)


def vectors_of(total, gathered):
    if D // total % 8:
        vec = gathered[:, -128:-112].T
        bias = vec[9:13].astype(F32).reshape(total, QUARTERS, -1).transpose(1, 0, 2)
        return vec, bias.reshape(QUARTERS, 1, D)
    return pl.pallas_call(
        functools.partial(vectors_kernel, total),
        grid=(1,),
        in_specs=[pl.BlockSpec((D, 128), lambda i: (0, gathered.shape[1] // 128 - 1))],
        out_specs=[whole((16, D)), whole((QUARTERS, 1, D))],
        out_shape=[
            jax.ShapeDtypeStruct((16, D), BF),
            jax.ShapeDtypeStruct((QUARTERS, 1, D), F32),
        ],
        compiler_params=params(16),
        cost_estimate=cost(0, 4 * D * 128),
        name="vectors",
    )(gathered)


def pair_sums(core, sums, groups, part):
    width = 3 * PW
    half = len(groups) * width
    pieces = []
    for index in range(len(groups)):
        at = index * width + part * PW
        own = sums[0:1, at : at + PW]
        other = sums[0:1, half + at : half + at + PW]
        pieces += [jnp.where(core == 0, own, other), jnp.where(core == 0, other, own)]
    return pieces


def table_kernel(total, place, *refs):
    (first, sums_a, sums_b, turn, sums_0, sums_1, summed) = refs[:7]
    parts, (table, mine, send) = refs[7:-3], refs[-3:]
    core = place[2]
    table[...] = jnp.zeros_like(table)
    table[0:2, :] = first[0:2, :]
    for row, part in ((2, 0), (3, 2)):
        pieces = pair_sums(core, sums_a, SETS[0], part) + pair_sums(core, sums_b, SETS[1], part)
        table[row : row + 1, :] = jnp.concatenate(pieces, axis=1)
    table[4:9, :] = turn[0:5, :]
    size = D // total
    pieces = sorted((row, lane, quarter, at) for quarter, at, row, lane in unit_pieces(total))
    for row in range(4):
        values = []
        for _, _, quarter, at in pieces[row * len(pieces) // 4 : (row + 1) * len(pieces) // 4]:
            source = sums_1 if quarter // 2 else sums_0
            values.append(source[quarter % 2][:, at : at + size])
        table[9 + row : 10 + row, :] = jnp.concatenate(values, axis=1)
    last = parts[0][...].astype(F32)
    for part in parts[1:]:
        last = last + part[...].astype(F32)
    squares = jnp.sum(last * last, keepdims=True)
    for at in range(0, summed.shape[1], 2 * D):
        piece = summed[:, at : min(at + 2 * D, summed.shape[1])].astype(F32)
        squares = squares + jnp.sum(piece * piece, keepdims=True)
    table[13:14, :] = jnp.broadcast_to(squares, (1, D))
    width = last.shape[1] // 2
    one, two = last[:, :width], last[:, width:]
    mine[...] = jnp.where(core == 0, one, two)
    send[...] = jnp.where(core == 0, two, one)


def make_table(total, place, first, sums_a, sums_b, turn, sums_0, sums_1, summed, parts):
    rows = summed.shape[0]
    lanes = parts[0].shape[1] // 2
    vmem = pl.BlockSpec(memory_space=pltpu.VMEM)
    half = jax.ShapeDtypeStruct((rows, lanes), F32)
    return pl.pallas_call(
        functools.partial(table_kernel, total),
        in_specs=[SMEM] + [vmem] * (7 + len(parts)),
        out_specs=[vmem] * 3,
        out_shape=[jax.ShapeDtypeStruct((16, D), F32), half, half],
        compiler_params=params(),
        cost_estimate=cost(0, 20 * rows * lanes),
        name="table",
    )(place, first, sums_a, sums_b, turn, sums_0, sums_1, summed, *parts)


def whole_rows(core, mine, theirs):
    ordered = (
        jnp.where(core == 0, mine[...], theirs[...]),
        jnp.where(core == 0, theirs[...], mine[...]),
    )
    half = D // 2
    outs = jnp.concatenate([value[:, :half] for value in ordered], axis=1)
    pieces = []
    for part in range(3):
        at = half
        for groups in SETS:
            for index in range(len(groups)):
                lane = at + (3 * index + part) * PW
                pieces += [value[:, lane : lane + PW] for value in ordered]
            at += 3 * PW * len(groups)
    return jnp.concatenate(pieces, axis=1), outs


def adam_kernel(place, table, mine, theirs, up, down, own, *refs):
    kinds = 5
    masters, firsts, seconds = (refs[i * kinds : (i + 1) * kinds] for i in range(3))
    outs = refs[3 * kinds :]
    grads = whole_rows(place[2], mine, theirs) + (up[...], down[...], own[...])
    vector_rows = masters[4].shape[0]
    vectors = table[:vector_rows, :]
    squares = jnp.sum(vectors * vectors, keepdims=True) + table[vector_rows : vector_rows + 1, :1]
    grad_norm = jnp.sqrt(squares)
    factor = jnp.minimum(1.0, clip_share * math.sqrt(PARAMS) / (grad_norm + 1e-06))
    outs[0][...] = grad_norm
    for kind in range(kinds):
        rate = vector_rate if kind == 4 else matrix_rate
        decay = 0.0 if kind == 4 else matrix_decay
        master = masters[kind][...]
        grad = grads[kind] * factor
        first_new = first_beta * firsts[kind][...] + (1.0 - first_beta) * grad
        second_new = second_beta * seconds[kind][...] + (1.0 - second_beta) * grad * grad
        first_hat = first_new * (1.0 / (1.0 - first_beta**STEP))
        second_hat = second_new * (1.0 / (1.0 - second_beta**STEP))
        step = first_hat / (jnp.sqrt(second_hat) + adam_eps)
        updated = master - rate * (step + decay * master)
        outs[1 + kind][...] = first_new
        outs[1 + kinds + kind][...] = second_new
        outs[1 + 2 * kinds + kind][...] = updated
        outs[1 + 3 * kinds + kind][...] = updated.astype(BF)


def adam(place, table, mine, theirs, up, down, own, masters, firsts, seconds):
    vmem = pl.BlockSpec(memory_space=pltpu.VMEM)
    shapes = [master.shape for master in masters]
    states = [jax.ShapeDtypeStruct(shape, F32) for shape in shapes]
    outs = [jax.ShapeDtypeStruct((1, 1), F32)] + states * 3
    outs += [jax.ShapeDtypeStruct(shape, BF) for shape in shapes]
    elements = sum(math.prod(shape) for shape in shapes)
    return pl.pallas_call(
        adam_kernel,
        in_specs=[SMEM] + [vmem] * 21,
        out_specs=[vmem] * len(outs),
        out_shape=outs,
        compiler_params=params(),
        cost_estimate=cost(20 * elements, 30 * elements),
        name="adam",
    )(place, table, mine, theirs, up, down, own, *masters, *firsts, *seconds)


def on_device(
    n_dp,
    n_fsdp,
    tokens,
    keep_slots,
    cotangent,
    project_in,
    project_out,
    expand,
    contract,
    vectors,
    first_in,
    first_out,
    first_expand,
    first_contract,
    first_vectors,
    second_in,
    second_out,
    second_expand,
    second_contract,
    second_vectors,
):
    moves = Moves(n_dp, n_fsdp)
    place, core = moves.place, moves.core
    total = n_dp * n_fsdp
    rows_in = project_in.shape[0]
    part = contract.shape[0] // QUARTERS
    owner = moves.z * n_fsdp + lax.axis_index("fsdp")
    columns = vectors.shape[1]

    shards = to_quarters(total, expand, contract, project_out)
    w_hidden = [lax.all_gather(shards[0], AXES, axis=0, tiled=True)]

    def pair_columns(value, pair):
        return [value[:, at * D + pair * PW : at * D + (pair + 1) * PW] for at in range(3)]

    low_in = project_in.astype(BF)
    low_vec = jnp.pad(vectors.astype(BF).T, ((0, 0), (0, 128 - vectors.shape[0])))
    halves = []
    for parity in range(2):
        parts = []
        for index, groups in enumerate(SETS):
            for group in groups:
                parts += pair_columns(low_in, 2 * group + parity)
            if index == 0:
                parts.append(low_vec)
        halves.append(jnp.concatenate(parts, axis=1))
    mine = jnp.where(core == 0, halves[0], halves[1])
    theirs = jnp.where(core == 0, halves[1], halves[0])
    arrived = moves.over_core(theirs)
    rows = jnp.where(
        core == 0,
        jnp.concatenate([mine, arrived], axis=0),
        jnp.concatenate([arrived, mine], axis=0),
    )
    step = 3 * PW
    cut = len(SETS[0]) * step + 128
    widths = (cut, rows.shape[1] - cut)

    count = keep_slots.shape[0]
    image_tokens = tokens.shape[0] // count
    slots = jnp.pad(keep_slots, ((0, 0), (0, PAD - KEEP)), constant_values=-4 * image_tokens)
    slots = slots[:, :, None]
    parts = moves.over_z([rows] * n_dp)
    picked = pick(place, tokens, slots)
    picked, *parts = together(picked, *parts)
    first_stack, second_stack = place_blocks(place, 0, parts, widths)
    parts = moves.over_yx([first_stack] * moves.squares)
    (first_own,) = place_blocks(place, 1, parts, widths[:1])
    first_own = first_own.reshape(D, widths[0])
    first_other = moves.over_core(first_own)
    vec, bias = vectors_of(total, first_own)

    mask = local_mask()
    first_own, first_other, second_stack = together(first_own, first_other, second_stack)
    parts = moves.over_yx([second_stack] * moves.squares)
    mixed_0, heads_0, normed_one = heads_forward(
        SETS[0], place, mask, vec, picked, first_own, first_other
    )
    grad_rows = pick(after(place, heads_0), cotangent, slots)
    mixed_0, heads_0, normed_one, grad_rows, *parts = together(
        mixed_0, heads_0, normed_one, grad_rows, *parts
    )
    (second_own,) = place_blocks(place, 1, parts, widths[1:])
    second_own = second_own.reshape(D, widths[1])
    second_other = moves.over_core(second_own)
    w_in = [(first_own, first_other), (second_own, second_other)]
    shard = after(shards[1], second_own)
    parts = moves.over_z([shard] * n_dp)
    mixed_1, heads_1 = heads_forward(SETS[1], place, mask, vec, normed_one, *w_in[1])
    mixed_1, heads_1, *parts = together(mixed_1, heads_1, *parts)
    (stack,) = place_blocks(place, 0, parts, [shard.shape[1]])
    gathered = lax.all_gather(stack, "fsdp", axis=1, tiled=True)
    w_hidden.append(gathered.reshape(D, shard.shape[1]))
    heads = [heads_0, heads_1]

    blocks = moves.square_blocks(rows_in) if rows_in % 8 == 0 else []
    attended, normed_two, out, back, gw_0, sums_0 = first_mlp(
        blocks, bias, vec, picked, grad_rows, heads, w_hidden[0]
    )
    hidden_0 = moves.over_square(gw_0, blocks)
    (
        grad_attended,
        carry,
        put_values,
        turn_sums,
        sums_1,
        gw_1,
    ) = second_mlp(
        blocks,
        place,
        bias,
        vec,
        picked,
        grad_rows,
        normed_two,
        attended,
        out,
        back,
        w_hidden[1],
    )
    hidden_1 = moves.over_square(gw_1, blocks)
    places = put_places(keep_slots, image_tokens)

    results = heads_backward(
        SETS[0], place, mask, grad_attended, normed_one, w_hidden[0], mixed_0, heads
    )
    gm_0, gw_own, gw_other, sums_a, hidden_0 = together(*results, hidden_0)
    arrived = moves.over_core(gw_other)
    results = heads_backward(
        SETS[1], after(place, gm_0), mask, grad_attended, normed_one, w_hidden[0], mixed_1
    )
    gm_1, gw_own_1, gw_other_1, sums_b, arrived = together(*results, arrived)
    blocks = moves.add_cores(
        place, [gw_own, gw_own_1], [arrived, moves.over_core(gw_other_1)]
    )
    last = moves.over_yx(blocks)
    activations = put(after(places, *blocks), tokens, put_values)
    hidden = [value.reshape(n_dp, rows_in, -1) for value in (hidden_0, hidden_1)]
    plane_sums = planes(after(place, activations), hidden)
    summed = lax.psum_scatter(
        plane_sums.reshape(n_dp * rows_in, -1), "dp", scatter_dimension=0, tiled=True
    )
    results = first_back(
        after(vec, plane_sums), picked, grad_rows, carry, [gm_0, gm_1], w_in
    )
    grad_values, first_sums, *last = together(*results, *last)
    blocks = add_blocks(place, [last], n_dp, rows_in)
    last = moves.over_z(blocks)
    input_grad = put(after(places, *blocks), cotangent, grad_values)
    input_grad, *last = together(input_grad, *last)
    table, mine, send = make_table(
        total,
        place,
        first_sums,
        sums_a,
        sums_b,
        turn_sums,
        sums_0,
        sums_1,
        summed,
        last,
    )
    parts = moves.over_z([table] * n_dp)
    theirs = moves.over_core(send)
    summed_expand, summed_contract = from_quarters(total, summed)
    theirs, summed_expand, summed_contract, *parts = together(
        theirs, summed_expand, summed_contract, *parts
    )
    table = add_parts(moves.over_yx([add_parts(parts)] * moves.squares))
    table = table + moves.over_core(table)

    own = lax.dynamic_slice_in_dim(table[:13], owner * columns, columns, axis=1)
    masters = (project_in, project_out, expand, contract, vectors)
    firsts = (first_in, first_out, first_expand, first_contract, first_vectors)
    seconds = (second_in, second_out, second_expand, second_contract, second_vectors)
    grad_norm, *updates = adam(
        place,
        table,
        mine,
        theirs,
        summed_expand,
        summed_contract,
        own,
        masters,
        firsts,
        seconds,
    )
    return (activations, input_grad, grad_norm.reshape(1), *updates)


def solution(mesh):
    split = P(AXES, None)
    columns = P(None, AXES)
    weights = (split, split, split, split, columns)
    return jax.shard_map(
        functools.partial(on_device, mesh.shape["dp"], mesh.shape["fsdp"]),
        mesh=mesh,
        in_specs=(split, split, split) + weights * 3,
        out_specs=(split, split, P()) + weights * 4,
        check_vma=False,
    )
```

```python
import functools
import math

import jax
import jax.numpy as jnp
from jax import lax
from jax.experimental import pallas as pl
from jax.experimental.pallas import tpu as pltpu
from jax.sharding import PartitionSpec as P

D = 768
HEADS = 12
HEAD_DIM = 64
KEEP_GLOBAL = 98
KEEP_LOCAL = 18
KEEP = 268
PARAMS = 7087872
STEP = 5

norm_eps = 1e-06
clip_share = 0.05
matrix_rate = 0.04
vector_rate = 0.3
matrix_decay = 0.05
first_beta = 0.5
second_beta = 0.5
adam_eps = 1e-08

AXES = ("dp", "fsdp")
BF = jnp.bfloat16
F32 = jnp.float32
NT = (((1,), (1,)), ((), ()))
TN = (((0,), (0,)), ((), ()))
PAD = -(-KEEP // 16) * 16
PAIRS = HEADS // 2
PW = 2 * HEAD_DIM
SETS = ((0,), (1, 2))
CHUNKS = 2
QUARTERS = 2 * CHUNKS
HIDDEN = 4 * D
IMAGES = 2
NEG = -1e30
SEGMENTS = (
    (0, 112, 0, KEEP_GLOBAL),
    (96, 112, KEEP_GLOBAL, 2 * KEEP_GLOBAL),
    (192, 80, 2 * KEEP_GLOBAL, KEEP),
)


def nn(left, right):
    return jnp.dot(left, right, preferred_element_type=F32)


def nt(left, right):
    return lax.dot_general(left, right, NT, preferred_element_type=F32)


def tn(left, right):
    return lax.dot_general(left, right, TN, preferred_element_type=F32)


def params(limit=60):
    return pltpu.CompilerParams(vmem_limit_bytes=limit * 2**20)


def cost(flops, moved, exps=0):
    return pl.CostEstimate(flops=int(flops), bytes_accessed=int(moved), transcendentals=int(exps))


def whole(shape):
    return pl.BlockSpec(shape, lambda *_: (0,) * len(shape))


ANY = pl.BlockSpec(memory_space=pl.ANY)
SMEM = pl.BlockSpec(memory_space=pltpu.SMEM)


def normalize(values):
    centred = values - jnp.mean(values, axis=-1, keepdims=True)
    spread = jnp.mean(centred * centred, axis=-1, keepdims=True)
    inverse = lax.rsqrt(spread + norm_eps)
    return centred * inverse, inverse


def norm_back(grad, normed, inverse, gain):
    pulled = grad * gain
    return inverse * (
        pulled
        - jnp.mean(pulled, axis=-1, keepdims=True)
        - normed * jnp.mean(pulled * normed, axis=-1, keepdims=True)
    )


def column_sum(values):
    return jnp.sum(values, axis=0, keepdims=True)


def window_start(step, image_tokens, rows, window):
    return jnp.minimum((IMAGES * image_tokens * step) // 16, (rows - window) // 16) * 16


def pick_kernel(image_tokens, rows, window, part, place, slots, source, picked):
    step = pl.program_id(0)
    shift = IMAGES * image_tokens * step - window_start(step, image_tokens, rows, window)
    for image in range(IMAGES):
        first = (image * image_tokens) // 16 * 16
        span = min(part, window - first)
        target = slots[image] + shift + image * image_tokens - first
        hot = lax.broadcasted_iota(jnp.int32, (PAD, span), 1) == target
        values = nn(hot.astype(F32).astype(BF), source[first : first + span, :])
        picked[image * PAD : (image + 1) * PAD, :] = values.astype(BF)


def pick(place, source, slots):
    rows = source.shape[0]
    count = slots.shape[0]
    image_tokens = rows // count
    window = -(-(IMAGES * image_tokens + 15) // 16) * 16
    part = -(-(image_tokens + 32) // 16) * 16
    start = functools.partial(
        window_start, image_tokens=image_tokens, rows=rows, window=window
    )
    return pl.pallas_call(
        functools.partial(pick_kernel, image_tokens, rows, window, part),
        grid=(count // IMAGES,),
        in_specs=[
            SMEM,
            pl.BlockSpec((IMAGES, PAD, 1), lambda i: (i, 0, 0)),
            pl.BlockSpec((pl.Element(window), pl.Element(D)), lambda i: (start(i), 0)),
        ],
        out_specs=pl.BlockSpec((IMAGES * PAD, D), lambda i: (i, 0)),
        out_shape=jax.ShapeDtypeStruct((count * PAD, D), BF),
        compiler_params=params(20),
        cost_estimate=cost(2 * count * PAD * window * D, 2 * rows * D + 2 * count * PAD * D),
        name="pick_rows",
    )(place, slots, source)


def local_mask():
    first, rows, low, high = SEGMENTS[2]
    slot = jnp.arange(rows) + first
    crop = jnp.where((slot >= low) & (slot < high), (slot - low) // KEEP_LOCAL, -1)
    same = (crop[:, None] == crop[None, :]) & (crop[:, None] >= 0)
    bias = jnp.where(same, 0.0, NEG).astype(F32)
    return jnp.concatenate([bias, bias], axis=1)


def lanes_of(rows):
    return lax.broadcasted_iota(jnp.int32, (rows, PW), 1) < HEAD_DIM


def split_heads(values):
    first = lanes_of(values.shape[0])
    zero = jnp.zeros_like(values)
    return jnp.concatenate(
        [jnp.where(first, values, zero), jnp.where(first, zero, values)], axis=0
    )


def join_heads(values):
    rows = values.shape[0] // 2
    return jnp.where(lanes_of(rows), values[:rows], values[rows:])


def rows_of(segment):
    return slice(segment[0], segment[0] + segment[1])


def attention(jobs, mask):
    chains = [(job, segment) for job in jobs for segment in SEGMENTS]
    scores = []
    for (query, key_rows, _), segment in chains:
        rows = rows_of(segment)
        scores.append(nt(split_heads(query[rows] * HEAD_DIM**-0.5), key_rows[rows]))
    mask = jnp.concatenate([mask[:, : mask.shape[0]]] * 2, axis=0)
    probs = []
    for (_, segment), score in zip(chains, scores):
        first, count, low, high = segment
        if low == 2 * KEEP_GLOBAL:
            score = score + mask
        else:
            slot = lax.broadcasted_iota(jnp.int32, (1, count), 1) + first
            score = jnp.where((slot >= low) & (slot < high), score, NEG)
        grown = jnp.exp(score - jnp.max(score, axis=-1, keepdims=True))
        probs.append((grown * (1.0 / jnp.sum(grown, axis=-1, keepdims=True))).astype(BF))
    parts = []
    for ((_, _, value), segment), prob in zip(chains, probs):
        parts.append(join_heads(nn(prob, value[rows_of(segment)])))
    slot = lax.broadcasted_iota(jnp.int32, (16, 1), 0)
    results = []
    for index in range(len(jobs)):
        one, two, three = parts[3 * index : 3 * index + 3]
        results.append(
            jnp.concatenate(
                [
                    one[:96],
                    jnp.where(slot + 96 < KEEP_GLOBAL, one[96:], two[:16]),
                    two[16:96],
                    jnp.where(slot + 192 < 2 * KEEP_GLOBAL, two[96:], three[:16]),
                    three[16:],
                ],
                axis=0,
            ).astype(BF)
        )
    return results


def attention_back(jobs, mask):
    chains = [(job, segment) for job in jobs for segment in SEGMENTS]
    halves, grads = [], []
    for (query, _, _, grad), segment in chains:
        first, count, low, high = segment
        rows = rows_of(segment)
        halves.append(split_heads(query[rows] * HEAD_DIM**-0.5))
        slot = lax.broadcasted_iota(jnp.int32, (count, 1), 0) + first
        kept = jnp.where((slot >= low) & (slot < high), grad[rows], jnp.zeros((), BF))
        grads.append(split_heads(kept))
    scores, grad_probs = [], []
    for ((_, key_rows, value, _), segment), half, grad in zip(chains, halves, grads):
        rows = rows_of(segment)
        scores.append(nt(key_rows[rows], half))
        grad_probs.append(nt(value[rows], grad))
    probs, grad_scores = [], []
    for (_, segment), score, pulled in zip(chains, scores, grad_probs):
        first, count, low, high = segment
        if low == 2 * KEEP_GLOBAL:
            score = score + mask
        else:
            slot = lax.broadcasted_iota(jnp.int32, (count, 1), 0) + first
            score = jnp.where((slot >= low) & (slot < high), score, NEG)
        grown = jnp.exp(score - jnp.max(score, axis=0, keepdims=True))
        prob = grown * (1.0 / jnp.sum(grown, axis=0, keepdims=True))
        weighted = jnp.sum(prob * pulled, axis=0, keepdims=True)
        probs.append(prob.astype(BF))
        grad_scores.append((prob * (pulled - weighted)).astype(BF))
    parts = [[], [], []]
    for prob, grad in zip(probs, grads):
        parts[2].append(nn(prob, grad))
    for score, half in zip(grad_scores, halves):
        parts[1].append(nn(score, half))
    for ((_, key_rows, _, _), segment), score in zip(chains, grad_scores):
        parts[0].append(join_heads(tn(score, key_rows[rows_of(segment)])) * HEAD_DIM**-0.5)
    results = []
    for index in range(len(jobs)):
        joined = []
        for part in parts:
            one, two, three = part[3 * index : 3 * index + 3]
            joined.append(
                jnp.concatenate(
                    [
                        one[:96],
                        one[96:] + two[:16],
                        two[16:96],
                        two[96:] + three[:16],
                        three[16:],
                    ],
                    axis=0,
                ).astype(BF)
            )
        results.append(joined)
    return results


def pairs_of(place, groups):
    core = place[2]
    return [2 * group + core for group in groups] + [2 * group + 1 - core for group in groups]


def lane_block(index):
    return pl.ds(pl.multiple_of(index * PW, PW), PW)


def heads_kernel(groups, place, mask, vec, source, own_w, other_w, *refs):
    if groups[0] == 0:
        mixed, heads, normed, weight = refs
        unit, _ = normalize(source[...].astype(F32))
        rows = (unit * vec[0:1, :].astype(F32) + vec[1:2, :].astype(F32)).astype(BF)
        normed[...] = rows
    else:
        mixed, heads, weight = refs
        rows = source[...]
    width = 3 * PW
    half = len(groups) * width

    @pl.when(pl.program_id(0) == 0)
    def _():
        weight[:, :half] = own_w[:, :half]
        weight[:, half:] = other_w[:, :half]

    product = nn(rows, weight[...])
    jobs, lanes = [], []
    for index, pair in enumerate(pairs_of(place, groups)):
        at = index * width
        block = lane_block(pair)
        query = (product[:, at : at + PW] + vec[2:3, block].astype(F32)).astype(BF)
        key_rows = product[:, at + PW : at + 2 * PW].astype(BF)
        value = (product[:, at + 2 * PW : at + width] + vec[3:4, block].astype(F32)).astype(BF)
        mixed[:, at : at + PW] = query
        mixed[:, at + PW : at + 2 * PW] = key_rows
        mixed[:, at + 2 * PW : at + width] = value
        for image in range(IMAGES):
            span = slice(image * PAD, (image + 1) * PAD)
            jobs.append((query[span], key_rows[span], value[span]))
            lanes.append((span, lane_block(pair - 2 * groups[0])))
    for (span, block), result in zip(lanes, attention(jobs, mask[...])):
        heads[span, block] = result


def heads_forward(groups, place, mask, vec, source, own_w, other_w):
    rows = source.shape[0]
    size = IMAGES * PAD
    width = 6 * PW * len(groups)
    wide = pl.BlockSpec((size, D), lambda i: (i, 0))
    weight = whole(own_w.shape)
    outs = [
        (pl.BlockSpec((size, width), lambda i: (i, 0)), jax.ShapeDtypeStruct((rows, width), BF)),
        (
            pl.BlockSpec((size, width // 3), lambda i: (i, 0)),
            jax.ShapeDtypeStruct((rows, width // 3), BF),
        ),
    ]
    if groups[0] == 0:
        outs.append((wide, jax.ShapeDtypeStruct((rows, D), BF)))
    return pl.pallas_call(
        functools.partial(heads_kernel, groups),
        grid=(rows // size,),
        in_specs=[SMEM, whole(mask.shape), whole((16, D)), wide, weight, weight],
        out_specs=tuple(out[0] for out in outs),
        out_shape=tuple(out[1] for out in outs),
        scratch_shapes=[pltpu.VMEM((D, width), BF)],
        compiler_params=params(32),
        cost_estimate=cost(2 * rows * D * width + rows * 1e5 * len(groups), 8 * rows * D),
        name=f"attention_{groups[0]}",
    )(place, mask, vec, source, own_w, other_w)


def heads_back_kernel(groups, steps, place, mask, grad_attended, normed, w_out, mixed, *refs):
    heads = refs[:-6] if len(refs) == 6 else refs[: -8]
    (grad_mixed, gw_own, gw_other, sums, kept_normed, kept_mixed) = refs[len(heads) :][:6]
    kept_heads, kept_grad = refs[len(heads) + 6 :] if heads else (None, None)
    step = pl.program_id(0)
    size = IMAGES * PAD
    width = 3 * PW
    half = len(groups) * width

    @pl.when(step == 0)
    def _():
        sums[...] = jnp.zeros_like(sums)

    @pl.when(step < steps)
    def _():
        rows = pl.ds(pl.multiple_of(step * size, 16), size)
        kept_normed[rows, :] = normed[...]
        incoming = grad_attended[...]
        if heads:
            kept_grad[rows, :] = incoming
            at = 0
            for part in heads:
                kept_heads[rows, at : at + part.shape[1]] = part[...]
                at += part.shape[1]
        jobs, places = [], []
        for index, pair in enumerate(pairs_of(place, groups)):
            at = index * width
            grad_heads = nt(incoming, w_out[lane_block(pair), :]).astype(BF)
            for image in range(IMAGES):
                span = slice(image * PAD, (image + 1) * PAD)
                jobs.append(
                    (
                        mixed[span, at : at + PW],
                        mixed[span, at + PW : at + 2 * PW],
                        mixed[span, at + 2 * PW : at + width],
                        grad_heads[span],
                    )
                )
                places.append((image, at))
        for (image, at), parts in zip(places, attention_back(jobs, mask[...])):
            for index, low in enumerate(parts):
                columns = slice(at + index * PW, at + (index + 1) * PW)
                grad_mixed[image * PAD : (image + 1) * PAD, columns] = low
                here = pl.ds(pl.multiple_of(step * size + image * PAD, 16), PAD)
                kept_mixed[here, columns] = low
                if index != 1:
                    sums[0:1, columns] += column_sum(low.astype(F32))

    @pl.when(step == steps)
    def _():
        first = 0
        if heads:
            first = D // 2
            core = place[2]
            own = pl.ds(pl.multiple_of(core * first, 128), first)
            other = pl.ds(pl.multiple_of((1 - core) * first, 128), first)
            gw_own[:, :first] = tn(kept_heads[...], kept_grad[:, own]).astype(BF)
            gw_other[:, :first] = tn(kept_heads[...], kept_grad[:, other]).astype(BF)
        gw_other[:, first:] = tn(kept_normed[...], kept_mixed[:, half:]).astype(BF)
        gw_own[:, first:] = tn(kept_normed[...], kept_mixed[:, :half]).astype(BF)


def heads_backward(groups, place, mask, grad_attended, normed, w_out, mixed, heads=()):
    rows, width = mixed.shape
    size = IMAGES * PAD
    steps = rows // size
    last = steps - 1

    def block(width):
        return pl.BlockSpec((size, width), lambda i: (jnp.minimum(i, last), 0))

    weight = (D, width // 2 + (D // 2 if heads else 0))
    kept = [D, width] + [D, D] * bool(heads)
    return pl.pallas_call(
        functools.partial(heads_back_kernel, groups, steps),
        grid=(steps + 1,),
        in_specs=[SMEM, whole(mask.shape), block(D), block(D)]
        + [pl.BlockSpec((D, D), lambda i: (0, w_out.shape[1] // D - 1)), block(width)]
        + [block(part.shape[1]) for part in heads],
        out_specs=(block(width), whole(weight), whole(weight), whole((8, width))),
        out_shape=(
            jax.ShapeDtypeStruct((rows, width), BF),
            jax.ShapeDtypeStruct(weight, BF),
            jax.ShapeDtypeStruct(weight, BF),
            jax.ShapeDtypeStruct((8, width), F32),
        ),
        scratch_shapes=[pltpu.VMEM((rows, lanes), BF) for lanes in kept],
        compiler_params=params(60 if heads else 40),
        cost_estimate=cost(
            2 * rows * D * (width // 3 + width) + rows * 3e5 * len(groups), 12 * rows * D
        ),
        name=f"attention_back_{groups[0]}",
    )(place, mask, grad_attended, normed, w_out, mixed, *heads)


TILE = 256


def gelu_and_slope(values):
    below = 0.5 + 0.5 * lax.erf(values * math.sqrt(0.5))
    bell = jnp.exp(-0.5 * values * values) * (1.0 / math.sqrt(2.0 * math.pi))
    return values * below, below + values * bell


def alternating(bias, weights, make_left, right, rows, kept_active, kept_before, sums):
    result = pulled = 0.0
    grad = nt(right, weights[1][...])
    left = make_left()
    before = nn(left, weights[0][...])
    for half in range(2):
        kept = slice(half * D, (half + 1) * D)
        active, slope = gelu_and_slope(before + bias[half])
        low = (grad * slope).astype(BF)
        active = active.astype(BF)
        kept_active[rows, kept] = active
        kept_before[rows, kept] = low
        if half == 0:
            before, grad = nn(left, weights[2][...]), nt(right, weights[3][...])
        sums[half] += column_sum(low.astype(F32))
        result = result + nn(active, weights[2 * half + 1][...])
        pulled = pulled + nt(low, weights[2 * half][...])
    return result, pulled


def both_ways(chunk, bias, weights, left, right, rows, kept_active, kept_before, sums):
    tiles = D // TILE
    for half in range(2):
        up, down = weights[2 * half], weights[2 * half + 1]
        for tile in range(tiles):
            columns = slice(tile * TILE, (tile + 1) * TILE)
            kept = slice(half * D + tile * TILE, half * D + (tile + 1) * TILE)
            before = nn(left, up[:, columns]) + bias[2 * chunk + half, :, columns]
            active, slope = gelu_and_slope(before)
            kept_active[rows, kept] = active.astype(BF)
            low = (nt(right, down[columns, :]) * slope).astype(BF)
            kept_before[rows, kept] = low
            sums[half, :, columns] += column_sum(low.astype(F32))
    result = nn(kept_active[rows, :D], weights[1][...])
    result += nn(kept_active[rows, D:], weights[3][...])
    pulled = nt(kept_before[rows, :D], weights[0][...])
    pulled += nt(kept_before[rows, D:], weights[2][...])
    return result, pulled


def hidden_grads(tile, blocks, kept, gw):
    kept_normed, kept_grad, kept_active, kept_before = kept

    def ordered(value):
        if blocks:
            value = jnp.concatenate([value[at : at + size] for at, size in blocks], axis=0)
        return value.astype(BF)

    for half in range(2):
        columns = slice(half * D, (half + 1) * D)

        @pl.when(tile == 2 * half)
        def _():
            gw[...] = ordered(tn(kept_normed[...], kept_before[:, columns]))

        @pl.when(tile == 2 * half + 1)
        def _():
            gw[...] = ordered(tn(kept_active[:, columns], kept_grad[...]))


def routed_rows(picked, grads, vec):
    inputs = picked[...].astype(F32)
    grad_rows = grads[...].astype(F32)
    routed = jnp.sum(inputs * vec[8:9, :].astype(F32), axis=-1, keepdims=True)
    return inputs, grad_rows, routed, routed * grad_rows


def first_mlp_kernel(steps, size, blocks, bias, vec, w_out, picked, grads, *refs):
    heads = refs[: len(SETS)]
    refs = refs[len(SETS) :]
    weights = refs[:4]
    attended, normed, out, back, gw, sums = refs[4:10]
    kept = refs[10:]
    kept_normed, kept_grad, kept_active, kept_before = kept
    step = pl.program_id(0)

    @pl.when(step == 0)
    def _():
        sums[...] = jnp.zeros_like(sums)

    @pl.when(step < steps)
    def _():
        rows = pl.ds(pl.multiple_of(step * size, 16), size)
        inputs, _, _, grad_branch = routed_rows(picked, grads, vec)
        right = grad_branch.astype(BF)
        joined = jnp.concatenate([part[...] for part in heads], axis=1)
        mixed = nn(joined, w_out[...]) + vec[4:5, :].astype(F32)
        attended[...] = mixed
        kept_grad[rows, :] = right

        def make_left():
            unit, _ = normalize(inputs + mixed)
            left = (unit * vec[5:6, :].astype(F32) + vec[6:7, :].astype(F32)).astype(BF)
            normed[...] = left
            kept_normed[rows, :] = left
            return left

        out[...], back[...] = alternating(
            bias, weights, make_left, right, rows, kept_active, kept_before, sums
        )

    @pl.when(step >= steps)
    def _():
        hidden_grads(step - steps, blocks, kept, gw)


def second_mlp_kernel(
    steps, size, blocks, place, bias, vec, picked, grads, normed, attended, out, back, *refs
):
    weights = refs[:4]
    (grad_attended, carry, values, turn_sums, sums, gw) = refs[4:10]
    kept = refs[10:]
    kept_normed, kept_grad, kept_active, kept_before = kept
    step = pl.program_id(0)

    @pl.when(step == 0)
    def _():
        sums[...] = jnp.zeros_like(sums)
        turn_sums[...] = jnp.zeros_like(turn_sums)

    @pl.when(step < steps)
    def _():
        rows = pl.ds(pl.multiple_of(step * size, 16), size)
        inputs, grad_rows, routed, grad_branch = routed_rows(picked, grads, vec)
        left = normed[...]
        right = grad_branch.astype(BF)
        kept_normed[rows, :] = left
        kept_grad[rows, :] = right
        result, pulled = both_ways(
            1, bias, weights, left, right, rows, kept_active, kept_before, sums
        )
        pulled += back[...]
        router = vec[8:9, :].astype(F32)
        mixed = attended[...]
        branch = mixed + (result + out[...]) + vec[7:8, :].astype(F32)
        values[...] = (inputs + routed * branch).astype(BF)
        grad_routed = jnp.sum(grad_rows * branch, axis=-1, keepdims=True)
        unit, inverse = normalize(inputs + mixed)
        residual = norm_back(pulled, unit, inverse, vec[5:6, :].astype(F32))
        low = (grad_branch + residual).astype(BF)
        grad_attended[...] = low
        carry[...] = residual + grad_routed * router
        turn_sums[0:1, :] += column_sum(low.astype(F32))
        turn_sums[1:2, :] += column_sum(pulled * unit)
        turn_sums[2:3, :] += column_sum(pulled)
        turn_sums[3:4, :] += column_sum(right.astype(F32))
        turn_sums[4:5, :] += column_sum(inputs * grad_routed)

    @pl.when(step >= steps)
    def _():
        hidden_grads(step - steps, blocks, kept, gw)


def mlp_specs(chunk, rows):
    size = PAD
    steps = rows // size
    last = steps - 1

    def wide(width=D):
        return pl.BlockSpec((size, width), lambda i: (jnp.minimum(i, last), 0))

    weights = [
        pl.BlockSpec((D, D), lambda i, at=at: (0, at), pipeline_mode=pl.Buffered(1))
        for at in (0, 2, 1, 3)
    ]

    def gw_block(i):
        tile = jnp.clip(i - steps, 0, 3)
        return (0, tile // 2 + 2 * (tile % 2))

    scratch = [
        pltpu.VMEM((rows, D), BF),
        pltpu.VMEM((rows, D), BF),
        pltpu.VMEM((rows, 2 * D), BF),
        pltpu.VMEM((rows, 2 * D), BF),
    ]
    return size, steps, 4, wide, weights, pl.BlockSpec((D, D), gw_block), scratch


def first_mlp(blocks, bias, vec, picked, grads, heads, weights):
    rows = picked.shape[0]
    size, steps, tiles, wide, weight_specs, gw, scratch = mlp_specs(0, rows)
    total = jax.ShapeDtypeStruct((rows, D), F32)
    return pl.pallas_call(
        functools.partial(first_mlp_kernel, steps, size, blocks),
        grid=(steps + tiles,),
        in_specs=[whole(bias.shape), whole((16, D))]
        + [pl.BlockSpec((D, D), lambda i: (0, 4), pipeline_mode=pl.Buffered(1))]
        + [wide()] * 2
        + [wide(part.shape[1]) for part in heads]
        + weight_specs,
        out_specs=(wide(),) * 4 + (gw, whole((2, 1, D))),
        out_shape=(
            total,
            jax.ShapeDtypeStruct((rows, D), BF),
            total,
            total,
            jax.ShapeDtypeStruct((D, 4 * D), BF),
            jax.ShapeDtypeStruct((2, 1, D), F32),
        ),
        scratch_shapes=scratch,
        compiler_params=params(),
        cost_estimate=cost(26 * rows * D * D, 30 * rows * D, 4 * rows * D),
        name="feed_forward_0",
    )(bias, vec, weights, picked, grads, *heads, *[weights] * 4)


def second_mlp(blocks, place, bias, vec, picked, grads, normed, attended, out, back, weights):
    rows = picked.shape[0]
    size, steps, tiles, wide, weight_specs, gw, scratch = mlp_specs(1, rows)
    low = jax.ShapeDtypeStruct((rows, D), BF)
    return pl.pallas_call(
        functools.partial(second_mlp_kernel, steps, size, blocks),
        grid=(steps + tiles,),
        in_specs=[SMEM, whole(bias.shape), whole((16, D))]
        + [wide()] * 6
        + weight_specs,
        out_specs=(wide(), wide(), wide(), whole((8, D)), whole((2, 1, D)), gw),
        out_shape=(
            low,
            jax.ShapeDtypeStruct((rows, D), F32),
            low,
            jax.ShapeDtypeStruct((8, D), F32),
            jax.ShapeDtypeStruct((2, 1, D), F32),
            jax.ShapeDtypeStruct((D, 4 * D), BF),
        ),
        scratch_shapes=scratch,
        compiler_params=params(),
        cost_estimate=cost(26 * rows * D * D, 40 * rows * D, 4 * rows * D),
        name="feed_forward_1",
    )(place, bias, vec, picked, grads, normed, attended, out, back, *[weights] * 4)


def first_back_kernel(count, vec, picked, grads, carry, *refs):
    mixed = refs[:count]
    weights = refs[count : 3 * count]
    values, sums = refs[3 * count : 3 * count + 2]
    kept = refs[3 * count + 2 :]

    @pl.when(pl.program_id(0) == 0)
    def _():
        sums[...] = jnp.zeros_like(sums)
        for index in range(count):
            half = mixed[index].shape[1] // 2
            kept[index][:, :half] = weights[2 * index][:, :half]
            kept[index][:, half:] = weights[2 * index + 1][:, :half]

    pulled = nt(mixed[0][...], kept[0][...])
    for index in range(1, count):
        pulled += nt(mixed[index][...], kept[index][...])
    unit, inverse = normalize(picked[...].astype(F32))
    grad = norm_back(pulled, unit, inverse, vec[0:1, :].astype(F32))
    values[...] = (grads[...].astype(F32) + grad + carry[...]).astype(BF)
    sums[0:1, :] += column_sum(pulled * unit)
    sums[1:2, :] += column_sum(pulled)


def first_back(vec, picked, grads, carry, mixed, weights):
    rows = picked.shape[0]
    size = 2 * PAD
    wide = pl.BlockSpec((size, D), lambda i: (i, 0))
    flat = [weight for pair in weights for weight in pair]
    return pl.pallas_call(
        functools.partial(first_back_kernel, len(mixed)),
        grid=(rows // size,),
        in_specs=[whole((16, D)), wide, wide, wide]
        + [pl.BlockSpec((size, part.shape[1]), lambda i: (i, 0)) for part in mixed]
        + [whole(weight.shape) for weight in flat],
        out_specs=(wide, whole((8, D))),
        out_shape=(jax.ShapeDtypeStruct((rows, D), BF), jax.ShapeDtypeStruct((8, D), F32)),
        scratch_shapes=[pltpu.VMEM((D, part.shape[1]), BF) for part in mixed],
        compiler_params=params(44),
        cost_estimate=cost(6 * rows * D * D, 16 * rows * D),
        name="first_norm_back",
    )(vec, picked, grads, carry, *mixed, *flat)


def put_kernel(span, places, source, value, after, out, both):
    width = places.shape[2]
    for image in range(IMAGES):
        rows = slice(image * span, (image + 1) * span)
        both[:PAD, :] = value[image * PAD : (image + 1) * PAD, :]
        if image + 1 < IMAGES:
            both[PAD:, :] = value[(image + 1) * PAD : (image + 1) * PAD + 16, :]
        else:
            both[PAD:, :] = after[...]
        same = lax.broadcasted_iota(jnp.int32, (span, width), 0) == places[image]
        hot = same.astype(F32)
        kept = jnp.max(hot, axis=-1, keepdims=True) > 0.5
        moved = nn(hot.astype(BF), both[...])
        out[rows, :] = jnp.where(kept, moved, source[rows, :].astype(F32)).astype(BF)


def put(places, source, values):
    rows = source.shape[0]
    count = places.shape[0]
    span = -(-(rows // count) // 16) * 16
    steps = count // IMAGES
    block = pl.BlockSpec((IMAGES * span, D), lambda i: (i, 0))
    return pl.pallas_call(
        functools.partial(put_kernel, span),
        grid=(steps,),
        in_specs=[
            pl.BlockSpec((IMAGES, 1, places.shape[2]), lambda i: (i, 0, 0)),
            block,
            pl.BlockSpec((IMAGES * PAD, D), lambda i: (i, 0)),
            pl.BlockSpec(
                (16, D), lambda i: (jnp.minimum(i + 1, steps - 1) * (IMAGES * PAD // 16), 0)
            ),
        ],
        out_specs=block,
        out_shape=jax.ShapeDtypeStruct((rows, D), BF),
        scratch_shapes=[pltpu.VMEM((PAD + 16, D), BF)],
        compiler_params=params(24),
        cost_estimate=cost(2 * rows * D * (PAD + 16), 6 * rows * D),
        name="put_rows",
    )(places, source, values, values)


def put_places(keep_slots, image_tokens):
    count = keep_slots.shape[0]
    span = -(-image_tokens // 16) * 16
    image = jnp.arange(count, dtype=jnp.int32)[:, None]
    own = keep_slots + image * (image_tokens - span)
    following = jnp.concatenate([keep_slots[1:, :16], jnp.full((1, 16), -span, jnp.int32)], axis=0)
    following = following + (image + 1) * image_tokens - image * span
    following = jnp.where(image < count - 1, following, -1)
    gap = jnp.full((count, PAD - KEEP), -1, jnp.int32)
    return jnp.concatenate([own, gap, following], axis=1)[:, None, :]


class Moves:
    def __init__(self, n_dp, n_fsdp):
        self.n_dp = n_dp
        self.n_fsdp = n_fsdp
        self.squares = n_fsdp // 2
        outer = lax.axis_index("dp")
        inner = lax.axis_index("fsdp")
        self.z = outer
        self.yx = inner // 2
        self.core = inner % 2
        self.place = jnp.stack([self.z, self.yx, self.core]).astype(jnp.int32)

    def swap(self, value, mask):
        total = self.n_dp * self.n_fsdp
        return lax.ppermute(value, AXES, [(i, i ^ mask) for i in range(total)])

    def over_z(self, values):
        return [values[0]] + [self.swap(values[k], k * self.n_fsdp) for k in range(1, self.n_dp)]

    def over_yx(self, values):
        return [values[0]] + [self.swap(values[k], 2 * k) for k in range(1, self.squares)]

    def over_core(self, value):
        return self.swap(value, 1)

    def square_blocks(self, size):
        return [
            ((z * self.n_fsdp + inner) * size, size)
            for inner in range(self.n_fsdp)
            for z in range(self.n_dp)
        ]

    def over_square(self, value, ordered):
        rows, n = value.shape
        if not ordered:
            value = value.reshape(self.n_dp, self.n_fsdp, -1, n).transpose(1, 0, 2, 3)
        value = value.reshape(rows, n)
        return lax.psum_scatter(value, "fsdp", scatter_dimension=0, tiled=True)

    def by_chip(self, value):
        chips = self.n_dp * self.squares
        return value.reshape(self.n_dp, self.squares, value.shape[0] // chips, value.shape[1])

    def add_cores(self, place, keeps, arrived):
        keeps = [self.by_chip(value) for value in keeps]
        arrived = [self.by_chip(value) for value in arrived]
        return add_pairs(place, keeps, arrived, self.squares)


def add_parts(parts):
    total = parts[0].astype(F32)
    for part in parts[1:]:
        total = total + part.astype(F32)
    return total


def together(*values):
    return lax.optimization_barrier(values)


def after(value, *others):
    return lax.optimization_barrier((value, *others))[0]


def place_kernel(axis, count, cuts, place, *refs):
    outs = refs[count:]
    me = place[axis]
    for k in range(count):
        for (first, width), out in zip(cuts, outs):
            if axis == 0:
                out[me ^ k] = refs[k][:, first : first + width]
            else:
                out[:, me ^ k] = refs[k][...]


def place_blocks(place, axis, blocks, widths):
    count = len(blocks)
    cuts, at = [], 0
    for width in widths:
        cuts.append((at, width))
        at += width
    shape = blocks[0].shape[:-1]
    shape = shape[:axis] + (count,) + shape[axis:]
    vmem = pl.BlockSpec(memory_space=pltpu.VMEM)
    return pl.pallas_call(
        functools.partial(place_kernel, axis, count, cuts),
        in_specs=[SMEM] + [vmem] * count,
        out_specs=[vmem] * len(widths),
        out_shape=[jax.ShapeDtypeStruct(shape + (width,), BF) for width in widths],
        compiler_params=params(24),
        cost_estimate=cost(0, 4 * math.prod(shape) * at),
        name="place_blocks",
    )(place, *blocks)


def add_pairs_kernel(parts, squares, place, *refs):
    outs = refs[2 * parts * squares :]
    at = 0
    for part in range(parts):
        for k in range(squares):
            index = part * squares + k
            left, right = refs[index], refs[parts * squares + index]
            width = left.shape[3]
            total = left[...].astype(F32) + right[...].astype(F32)
            outs[k][:, :, at : at + width] = total[:, 0].astype(BF)
        at += width


def add_pairs(place, keeps, arrived, squares):
    specs, left, right = [], [], []
    n_dp, _, m, _ = keeps[0].shape
    for keep, other in zip(keeps, arrived):
        for k in range(squares):
            specs.append(
                pl.BlockSpec(
                    (n_dp, 1, m, keep.shape[3]), lambda i, place, k=k: (0, place[1] ^ k, 0, 0)
                )
            )
            left.append(keep)
            right.append(other)
    shape = (n_dp, m, sum(keep.shape[3] for keep in keeps))
    return pl.pallas_call(
        functools.partial(add_pairs_kernel, len(keeps), squares),
        grid_spec=pltpu.PrefetchScalarGridSpec(
            num_scalar_prefetch=1,
            grid=(1,),
            in_specs=specs + specs,
            out_specs=[pl.BlockSpec(shape, lambda i, place: (0, 0, 0))] * squares,
        ),
        out_shape=[jax.ShapeDtypeStruct(shape, BF)] * squares,
        compiler_params=params(24),
        cost_estimate=cost(0, 6 * squares * math.prod(shape)),
        name="add_cores",
    )(place, *left, *right)


def add_blocks_kernel(count, rows, sizes, place, *refs):
    outs = refs[count * sum(sizes) :]
    at = 0
    for index in range(count):
        lane = 0
        for terms in sizes:
            total = refs[at][0].astype(F32)
            for term in range(1, terms):
                total = total + refs[at + term][0].astype(F32)
            at += terms
            for first in range(0, total.shape[0], rows):
                width = total.shape[1]
                outs[index][:, lane : lane + width] = total[first : first + rows].astype(BF)
                lane += width


def add_blocks(place, groups, n_dp, rows):
    specs, operands, lanes = [], [], 0
    for arrays in groups:
        _, m, n = arrays[0].shape
        lanes += n * (m // rows)
    for k in range(n_dp):
        for arrays in groups:
            _, m, n = arrays[0].shape
            spec = pl.BlockSpec((1, m, n), lambda i, place, k=k: (place[0] ^ k, 0, 0))
            specs += [spec] * len(arrays)
            operands += arrays
    sizes = [len(arrays) for arrays in groups]
    return pl.pallas_call(
        functools.partial(add_blocks_kernel, n_dp, rows, sizes),
        grid_spec=pltpu.PrefetchScalarGridSpec(
            num_scalar_prefetch=1,
            grid=(1,),
            in_specs=specs,
            out_specs=[pl.BlockSpec((rows, lanes), lambda i, place: (0, 0))] * n_dp,
        ),
        out_shape=[jax.ShapeDtypeStruct((rows, lanes), BF)] * n_dp,
        compiler_params=params(24),
        cost_estimate=cost(0, 4 * n_dp * rows * lanes * max(sizes)),
        name="add_squares",
    )(place, *operands)


def planes_kernel(place, *refs):
    out = refs[-1]
    lane = 0
    for ref in refs[:-1]:
        out[:, :, lane : lane + ref.shape[2]] = ref[...]
        lane += ref.shape[2]


def planes(place, arrays):
    n_dp, rows, _ = arrays[0].shape
    lanes = sum(value.shape[2] for value in arrays)
    vmem = pl.BlockSpec(memory_space=pltpu.VMEM)
    return pl.pallas_call(
        planes_kernel,
        in_specs=[SMEM] + [vmem] * len(arrays),
        out_specs=vmem,
        out_shape=jax.ShapeDtypeStruct((n_dp, rows, lanes), BF),
        compiler_params=params(),
        cost_estimate=cost(0, 4 * n_dp * rows * lanes),
        name="planes",
    )(place, *arrays)


def quarters_kernel(total, part, up, down, project_out, *outs):
    outs[0][:, 4 * D :] = project_out[...].astype(BF)
    for chunk, out in enumerate(outs):
        for half in range(2):
            quarter = 2 * chunk + half
            pieces = [
                up[:, (owner * QUARTERS + quarter) * part : (owner * QUARTERS + quarter + 1) * part]
                for owner in range(total)
            ]
            out[:, half * D : (half + 1) * D] = jnp.concatenate(pieces, axis=1).astype(BF)
            rows = slice(quarter * part, (quarter + 1) * part)
            out[:, (2 + half) * D : (3 + half) * D] = down[rows, :].astype(BF)


def to_quarters(total, up, down, project_out):
    rows = up.shape[0]
    part = down.shape[0] // QUARTERS
    shape = jax.ShapeDtypeStruct((rows, 4 * D), BF)
    if part % 8:
        ups = up.astype(BF).reshape(rows, total, QUARTERS, part).transpose(2, 0, 1, 3)
        ups = ups.reshape(QUARTERS, rows, D)
        downs = down.astype(BF).reshape(QUARTERS, part, D)
        first = [ups[0], ups[1], downs[0], downs[1], project_out.astype(BF)]
        second = [ups[2], ups[3], downs[2], downs[3]]
        return [jnp.concatenate(first, axis=1), jnp.concatenate(second, axis=1)]
    vmem = pl.BlockSpec(memory_space=pltpu.VMEM)
    return pl.pallas_call(
        functools.partial(quarters_kernel, total, part),
        in_specs=[vmem] * 3,
        out_specs=[vmem] * 2,
        out_shape=[jax.ShapeDtypeStruct((rows, 5 * D), BF), shape],
        compiler_params=params(),
        cost_estimate=cost(0, 12 * rows * 4 * D),
        name="to_quarters",
    )(up, down, project_out)


def hidden_kernel(total, part, value, up, down):
    pieces = []
    for owner in range(total):
        for quarter in range(QUARTERS):
            at = (4 * (quarter // 2) + quarter % 2) * D + owner * part
            pieces.append(value[:, at : at + part].astype(F32))
    up[...] = jnp.concatenate(pieces, axis=1)
    for quarter in range(QUARTERS):
        at = (4 * (quarter // 2) + 2 + quarter % 2) * D
        down[quarter * part : (quarter + 1) * part, :] = value[:, at : at + D].astype(F32)


def from_quarters(total, value):
    rows = value.shape[0]
    part = D // total
    if part % 8:
        quarters = value[:, : 8 * D].astype(F32).reshape(rows, CHUNKS, 2, 2, D)
        ups = quarters[:, :, 0].reshape(rows, QUARTERS, total, part).transpose(0, 2, 1, 3)
        downs = quarters[:, :, 1].reshape(rows, QUARTERS, D).transpose(1, 0, 2)
        return ups.reshape(rows, HIDDEN), downs.reshape(QUARTERS * part, D)
    vmem = pl.BlockSpec(memory_space=pltpu.VMEM)
    return pl.pallas_call(
        functools.partial(hidden_kernel, total, part),
        in_specs=[vmem],
        out_specs=[vmem] * 2,
        out_shape=[
            jax.ShapeDtypeStruct((rows, HIDDEN), F32),
            jax.ShapeDtypeStruct((QUARTERS * part, D), F32),
        ],
        compiler_params=params(),
        cost_estimate=cost(0, 6 * rows * 8 * D),
        name="from_quarters",
    )(value)


def unit_pieces(total):
    part = D // total
    for quarter in range(QUARTERS):
        for owner in range(total):
            first = (owner * QUARTERS + quarter) * part
            yield quarter, owner * part, first // D, first % D


def vectors_kernel(total, source, vec, bias):
    rows = source[...].astype(F32).T[:16, :]
    vec[...] = rows.astype(BF)
    part = D // total
    pieces = [[] for _ in range(QUARTERS)]
    for quarter, _, row, lane in unit_pieces(total):
        pieces[quarter].append(rows[9 + row : 10 + row, lane : lane + part])
    for quarter in range(QUARTERS):
        bias[quarter] = jnp.concatenate(pieces[quarter], axis=1)


def vectors_of(total, gathered):
    if D // total % 8:
        vec = gathered[:, -128:-112].T
        bias = vec[9:13].astype(F32).reshape(total, QUARTERS, -1).transpose(1, 0, 2)
        return vec, bias.reshape(QUARTERS, 1, D)
    return pl.pallas_call(
        functools.partial(vectors_kernel, total),
        grid=(1,),
        in_specs=[pl.BlockSpec((D, 128), lambda i: (0, gathered.shape[1] // 128 - 1))],
        out_specs=[whole((16, D)), whole((QUARTERS, 1, D))],
        out_shape=[
            jax.ShapeDtypeStruct((16, D), BF),
            jax.ShapeDtypeStruct((QUARTERS, 1, D), F32),
        ],
        compiler_params=params(16),
        cost_estimate=cost(0, 4 * D * 128),
        name="vectors",
    )(gathered)


def pair_sums(core, sums, groups, part):
    width = 3 * PW
    half = len(groups) * width
    pieces = []
    for index in range(len(groups)):
        at = index * width + part * PW
        own = sums[0:1, at : at + PW]
        other = sums[0:1, half + at : half + at + PW]
        pieces += [jnp.where(core == 0, own, other), jnp.where(core == 0, other, own)]
    return pieces


def table_kernel(total, place, *refs):
    (first, sums_a, sums_b, turn, sums_0, sums_1, summed) = refs[:7]
    parts, (table, mine, send) = refs[7:-3], refs[-3:]
    core = place[2]
    table[...] = jnp.zeros_like(table)
    table[0:2, :] = first[0:2, :]
    for row, part in ((2, 0), (3, 2)):
        pieces = pair_sums(core, sums_a, SETS[0], part) + pair_sums(core, sums_b, SETS[1], part)
        table[row : row + 1, :] = jnp.concatenate(pieces, axis=1)
    table[4:9, :] = turn[0:5, :]
    size = D // total
    pieces = sorted((row, lane, quarter, at) for quarter, at, row, lane in unit_pieces(total))
    for row in range(4):
        values = []
        for _, _, quarter, at in pieces[row * len(pieces) // 4 : (row + 1) * len(pieces) // 4]:
            source = sums_1 if quarter // 2 else sums_0
            values.append(source[quarter % 2][:, at : at + size])
        table[9 + row : 10 + row, :] = jnp.concatenate(values, axis=1)
    last = parts[0][...].astype(F32)
    for part in parts[1:]:
        last = last + part[...].astype(F32)
    squares = jnp.sum(last * last, keepdims=True)
    for at in range(0, summed.shape[1], 2 * D):
        piece = summed[:, at : min(at + 2 * D, summed.shape[1])].astype(F32)
        squares = squares + jnp.sum(piece * piece, keepdims=True)
    table[13:14, :] = jnp.broadcast_to(squares, (1, D))
    width = last.shape[1] // 2
    one, two = last[:, :width], last[:, width:]
    mine[...] = jnp.where(core == 0, one, two)
    send[...] = jnp.where(core == 0, two, one)


def make_table(total, place, first, sums_a, sums_b, turn, sums_0, sums_1, summed, parts):
    rows = summed.shape[0]
    lanes = parts[0].shape[1] // 2
    vmem = pl.BlockSpec(memory_space=pltpu.VMEM)
    half = jax.ShapeDtypeStruct((rows, lanes), F32)
    return pl.pallas_call(
        functools.partial(table_kernel, total),
        in_specs=[SMEM] + [vmem] * (7 + len(parts)),
        out_specs=[vmem] * 3,
        out_shape=[jax.ShapeDtypeStruct((16, D), F32), half, half],
        compiler_params=params(),
        cost_estimate=cost(0, 20 * rows * lanes),
        name="table",
    )(place, first, sums_a, sums_b, turn, sums_0, sums_1, summed, *parts)


def whole_rows(core, mine, theirs):
    ordered = (
        jnp.where(core == 0, mine[...], theirs[...]),
        jnp.where(core == 0, theirs[...], mine[...]),
    )
    half = D // 2
    outs = jnp.concatenate([value[:, :half] for value in ordered], axis=1)
    pieces = []
    for part in range(3):
        at = half
        for groups in SETS:
            for index in range(len(groups)):
                lane = at + (3 * index + part) * PW
                pieces += [value[:, lane : lane + PW] for value in ordered]
            at += 3 * PW * len(groups)
    return jnp.concatenate(pieces, axis=1), outs


def adam_kernel(place, table, mine, theirs, up, down, own, *refs):
    kinds = 5
    masters, firsts, seconds = (refs[i * kinds : (i + 1) * kinds] for i in range(3))
    outs = refs[3 * kinds :]
    grads = whole_rows(place[2], mine, theirs) + (up[...], down[...], own[...])
    vector_rows = masters[4].shape[0]
    vectors = table[:vector_rows, :]
    squares = jnp.sum(vectors * vectors, keepdims=True) + table[vector_rows : vector_rows + 1, :1]
    grad_norm = jnp.sqrt(squares)
    factor = jnp.minimum(1.0, clip_share * math.sqrt(PARAMS) / (grad_norm + 1e-06))
    outs[0][...] = grad_norm
    for kind in range(kinds):
        rate = vector_rate if kind == 4 else matrix_rate
        decay = 0.0 if kind == 4 else matrix_decay
        master = masters[kind][...]
        grad = grads[kind] * factor
        first_new = first_beta * firsts[kind][...] + (1.0 - first_beta) * grad
        second_new = second_beta * seconds[kind][...] + (1.0 - second_beta) * grad * grad
        first_hat = first_new * (1.0 / (1.0 - first_beta**STEP))
        second_hat = second_new * (1.0 / (1.0 - second_beta**STEP))
        step = first_hat / (jnp.sqrt(second_hat) + adam_eps)
        updated = master - rate * (step + decay * master)
        outs[1 + kind][...] = first_new
        outs[1 + kinds + kind][...] = second_new
        outs[1 + 2 * kinds + kind][...] = updated
        outs[1 + 3 * kinds + kind][...] = updated.astype(BF)


def adam(place, table, mine, theirs, up, down, own, masters, firsts, seconds):
    vmem = pl.BlockSpec(memory_space=pltpu.VMEM)
    shapes = [master.shape for master in masters]
    states = [jax.ShapeDtypeStruct(shape, F32) for shape in shapes]
    outs = [jax.ShapeDtypeStruct((1, 1), F32)] + states * 3
    outs += [jax.ShapeDtypeStruct(shape, BF) for shape in shapes]
    elements = sum(math.prod(shape) for shape in shapes)
    return pl.pallas_call(
        adam_kernel,
        in_specs=[SMEM] + [vmem] * 21,
        out_specs=[vmem] * len(outs),
        out_shape=outs,
        compiler_params=params(),
        cost_estimate=cost(20 * elements, 30 * elements),
        name="adam",
    )(place, table, mine, theirs, up, down, own, *masters, *firsts, *seconds)


def on_device(
    n_dp,
    n_fsdp,
    tokens,
    keep_slots,
    cotangent,
    project_in,
    project_out,
    expand,
    contract,
    vectors,
    first_in,
    first_out,
    first_expand,
    first_contract,
    first_vectors,
    second_in,
    second_out,
    second_expand,
    second_contract,
    second_vectors,
):
    moves = Moves(n_dp, n_fsdp)
    place, core = moves.place, moves.core
    total = n_dp * n_fsdp
    rows_in = project_in.shape[0]
    part = contract.shape[0] // QUARTERS
    owner = moves.z * n_fsdp + lax.axis_index("fsdp")
    columns = vectors.shape[1]

    shards = to_quarters(total, expand, contract, project_out)
    w_hidden = [lax.all_gather(shards[0], AXES, axis=0, tiled=True)]

    def pair_columns(value, pair):
        return [value[:, at * D + pair * PW : at * D + (pair + 1) * PW] for at in range(3)]

    low_in = project_in.astype(BF)
    low_vec = jnp.pad(vectors.astype(BF).T, ((0, 0), (0, 128 - vectors.shape[0])))
    halves = []
    for parity in range(2):
        parts = []
        for index, groups in enumerate(SETS):
            for group in groups:
                parts += pair_columns(low_in, 2 * group + parity)
            if index == 0:
                parts.append(low_vec)
        halves.append(jnp.concatenate(parts, axis=1))
    mine = jnp.where(core == 0, halves[0], halves[1])
    theirs = jnp.where(core == 0, halves[1], halves[0])
    arrived = moves.over_core(theirs)
    rows = jnp.where(
        core == 0,
        jnp.concatenate([mine, arrived], axis=0),
        jnp.concatenate([arrived, mine], axis=0),
    )
    step = 3 * PW
    cut = len(SETS[0]) * step + 128
    widths = (cut, rows.shape[1] - cut)

    count = keep_slots.shape[0]
    image_tokens = tokens.shape[0] // count
    slots = jnp.pad(keep_slots, ((0, 0), (0, PAD - KEEP)), constant_values=-4 * image_tokens)
    slots = slots[:, :, None]
    parts = moves.over_z([rows] * n_dp)
    picked = pick(place, tokens, slots)
    picked, *parts = together(picked, *parts)
    first_stack, second_stack = place_blocks(place, 0, parts, widths)
    parts = moves.over_yx([first_stack] * moves.squares)
    (first_own,) = place_blocks(place, 1, parts, widths[:1])
    first_own = first_own.reshape(D, widths[0])
    first_other = moves.over_core(first_own)
    vec, bias = vectors_of(total, first_own)

    mask = local_mask()
    first_own, first_other, second_stack = together(first_own, first_other, second_stack)
    parts = moves.over_yx([second_stack] * moves.squares)
    mixed_0, heads_0, normed_one = heads_forward(
        SETS[0], place, mask, vec, picked, first_own, first_other
    )
    grad_rows = pick(after(place, heads_0), cotangent, slots)
    mixed_0, heads_0, normed_one, grad_rows, *parts = together(
        mixed_0, heads_0, normed_one, grad_rows, *parts
    )
    (second_own,) = place_blocks(place, 1, parts, widths[1:])
    second_own = second_own.reshape(D, widths[1])
    second_other = moves.over_core(second_own)
    w_in = [(first_own, first_other), (second_own, second_other)]
    shard = after(shards[1], second_own)
    parts = moves.over_z([shard] * n_dp)
    mixed_1, heads_1 = heads_forward(SETS[1], place, mask, vec, normed_one, *w_in[1])
    mixed_1, heads_1, *parts = together(mixed_1, heads_1, *parts)
    (stack,) = place_blocks(place, 0, parts, [shard.shape[1]])
    gathered = lax.all_gather(stack, "fsdp", axis=1, tiled=True)
    w_hidden.append(gathered.reshape(D, shard.shape[1]))
    heads = [heads_0, heads_1]

    blocks = moves.square_blocks(rows_in) if rows_in % 8 == 0 else []
    attended, normed_two, out, back, gw_0, sums_0 = first_mlp(
        blocks, bias, vec, picked, grad_rows, heads, w_hidden[0]
    )
    hidden_0 = moves.over_square(gw_0, blocks)
    (
        grad_attended,
        carry,
        put_values,
        turn_sums,
        sums_1,
        gw_1,
    ) = second_mlp(
        blocks,
        place,
        bias,
        vec,
        picked,
        grad_rows,
        normed_two,
        attended,
        out,
        back,
        w_hidden[1],
    )
    hidden_1 = moves.over_square(gw_1, blocks)
    places = put_places(keep_slots, image_tokens)

    results = heads_backward(
        SETS[0], place, mask, grad_attended, normed_one, w_hidden[0], mixed_0, heads
    )
    gm_0, gw_own, gw_other, sums_a, hidden_0 = together(*results, hidden_0)
    arrived = moves.over_core(gw_other)
    results = heads_backward(
        SETS[1], after(place, gm_0), mask, grad_attended, normed_one, w_hidden[0], mixed_1
    )
    gm_1, gw_own_1, gw_other_1, sums_b, arrived = together(*results, arrived)
    blocks = moves.add_cores(
        place, [gw_own, gw_own_1], [arrived, moves.over_core(gw_other_1)]
    )
    direct = [k for k in range(1, moves.squares) if k & (k - 1) == 0]
    last = [moves.swap(blocks[k], 2 * k) for k in direct]
    activations = put(after(places, *blocks), tokens, put_values)
    activations, *last = together(activations, *last)
    diagonal = [k for k in range(1, moves.squares) if k & (k - 1)]
    beyond = [moves.swap(after(blocks[k], activations), 2 * k) for k in diagonal]
    hidden = [value.reshape(n_dp, rows_in, -1) for value in (hidden_0, hidden_1)]
    plane_sums = planes(after(place, activations), hidden)
    summed = lax.psum_scatter(
        plane_sums.reshape(n_dp * rows_in, -1), "dp", scatter_dimension=0, tiled=True
    )
    results = first_back(
        after(vec, plane_sums), picked, grad_rows, carry, [gm_0, gm_1], w_in
    )
    grad_values, first_sums, *beyond = together(*results, *beyond)
    last = [blocks[0], *last, *beyond]
    blocks = add_blocks(place, [last], n_dp, rows_in)
    last = moves.over_z(blocks)
    input_grad = put(after(places, *blocks), cotangent, grad_values)
    input_grad, *last = together(input_grad, *last)
    table, mine, send = make_table(
        total,
        place,
        first_sums,
        sums_a,
        sums_b,
        turn_sums,
        sums_0,
        sums_1,
        summed,
        last,
    )
    parts = moves.over_z([table] * n_dp)
    theirs = moves.over_core(send)
    summed_expand, summed_contract = from_quarters(total, summed)
    theirs, summed_expand, summed_contract, *parts = together(
        theirs, summed_expand, summed_contract, *parts
    )
    table = add_parts(moves.over_yx([add_parts(parts)] * moves.squares))
    table = table + moves.over_core(table)

    own = lax.dynamic_slice_in_dim(table[:13], owner * columns, columns, axis=1)
    masters = (project_in, project_out, expand, contract, vectors)
    firsts = (first_in, first_out, first_expand, first_contract, first_vectors)
    seconds = (second_in, second_out, second_expand, second_contract, second_vectors)
    grad_norm, *updates = adam(
        place,
        table,
        mine,
        theirs,
        summed_expand,
        summed_contract,
        own,
        masters,
        firsts,
        seconds,
    )
    return (activations, input_grad, grad_norm.reshape(1), *updates)


def solution(mesh):
    split = P(AXES, None)
    columns = P(None, AXES)
    weights = (split, split, split, split, columns)
    return jax.shard_map(
        functools.partial(on_device, mesh.shape["dp"], mesh.shape["fsdp"]),
        mesh=mesh,
        in_specs=(split, split, split) + weights * 3,
        out_specs=(split, split, P()) + weights * 4,
        check_vma=False,
    )
```
